32 devices in a mesh: seq: 8 (over y, x, core), head: 4 (over z).
Axes of the slice: x: 2, y: 2, z: 4, core: 2. Of those that a mesh axis runs over, the one named last changes fastest.
Arguments:
- tokens: bfloat16 [18432, 1024], P('seq', 'head'), may hold values from -6 to 6
- lengths: int32 [24], replicated, may hold values from 0 to 12288, as said below
- pad_mask: int32 [18432], P('seq'), may hold values 0 or 1
- w_qkv: bfloat16 [3, 1024, 1024], P(None, None, 'head'), may hold values from -0.375 to 0.375
- w_out: bfloat16 [1024, 1024], P('head'), may hold values from -3 to 3
- w_up: bfloat16 [1024, 4096], P(None, 'head'), may hold values from -0.1875 to 0.1875
- w_down: bfloat16 [4096, 1024], P('head'), may hold values from -0.09375 to 0.09375
- norm_gains: float32 [2, 1024], replicated, may hold values from 0.25 to 1.75
- norm_biases: float32 [2, 1024], replicated, may hold values from -1.8 to 1.8
- out_cotangent: bfloat16 [18432, 1024], P('seq', 'head'), may hold values from -6 to 6
Outputs:
- layer_out: bfloat16 [18432, 1024], P('seq', 'head')
- grad_tokens: float32 [18432, 1024], P('seq', 'head')
- grad_w_qkv: float32 [3, 1024, 1024], P(None, 'seq', 'head')
- grad_w_out: float32 [1024, 1024], P('head', 'seq')
- grad_w_up: float32 [1024, 4096], P('seq', 'head')
- grad_w_down: float32 [4096, 1024], P('head', 'seq')
- grad_gains: float32 [2, 1024], P(None, ('head', 'seq'))
- grad_biases: float32 [2, 1024], P(None, ('head', 'seq'))
The draws below stay inside these ranges and needn't reach their ends.
Inputs may be any that keep to these rules, and one draw needn't show every extreme that they name: Each length is 768, 3072 or 12288 pixels (a 16x16, 32x32 or 64x64 image of three channels), but for the image cut at the end of the packed sequence, which keeps a multiple of 768; the entries after it are 0; the lengths sum to 18432; the first is min(12288, 18432).
All inputs are finite; a program needn't handle non-finite values. No bound on the sum of `pad_mask` on one device may be relied on, other than what follows from the above.
Results may differ from the reference program's by a relative error of at most 0.018.
Values may be sent and summed in bfloat16 or wider, within the bound.
A program may use at most 192 MiB of HBM per device.

```python
from functools import partial
import jax
import jax.numpy as jnp
from jax import lax

D = 1024
HEADS = 16
HD = 64
FF = 4096
BLOCK = 128
PIX_UNIT = 768
TOK_DEV = 2304
TOKENS = 18432
ITEMS = 24


def draw_lengths(key, part):
    key = jax.random.fold_in(key, 17)
    units_all = TOKENS // PIX_UNIT
    first_units = min(16, units_all)
    picks = jax.random.randint(key, (ITEMS,), 0, 3, dtype=jnp.int32)
    units = (1 + 3 * (picks >= 1).astype(jnp.int32) + 12 * (picks >= 2).astype(jnp.int32)).astype(jnp.int32)
    units = jnp.where(jnp.arange(ITEMS, dtype=jnp.int32) == 0, first_units, units).astype(jnp.int32)
    ends = jnp.cumsum(units).astype(jnp.int32)
    starts = (ends - units).astype(jnp.int32)
    taken = jnp.clip(units_all - starts, 0, units).astype(jnp.int32)
    return (taken * PIX_UNIT).astype(jnp.int32)


def with_ends(values, rng, least, high):
    shape = values.shape
    spot = [jax.random.randint(jax.random.fold_in(rng, axis), (), 0, shape[axis]) for axis in range(len(shape))]
    values = values.at[tuple(spot)].set(least)
    longest = shape.index(max(shape))
    spot[longest] = (spot[longest] + 1) % shape[longest]
    return values.at[tuple(spot)].set(high)


def spiked(values, rng, source, target, shards_of, factor):
    def block_of(position):
        return (jnp.arange(values.shape[position]) // (values.shape[position] // shards_of)).reshape((-1,) + (1,) * (values.ndim - 1 - position))

    first = jax.random.permutation(rng, shards_of)[block_of(target)]
    other_side = (block_of(target) + shards_of // 2) % shards_of
    return jnp.where((block_of(source) == first) | (block_of(source) == other_side), factor * values, values)


def steps_of(own_key, shape, split, smallest, high):
    def one(dim, shards_of):
        steps = jax.random.uniform(jax.random.fold_in(jax.random.fold_in(own_key, 6), dim), (shards_of,), jnp.float32, smallest / len(split), high / len(split))
        return jnp.repeat(jnp.exp(steps), shape[dim] // shards_of).reshape((-1,) + (1,) * (len(shape) - dim - 1))

    level = one(*split[0])
    for cut in split[1:]:
        level = level * one(*cut)
    return level


def centred(own_key, extent, spread, bound, pieces=(), kind=jnp.bfloat16):
    drawn = spread * jax.random.normal(own_key, extent, jnp.float32)
    if pieces:
        drawn = drawn * steps_of(own_key, extent, pieces, -0.22, 0.18)
    return jnp.clip(drawn, -bound, bound).astype(kind)


def bell_draw_with(stream_key, shape, spread, bound, split, heavy, kind=jnp.bfloat16):
    values = spread * jax.random.normal(stream_key, shape, jnp.float32)
    if split:
        values = values * steps_of(stream_key, shape, split, -0.22, 0.18)
    return jnp.clip(spiked(values, jax.random.fold_in(stream_key, 3), *heavy), -bound, bound).astype(kind)


def setup_inputs(seed: int = 0) -> dict:
    key_list = jax.random.split(jax.random.key(seed), 11)
    return {
        "tokens": bell_draw_with(key_list[0], (TOKENS, D), 1.0, 6.0, ((0, 8), (1, 4)), (0, 1, 8, 2.0)),
        "lengths": draw_lengths(jax.random.fold_in(key_list[10], 71), 0),
        "pad_mask": with_ends((jax.random.randint(key_list[2], (TOKENS,), 0, 8) < 7).astype(jnp.int32), jax.random.fold_in(key_list[2], 1), 0, 1),
        "w_qkv": centred(key_list[3], (3, D, D), (D // 4) ** -0.5, 0.375, ((2, 4),)),
        "w_out": centred(key_list[4], (D, D), 4 ** -0.5, 3.0, ((0, 4),)),
        "w_up": centred(key_list[5], (D, FF), D ** -0.5, 0.1875, ((1, 4),)),
        "w_down": centred(key_list[6], (FF, D), FF ** -0.5, 0.09375, ((0, 4),)),
        "norm_gains": jnp.clip(1.0 + 0.15 * jax.random.normal(key_list[7], (2, D), jnp.float32), 0.25, 1.75),
        "norm_biases": centred(key_list[8], (2, D), 0.3, 1.8, (), jnp.float32),
        "out_cotangent": bell_draw_with(key_list[9], (TOKENS, D), 1.0, 6.0, ((0, 8), (1, 4)), (0, 1, 8, 2.0)),
    }


@jax.custom_vjp
def low(v):
    return lax.optimization_barrier(v.astype(jnp.bfloat16)).astype(jnp.float32)

@jax.custom_vjp
def low_back(v):
    return v

def low_keep(v):
    return (low(v), None)

def low_pass(kept, grad):
    return (grad,)

def back_keep(v):
    return (v, None)

def back_low(kept, grad):
    return (low(grad),)
low.defvjp(low_keep, low_pass)
low_back.defvjp(back_keep, back_low)
highest_matmul_precision = lax.Precision.HIGHEST
norm_eps = 1e-05

def feature_map(values_in):
    return jax.nn.elu(values_in) + 1.0

def layer_norm(rows, gain, bias):
    mean_row = lax.optimization_barrier(jnp.mean(rows, axis=-1, keepdims=True))
    centered = rows - mean_row
    variance = lax.optimization_barrier(jnp.mean(centered * centered, axis=-1, keepdims=True))
    return centered * lax.rsqrt(variance + norm_eps) * gain + bias

def block_tables(seg_blocks, seg_before):
    block_count = seg_blocks.shape[0]
    block_width = seg_blocks.shape[1]
    prev_seg = jnp.concatenate([jnp.reshape(seg_before, (1,)).astype(jnp.int32), seg_blocks[:-1, -1].astype(jnp.int32)])
    cont_mask = (seg_blocks == prev_seg[:, None]).astype(jnp.float32)
    keep_flag = (seg_blocks[:, -1] == prev_seg).astype(jnp.int32)
    open_mask = (seg_blocks == seg_blocks[:, -1:]).astype(jnp.float32)
    causal = jnp.arange(block_width)[:, None] >= jnp.arange(block_width)[None, :]
    same_mask = ((seg_blocks[:, :, None] == seg_blocks[:, None, :]) & causal[None]).astype(jnp.float32)
    zeros_incl = jnp.cumsum(1 - keep_flag).astype(jnp.int32)
    zeros_excl = jnp.concatenate([jnp.zeros((1,), jnp.int32), zeros_incl])
    row_ids = jnp.arange(block_count + 1)[:, None]
    col_ids = jnp.arange(block_count)[None, :]
    carry_blend_term = ((col_ids < row_ids) & (zeros_excl[:, None] == zeros_incl[None, :])).astype(jnp.float32)
    carry_retain_factor = (zeros_excl == 0).astype(jnp.float32)
    return (cont_mask, open_mask, same_mask, carry_blend_term, carry_retain_factor)

def mix_blocks(feat_q, feat_k, block_vals, tables, state_in, norm_in):
    cont_mask, open_mask, same_mask, carry_blend_term, carry_retain_factor = tables
    open_keys = feat_k * open_mask[:, :, None, None]
    state_additions = low_back(jnp.einsum('nuhk,nuhv->nhkv', open_keys, block_vals, precision=highest_matmul_precision))
    norm_incs = lax.optimization_barrier(jnp.sum(open_keys, axis=1))
    states = jnp.einsum('me,ehkv->mhkv', carry_blend_term, state_additions, precision=highest_matmul_precision) + carry_retain_factor[:, None, None, None] * state_in[None]
    norms = jnp.einsum('me,ehk->mhk', carry_blend_term, norm_incs, precision=highest_matmul_precision) + carry_retain_factor[:, None, None] * norm_in[None]
    scores = low(low_back(same_mask[:, None] * jnp.einsum('nthk,nuhk->nhtu', feat_q, feat_k, precision=highest_matmul_precision)))
    cont_wide = cont_mask[:, :, None, None]
    numer = low_back(jnp.einsum('nhtu,nuhv->nthv', scores, block_vals, precision=highest_matmul_precision) + cont_wide * jnp.einsum('nthk,nhkv->nthv', feat_q, low(states[:-1]), precision=highest_matmul_precision))
    key_sums = jnp.einsum('ntu,nuhk->nthk', same_mask, feat_k, precision=highest_matmul_precision) + cont_wide * norms[:-1][:, None]
    denom = 1.0 + lax.optimization_barrier(jnp.sum(feat_q * key_sums, axis=-1))
    return (numer / denom[..., None], states[-1], norms[-1])

def layer_block(weights, carry, inputs):
    w_qkv, w_out, w_up, w_down, gains, biases = weights
    state_in, norm_in, seg_before = carry
    rows, seg_rows, mask_rows = inputs
    row_count = rows.shape[0]
    block_count = row_count // BLOCK
    tables = block_tables(seg_rows.reshape(block_count, BLOCK), seg_before)
    normed = low(layer_norm(rows, gains[0], biases[0]))
    queries = low_back(jnp.dot(normed, w_qkv[0], precision=highest_matmul_precision))
    keys_raw = low_back(jnp.dot(normed, w_qkv[1], precision=highest_matmul_precision))
    values_low = low(low_back(jnp.dot(normed, w_qkv[2], precision=highest_matmul_precision)))
    feat_q = low(feature_map(queries))
    feat_k = low(mask_rows[:, None] * feature_map(keys_raw))

    def split_heads(array_in):
        return array_in.reshape(block_count, BLOCK, HEADS, HD)
    mixed, state_out, norm_out = mix_blocks(split_heads(feat_q), split_heads(feat_k), split_heads(values_low), tables, state_in, norm_in)
    attended = low(mixed.reshape(row_count, D))
    middle = rows + low_back(jnp.dot(attended, w_out, precision=highest_matmul_precision))
    normed_mid = low(layer_norm(middle, gains[1], biases[1]))
    hidden = low(jax.nn.gelu(low_back(jnp.dot(normed_mid, w_up, precision=highest_matmul_precision))))
    result = middle + low_back(jnp.dot(hidden, w_down, precision=highest_matmul_precision))
    return ((state_out, norm_out, seg_rows[-1]), result)

def reference(tokens, lengths, pad_mask, w_qkv, w_out, w_up, w_down, norm_gains, norm_biases, out_cotangent):
    positions = jnp.arange(TOKENS).astype(jnp.int32)
    item_ends = jnp.cumsum(lengths).astype(jnp.int32)
    seg_ids = lax.optimization_barrier(jnp.sum((positions[:, None] >= item_ends[None, :]).astype(jnp.int32), axis=1)).astype(jnp.int32)
    mask_float = pad_mask.astype(jnp.float32)
    spans = TOKENS // TOK_DEV

    def forward(rows, wqkv_f, wout_f, wup_f, wdown_f, gains, biases):
        block_step = jax.checkpoint(partial(layer_block, (wqkv_f, wout_f, wup_f, wdown_f, gains, biases)))
        start_carry = (jnp.zeros((HEADS, HD, HD), jnp.float32), jnp.zeros((HEADS, HD), jnp.float32), jnp.array(-1, jnp.int32))
        block_inputs = (rows.reshape(spans, TOK_DEV, D), seg_ids.reshape(spans, TOK_DEV), mask_float.reshape(spans, TOK_DEV))
        final_carry, block_outs = lax.scan(block_step, start_carry, block_inputs)
        return block_outs.reshape(TOKENS, D)
    result, pullback = jax.vjp(forward, tokens.astype(jnp.float32), w_qkv.astype(jnp.float32), w_out.astype(jnp.float32), w_up.astype(jnp.float32), w_down.astype(jnp.float32), norm_gains, norm_biases)
    grads = pullback(out_cotangent.astype(jnp.float32))
    return (result.astype(jnp.bfloat16), grads[0], grads[1], grads[2], grads[3], grads[4], grads[5], grads[6])
```

```python
import functools
import math

import jax
import jax.numpy as jnp
from jax import lax
from jax.experimental import pallas as pl
from jax.experimental.pallas import tpu as pltpu
from jax.sharding import PartitionSpec as P

HD = 64
UNIT = 768
EPS = 1e-05
MESH = pl.DeviceIdType.MESH
BF = jnp.bfloat16
F32 = jnp.float32
MSG = 80


def bit_orders(ns):
    m = ns.bit_length() - 1
    xs = list(range(1, 1 + (m - 1) // 2))
    ys = list(range(1 + (m - 1) // 2, m))
    return xs + ys, ys + xs


def bits_to(s, order):
    out = 0
    for j, b in enumerate(order):
        out = out + (((s >> b) & 1) << j)
    return out


def rcopy(src, dst, send, recv, dev):
    return pltpu.make_async_remote_copy(
        src_ref=src, dst_ref=dst, send_sem=send, recv_sem=recv, device_id=dev, device_id_type=MESH
    )


def enter(devs):
    bar = pltpu.get_barrier_semaphore()
    for d in devs:
        pl.semaphore_signal(bar, inc=1, device_id=d, device_id_type=MESH)
    pl.semaphore_wait(bar, len(devs))


def z_others(s, h, nz):
    return [(s, lax.rem(h + d, nz)) for d in range(1, nz)]


def run_waves(groups):
    live = []
    pending = list(groups)
    while pending or live:
        if pending:
            live.append(pending.pop(0))
        nxt = []
        for group in live:
            kept = []
            for gen in group:
                try:
                    next(gen)
                    kept.append(gen)
                except StopIteration:
                    pass
            if kept:
                nxt.append(kept)
        live = nxt


def gather_kernel(ns, nz, tok, cot, w4, wu, wd, x, co, w4g, wug, wdg, lsem, tsend, trecv, zsend, zrecv, psend, precv):
    s, h = lax.axis_index("seq"), lax.axis_index("head")
    o0, o1 = bit_orders(ns)
    orders = (o0 + [0], o1 + [0])
    m = len(orders[0])
    t = x.shape[0]
    ew = tok.shape[1]
    arrays = ((w4, w4g), (wu, wug), (wd, wdg))
    half = w4.shape[1] // 2
    r = half // ns
    zdev = z_others(s, h, nz)
    enter(zdev + [(jnp.bitwise_xor(s, 1 << b), h) for b in orders[0]])
    sends = []
    local = []

    def a2a(i, src, dst):
        for d, dev in enumerate(zdev):
            cp = rcopy(
                src.at[pl.ds(dev[1] * t, t), :],
                dst.at[:, pl.ds(h * ew, ew)],
                tsend.at[i * (nz - 1) + d],
                trecv.at[i * (nz - 1) + d],
                dev,
            )
            cp.start()
            sends.append((None, cp))
        lc = pltpu.make_async_copy(src.at[pl.ds(h * t, t), :], dst.at[:, pl.ds(h * ew, ew)], lsem.at[i])
        lc.start()
        local.append(lc)

    def a2a_wait(i, src, dst):
        for d in range(nz - 1):
            frm = lax.rem(h + nz - 1 - d, nz)
            rcopy(
                src.at[pl.ds(h * t, t), :],
                dst.at[:, pl.ds(frm * ew, ew)],
                tsend.at[i * (nz - 1) + d],
                trecv.at[i * (nz - 1) + d],
                (s, frm),
            ).wait_recv()

    pos = [bits_to(s, order) for order in orders]

    def zsem(a, f, k, d):
        return ((a * 2 + f) * (nz - 1) + k) * 2 + d

    def zcopy(a, f, k, d, origin, own):
        w, wg = arrays[a]
        rows = pl.ds(f * half + pos[f] * r, r)
        dst = wg.at[origin, :, rows, :]
        src = w.at[:, rows, :] if own else dst
        i = zsem(a, f, k, d)
        return rcopy(src, dst, zsend.at[i], zrecv.at[i], (s, h + 1 if d == 0 else h - 1))

    def zstart(a, f, k, d, origin, cond):
        cp = zcopy(a, f, k, d, origin, k == 0)
        pl.when(cond)(cp.start)
        sends.append((cond, cp))

    def piece(a, f, k, d):
        wg = arrays[a][1]
        origin = h - 1 - k if d == 0 else h + 1 + k
        valid = origin >= 0 if d == 0 else origin < nz
        pl.when(valid)(zcopy(a, f, k, d, origin, False).wait_recv)
        if k + 1 < nz - 1:
            more = valid & ((h + 1 < nz) if d == 0 else (h >= 1))
            zstart(a, f, k + 1, d, origin, more)
        for j, b in enumerate(orders[f]):
            n = r << j
            begin = (pos[f] >> j) << j
            other = jnp.bitwise_xor(begin, 1 << j)
            i = zsem(a, f, k, d) * m + j
            dev = (jnp.bitwise_xor(s, 1 << b), h)
            mine = wg.at[origin, :, pl.ds(f * half + begin * r, n), :]
            theirs = wg.at[origin, :, pl.ds(f * half + other * r, n), :]
            out = rcopy(mine, mine, psend.at[i], precv.at[i], dev)
            pl.when(valid)(out.start)
            sends.append((valid, out))
            yield
            pl.when(valid)(rcopy(theirs, theirs, psend.at[i], precv.at[i], dev).wait_recv)

    a2a(0, tok, x)
    for a in range(3):
        for f in range(2):
            zstart(a, f, 0, 0, h, h + 1 < nz)
            zstart(a, f, 0, 1, h, h >= 1)
        if a == 0:
            a2a(1, cot, co)
    for a, (w, wg) in enumerate(arrays):
        lc = pltpu.make_async_copy(w, wg.at[h], lsem.at[2 + a])
        lc.start()
        local.append(lc)
    groups = [[piece(a, f, k, d) for d in range(2) for f in range(2)] for a in range(3) for k in range(nz - 1)]
    run_waves(groups)
    a2a_wait(0, tok, x)
    a2a_wait(1, cot, co)
    for lc in local:
        lc.wait()
    for cond, cp in sends:
        if cond is None:
            cp.wait_send()
        else:
            pl.when(cond)(cp.wait_send)


def any_spec():
    return pl.BlockSpec(memory_space=pl.ANY)


def vmem_spec():
    return pl.BlockSpec(memory_space=pltpu.VMEM)


def smem_spec():
    return pl.BlockSpec(memory_space=pltpu.SMEM)


def gather_all(ns, nz, tok, cot, w4, wu, wd):
    t, d = tok.shape[0] // nz, w4.shape[1]
    m = ns.bit_length() - 1
    nzs = 3 * 2 * (nz - 1) * 2
    dma = pltpu.SemaphoreType.DMA
    return pl.pallas_call(
        functools.partial(gather_kernel, ns, nz),
        out_shape=(
            jax.ShapeDtypeStruct((t, d), BF),
            jax.ShapeDtypeStruct((t, d), BF),
            jax.ShapeDtypeStruct((nz,) + w4.shape, BF),
            jax.ShapeDtypeStruct((nz,) + wu.shape, BF),
            jax.ShapeDtypeStruct((nz,) + wd.shape, BF),
        ),
        in_specs=[any_spec()] * 5,
        out_specs=(any_spec(),) * 5,
        scratch_shapes=[
            dma((5,)),
            dma((2 * (nz - 1),)),
            dma((2 * (nz - 1),)),
            dma((nzs,)),
            dma((nzs,)),
            dma((nzs * m,)),
            dma((nzs * m,)),
        ],
        name="gather_all",
        compiler_params=pltpu.CompilerParams(collective_id=0, has_side_effects=True),
    )(tok, cot, w4, wu, wd)


def scan_kernel(ns, nz, wt, wp, wl, msg, out, r1, r2, tot, outb, s1, q1, s2, q2, s3, q3):
    s, h = lax.axis_index("seq"), lax.axis_index("head")
    zdev = z_others(s, h, nz)
    sdev = [(jnp.bitwise_xor(s, d), h) for d in range(1, ns)]
    enter(zdev + sdev)
    sends = []
    for d, dev in enumerate(zdev):
        cp = rcopy(msg.at[dev[1]], r1.at[h], s1.at[d], q1.at[d], dev)
        cp.start()
        sends.append(cp)
    r1[h] = msg[h]
    for d in range(nz - 1):
        frm = lax.rem(h + nz - 1 - d, nz)
        rcopy(r1.at[frm], r1.at[frm], s1.at[d], q1.at[d], (s, frm)).wait_recv()
    total = jnp.zeros(tot.shape, F32)
    for z in range(nz):
        total = total + wt[z] * r1[z].astype(F32)
    tot[...] = total.astype(BF)
    for d, dev in enumerate(sdev):
        cp = rcopy(tot, r2.at[s], s2.at[d], q2.at[d], dev)
        cp.start()
        sends.append(cp)
    r2[s] = tot[...]
    line = [sum(wl[z, k] * r1[k].astype(F32) for k in range(nz)) for z in range(nz)]
    for d in range(ns - 1):
        frm = jnp.bitwise_xor(s, d + 1)
        rcopy(r2.at[frm], r2.at[frm], s2.at[d], q2.at[d], (frm, h)).wait_recv()
    for k in range(ns):
        got = r2[k].astype(F32)
        line = [line[z] + wp[z, k] * got for z in range(nz)]
    for z in range(nz):
        outb[z] = line[z].astype(BF)
    for d, dev in enumerate(zdev):
        cp = rcopy(outb.at[dev[1]], out.at[h], s3.at[d], q3.at[d], dev)
        cp.start()
        sends.append(cp)
    out[h] = outb[h]
    for d in range(nz - 1):
        frm = lax.rem(h + nz - 1 - d, nz)
        rcopy(out.at[frm], out.at[frm], s3.at[d], q3.at[d], (s, frm)).wait_recv()
    for cp in sends:
        cp.wait_send()


def scan_states(ns, nz, cid, wt, wp, wl, msg):
    dma = pltpu.SemaphoreType.DMA
    one = msg.shape[1:]
    return pl.pallas_call(
        functools.partial(scan_kernel, ns, nz),
        out_shape=jax.ShapeDtypeStruct(msg.shape, BF),
        in_specs=[smem_spec()] * 3 + [vmem_spec()],
        out_specs=vmem_spec(),
        scratch_shapes=[
            pltpu.VMEM(msg.shape, BF),
            pltpu.VMEM((ns,) + one, BF),
            pltpu.VMEM(one, BF),
            pltpu.VMEM(msg.shape, BF),
            dma((nz - 1,)),
            dma((nz - 1,)),
            dma((ns - 1,)),
            dma((ns - 1,)),
            dma((nz - 1,)),
            dma((nz - 1,)),
        ],
        name="scan_states",
        compiler_params=pltpu.CompilerParams(collective_id=cid, has_side_effects=True),
    )(wt, wp, wl, msg)


def add_rows(dst, lead, start, src, src_lead, src_start, n):
    blk = min(n, 32)

    def step(i, _):
        a = dst[lead + (pl.ds(pl.multiple_of(start + i * blk, 16), blk), slice(None))]
        b = src[src_lead + (pl.ds(pl.multiple_of(src_start + i * blk, 16), blk), slice(None))]
        dst[lead + (pl.ds(pl.multiple_of(start + i * blk, 16), blk), slice(None))] = (
            a.astype(F32) + b.astype(F32)
        ).astype(BF)
        return 0

    lax.fori_loop(0, n // blk, step, 0)


def reduce_kernel(ns, nz, lo, gt, gb, *refs):
    s, h = lax.axis_index("seq"), lax.axis_index("head")
    o0, o1 = bit_orders(ns)
    orders = ([0] + o0, [0] + o1)
    m = len(orders[0])
    g = refs[:3]
    lo_out, gt_out, gbo = refs[3:6]
    outs = refs[6:9]
    sc = refs[9:]
    acc = sc[0:3]
    rec = [sc[3 + i * m : 3 + (i + 1) * m] for i in range(3)]
    base = 3 + 3 * m
    zl, zr = sc[base : base + 3], sc[base + 3 : base + 6]
    gcur, grec, gz = sc[base + 6 : base + 9]
    lsem, tsend, trecv, csend, crecv, zsend, zrecv, gsend, grecv = sc[base + 9 :]
    t = lo.shape[0]
    ew = lo_out.shape[1]
    unit = g[0].shape[3] // ns
    zdev = z_others(s, h, nz)
    enter(zdev + [(jnp.bitwise_xor(s, 1 << b), h) for b in orders[0]])
    sends = []
    local = []

    def a2a(i, src, dst):
        for d, dev in enumerate(zdev):
            cp = rcopy(
                src.at[:, pl.ds(dev[1] * ew, ew)],
                dst.at[pl.ds(h * t, t), :],
                tsend.at[i * (nz - 1) + d],
                trecv.at[i * (nz - 1) + d],
                dev,
            )
            cp.start()
            sends.append((None, cp))
        lc = pltpu.make_async_copy(src.at[:, pl.ds(h * ew, ew)], dst.at[pl.ds(h * t, t), :], lsem.at[i])
        lc.start()
        local.append(lc)

    def a2a_wait(i, src, dst):
        for d in range(nz - 1):
            frm = lax.rem(h + nz - 1 - d, nz)
            rcopy(
                src.at[:, pl.ds(h * ew, ew)],
                dst.at[pl.ds(frm * t, t), :],
                tsend.at[i * (nz - 1) + d],
                trecv.at[i * (nz - 1) + d],
                (s, frm),
            ).wait_recv()

    def item(a, tz):
        c = g[a].shape[1]
        idx = a * nz + tz
        pos = [0, 0]
        for j in range(m + 1):
            if j > 0:
                for f in range(2):
                    i = (idx * m + j - 1) * 2 + f
                    n = unit * (ns >> j)
                    buf = rec[a][j - 1].at[tz, :, f]
                    rcopy(buf, buf, csend.at[i], crecv.at[i], (s, h)).wait_recv()
                    if j == 1:
                        pltpu.make_async_copy(
                            acc[a].at[tz, :, f], acc[a].at[tz, :, f], lsem.at[2 + idx * 2 + f]
                        ).wait()
                    for cc in range(c):
                        add_rows(acc[a], (tz, cc, f), pos[f], rec[a][j - 1], (tz, cc, f), 0, n)
            if j < m:
                for f in range(2):
                    i = (idx * m + j) * 2 + f
                    n = unit * (ns >> (j + 1))
                    b = (s >> orders[f][j]) & 1
                    dev = (jnp.bitwise_xor(s, 1 << orders[f][j]), h)
                    if j == 0:
                        src = g[a].at[tz, :, f, pl.ds((1 - b) * n, n), :]
                        lc = pltpu.make_async_copy(
                            g[a].at[tz, :, f, pl.ds(b * n, n), :], acc[a].at[tz, :, f], lsem.at[2 + idx * 2 + f]
                        )
                        lc.start()
                    else:
                        src = acc[a].at[tz, :, f, pl.ds(pl.multiple_of(pos[f] + (1 - b) * n, 16), n), :]
                        pos[f] = pos[f] + b * n
                    cp = rcopy(src, rec[a][j].at[tz, :, f], csend.at[i], crecv.at[i], dev)
                    cp.start()
                    sends.append((None, cp))
            yield
        for d, (buf, cond, first, nb) in enumerate(
            ((zl, h < tz, h >= 1, h + 1), (zr, h > tz, h + 1 < nz, h - 1))
        ):
            for f in range(2):
                i = (idx * 2 + d) * 2 + f
                mine = acc[a].at[tz, :, f, pl.ds(pl.multiple_of(pos[f], 16), unit), :]
                cp = rcopy(mine, buf[a].at[tz, :, f], zsend.at[i], zrecv.at[i], (s, nb))

                def relay(cp=cp, f=f, d=d, buf=buf, first=first):
                    def more():
                        cp.wait_recv()
                        for cc in range(c):
                            add_rows(acc[a], (tz, cc, f), pos[f], buf[a], (tz, cc, f), 0, unit)

                    pl.when(first)(more)
                    cp.start()

                pl.when(cond)(relay)
                sends.append((cond, cp))
        yield

        def finish():
            for f in range(2):
                for d, (buf, there) in enumerate(((zl, tz > 0), (zr, tz < nz - 1))):
                    if there:
                        i = (idx * 2 + d) * 2 + f
                        rcopy(
                            buf[a].at[tz, :, f], buf[a].at[tz, :, f], zsend.at[i], zrecv.at[i], (s, h)
                        ).wait_recv()
                for cc in range(c):
                    v = acc[a][tz, cc, f, pl.ds(pl.multiple_of(pos[f], 16), unit), :].astype(F32)
                    if tz > 0:
                        v = v + zl[a][tz, cc, f].astype(F32)
                    if tz < nz - 1:
                        v = v + zr[a][tz, cc, f].astype(F32)
                    outs[a][cc, f] = v.astype(BF)

        pl.when(h == tz)(finish)

    def small():
        gcur[0] = gb[...]
        for j, b in enumerate(orders[0]):
            dev = (jnp.bitwise_xor(s, 1 << b), h)
            cp = rcopy(gcur.at[j], grec.at[j], gsend.at[j], grecv.at[j], dev)
            cp.start()
            sends.append((None, cp))
            yield
            cp.wait_recv()
            gcur[j + 1] = gcur[j] + grec[j]
        for d, dev in enumerate(zdev):
            cp = rcopy(gcur.at[m], gz.at[h], gsend.at[m + d], grecv.at[m + d], dev)
            cp.start()
            sends.append((None, cp))
        gz[h] = gcur[m]
        yield
        for d in range(nz - 1):
            frm = lax.rem(h + nz - 1 - d, nz)
            rcopy(gz.at[frm], gz.at[frm], gsend.at[m + d], grecv.at[m + d], (s, frm)).wait_recv()
        total = gz[0]
        for z in range(1, nz):
            total = total + gz[z]
        gbo[...] = total

    a2a(0, lo, lo_out)
    order = [2, 1, 0]
    groups = [[item(a, tz)] for a in order for tz in range(nz)]
    groups[1].append(small())
    a2a(1, gt, gt_out)
    run_waves(groups)
    a2a_wait(0, lo, lo_out)
    a2a_wait(1, gt, gt_out)
    for lc in local:
        lc.wait()
    for cond, cp in sends:
        if cond is None:
            cp.wait_send()
        else:
            pl.when(cond)(cp.wait_send)


def reduce_all(ns, nz, lo, gt, gb, g4, gu, gd):
    t, d = lo.shape
    m = ns.bit_length() - 1
    dma = pltpu.SemaphoreType.DMA
    gs = (g4, gu, gd)
    unit = g4.shape[3] // ns

    def bufs(div):
        return [pltpu.VMEM((nz, a.shape[1], 2, a.shape[3] // div, a.shape[4]), BF) for a in gs]

    rec = []
    for i in range(3):
        rec += [bufs(2 << j)[i] for j in range(m)]
    outs = tuple(jax.ShapeDtypeStruct((a.shape[1], 2, unit, a.shape[4]), BF) for a in gs)
    n_items = 3 * nz
    return pl.pallas_call(
        functools.partial(reduce_kernel, ns, nz),
        out_shape=(
            jax.ShapeDtypeStruct((t * nz, d // nz), BF),
            jax.ShapeDtypeStruct((t * nz, d // nz), BF),
            jax.ShapeDtypeStruct(gb.shape, F32),
        )
        + outs,
        in_specs=[any_spec()] * 2 + [vmem_spec()] + [any_spec()] * 3,
        out_specs=(any_spec(),) * 2 + (vmem_spec(),) * 4,
        scratch_shapes=bufs(2)
        + rec
        + bufs(ns)
        + bufs(ns)
        + [
            pltpu.VMEM((m + 1,) + gb.shape, F32),
            pltpu.VMEM((m,) + gb.shape, F32),
            pltpu.VMEM((nz,) + gb.shape, F32),
            dma((2 + 2 * n_items,)),
            dma((2 * (nz - 1),)),
            dma((2 * (nz - 1),)),
            dma((n_items * m * 2,)),
            dma((n_items * m * 2,)),
            dma((n_items * 4,)),
            dma((n_items * 4,)),
            dma((m + nz - 1,)),
            dma((m + nz - 1,)),
        ],
        name="reduce_all",
        compiler_params=pltpu.CompilerParams(
            collective_id=3, has_side_effects=True, vmem_limit_bytes=58 * 2**20
        ),
    )(lo, gt, gb, g4, gu, gd)


def layer_norm(rows, gain, bias):
    mean_row = jnp.mean(rows, axis=-1, keepdims=True)
    centered = rows - mean_row
    variance = jnp.mean(centered * centered, axis=-1, keepdims=True)
    return centered * lax.rsqrt(variance + EPS) * gain + bias


def dot(spec, a, b):
    return jnp.einsum(spec, a, b, preferred_element_type=F32)


def shards(ns, nz, tokens, lengths, pad_mask, w_qkv, w_out, w_up, w_down, norm_gains, norm_biases, out_cotangent):
    rows = tokens.shape[0]
    t = rows // nz
    d = w_qkv.shape[1]
    nh = d // HD
    gh = nh // nz
    ew = d // nz
    blk = math.gcd(t, UNIT)
    nb = t // blk
    s, h = lax.axis_index("seq"), lax.axis_index("head")

    ends = jnp.cumsum(lengths)

    def item_at(p):
        return jnp.sum((p[..., None] >= ends).astype(jnp.int32), axis=-1)

    ndev = ns * nz
    last = item_at((jnp.arange(ndev, dtype=jnp.int32) + 1) * t - 1)
    before = jnp.concatenate([jnp.full((1,), -1, jnp.int32), last[:-1]])
    me = s * nz + h
    chunk = item_at(me * t + jnp.arange(nb, dtype=jnp.int32) * blk)
    prior = lax.dynamic_slice_in_dim(before, me, 1)
    cflag = (chunk == jnp.concatenate([prior, chunk[:-1]])).astype(F32)
    last2, before2 = last.reshape(ns, nz), before.reshape(ns, nz)
    my_last, my_before = last2[s], before2[s]
    sidx, zidx = jnp.arange(ns), jnp.arange(nz)
    fwt = (my_last == my_last[-1]).astype(F32)
    fwp = ((sidx[None, :] < s) & (last2[None, :, -1] == my_before[:, None])).astype(F32)
    fwl = ((zidx[None, :] < zidx[:, None]) & (my_last[None, :] == my_before[:, None])).astype(F32)
    bwt = (my_before == my_before[0]).astype(F32)
    bwp = ((sidx[None, :] > s) & (before2[None, :, 0] == my_last[:, None])).astype(F32)
    bwl = ((zidx[None, :] > zidx[:, None]) & (my_before[None, :] == my_last[:, None])).astype(F32)

    w4 = jnp.concatenate([w_qkv, w_out.T[None]], axis=0)
    x, co, w4g, wug, wdg = gather_all(ns, nz, tokens, out_cotangent, w4, w_up[None], w_down[None])
    wug, wdg = wug[:, 0], wdg[:, 0]
    pad = lax.dynamic_slice_in_dim(pad_mask, h * t, t).astype(F32)[:, None]
    xf = x.astype(F32)
    a1f, pull1 = jax.vjp(layer_norm, xf, norm_gains[0], norm_biases[0])
    a1 = a1f.astype(BF)
    qkv = dot("td,hcde->cthe", a1, w4g[:, :3]).reshape(3, t, d)
    q, k = qkv[0], qkv[1]
    fq = jnp.where(q > 0, q + 1.0, jnp.exp(jnp.minimum(q, 0.0))).astype(BF)
    fk = (pad * jnp.where(k > 0, k + 1.0, jnp.exp(jnp.minimum(k, 0.0)))).astype(BF)
    vb = qkv[2].astype(BF)

    def heads(a):
        return a.reshape(nb, blk, nh, HD)

    fqh, fkh, vbh = heads(fq), heads(fk), heads(vb)
    inc = dot("nuhk,nuhv->nhkv", fkh, vbh)
    zinc = jnp.sum(fkh.astype(F32), axis=1)

    def pack(state, norm):
        m1 = state.reshape(nz, gh, HD, HD).transpose(0, 2, 1, 3).reshape(nz, HD, ew)
        m2 = jnp.pad(norm.reshape(nz, 1, ew), ((0, 0), (0, MSG - HD - 1), (0, 0)))
        return jnp.concatenate([m1, m2], axis=1).astype(BF)

    def unpack(msg):
        msg = msg.astype(F32)
        st = msg[:, :HD].reshape(nz, HD, gh, HD).transpose(0, 2, 1, 3).reshape(nh, HD, HD)
        return st, msg[:, HD].reshape(nh, HD)

    sl, zl = inc[0], zinc[0]
    for n in range(1, nb):
        sl, zl = cflag[n] * sl + inc[n], cflag[n] * zl + zinc[n]
    st, zt = unpack(scan_states(ns, nz, 1, fwt, fwp, fwl, pack(sl, zl)))
    states, norms = [], []
    for n in range(nb):
        states.append(cflag[n] * st)
        norms.append(cflag[n] * zt)
        st, zt = cflag[n] * st + inc[n], cflag[n] * zt + zinc[n]
    states = jnp.stack(states).astype(BF)
    norms = jnp.stack(norms)
    causal = (jnp.arange(blk)[:, None] >= jnp.arange(blk)[None, :]).astype(F32)
    scores = (causal * dot("nthk,nuhk->nhtu", fqh, fkh)).astype(BF)
    numer = dot("nhtu,nuhv->nthv", scores, vbh) + dot("nthk,nhkv->nthv", fqh, states)
    ks = dot("tu,nuhk->nthk", causal.astype(BF), fkh) + norms[:, None]
    den = 1.0 + jnp.sum(fqh.astype(F32) * ks, axis=-1)
    att = (numer / den[..., None]).reshape(t, d).astype(BF)
    wot = w4g[:, 3]
    mid = xf + dot("the,hde->td", att.reshape(t, nz, ew), wot)
    a2f, pull2 = jax.vjp(layer_norm, mid, norm_gains[1], norm_biases[1])
    a2 = a2f.astype(BF)
    up = dot("td,hdf->thf", a2, wug)
    gel, pullg = jax.vjp(jax.nn.gelu, up)
    hid = gel.astype(BF)
    lo = (mid + dot("thf,hfd->td", hid, wdg)).astype(BF)
    d_up = pullg(dot("td,hfd->thf", co, wdg))[0].astype(BF)
    d_a2 = dot("thf,hdf->td", d_up, wug)
    d_mid_n, gain2, bias2 = pull2(d_a2)
    d_mid = co.astype(F32) + d_mid_n
    dml = d_mid.astype(BF)
    d_att = dot("td,hde->the", dml, wot).reshape(nb, blk, nh, HD)
    d_num = (d_att / den[..., None]).astype(BF)
    d_den = -jnp.sum(d_att * numer, axis=-1) / (den * den)
    d_ks = d_den[..., None] * fqh.astype(F32)
    gloc = dot("nthk,nthv->nhkv", fqh, d_num)
    yloc = jnp.sum(d_ks, axis=1)
    sl, zl = cflag[nb - 1] * gloc[nb - 1], cflag[nb - 1] * yloc[nb - 1]
    for n in range(nb - 2, -1, -1):
        sl, zl = cflag[n] * (sl + gloc[n]), cflag[n] * (zl + yloc[n])
    st, zt = unpack(scan_states(ns, nz, 2, bwt, bwp, bwl, pack(sl, zl)))
    d_inc, d_zinc = [None] * nb, [None] * nb
    for n in range(nb - 1, -1, -1):
        d_inc[n], d_zinc[n] = st, zt
        st, zt = cflag[n] * (st + gloc[n]), cflag[n] * (zt + yloc[n])
    d_inc = jnp.stack(d_inc).astype(BF)
    d_zinc = jnp.stack(d_zinc)
    d_scores = (causal * dot("nthv,nuhv->nhtu", d_num, vbh)).astype(BF)
    d_fq = (
        d_den[..., None] * ks
        + dot("nthv,nhkv->nthk", d_num, states)
        + dot("nhtu,nuhk->nthk", d_scores, fkh)
    )
    d_fk = (
        dot("tu,nthk->nuhk", causal.astype(BF), d_ks.astype(BF))
        + dot("nhtu,nthk->nuhk", d_scores, fqh)
        + dot("nuhv,nhkv->nuhk", vbh, d_inc)
        + d_zinc[:, None]
    )
    d_v = dot("nhtu,nthv->nuhv", scores, d_num) + dot("nuhk,nhkv->nuhv", fkh, d_inc)
    d_q = (d_fq.reshape(t, d) * jnp.where(q > 0, 1.0, jnp.exp(jnp.minimum(q, 0.0)))).astype(BF)
    d_k = (d_fk.reshape(t, d) * pad * jnp.where(k > 0, 1.0, jnp.exp(jnp.minimum(k, 0.0)))).astype(BF)
    d_qkv = jnp.stack([d_q, d_k, d_v.reshape(t, d).astype(BF)]).reshape(3, t, nz, ew)
    d_a1 = dot("cthe,hcde->td", d_qkv, w4g[:, :3])
    d_x, gain1, bias1 = pull1(d_a1)
    gt = (d_mid + d_x).astype(BF)

    o0, o1 = bit_orders(ns)
    m = ns.bit_length() - 1

    def perm(a):
        u = d // (2 * ns)
        a = a.reshape((t,) + (2,) * m + (2, u))
        parts = []
        for f, order in enumerate(([0] + o0, [0] + o1)):
            v = a[..., f, :]
            v = v.transpose((0,) + tuple(m - b for b in order) + (m + 1,))
            parts.append(v.reshape(t, d // 2))
        return jnp.concatenate(parts, axis=1)

    a1p = perm(a1)
    g_qkv = dot("td,cthe->hcde", a1p, d_qkv).astype(BF)
    g_out = dot("td,the->hde", perm(dml), att.reshape(t, nz, ew)).astype(BF)
    g4 = jnp.concatenate([g_qkv, g_out[:, None]], axis=1).reshape(nz, 4, 2, d // 2, ew)
    ff = w_up.shape[1]
    gu = dot("td,thf->hdf", perm(a2), d_up).astype(BF).reshape(nz, 1, 2, d // 2, ff)
    gd = dot("td,thf->hdf", perm(co), hid).astype(BF).reshape(nz, 1, 2, d // 2, ff)
    gb = jnp.concatenate([jnp.stack([gain1, gain2, bias1, bias2]), jnp.zeros((4, d), F32)])
    lo_o, gt_o, gbo, o4, ou, od = reduce_all(ns, nz, lo, gt, gb, g4, gu, gd)
    piece = d // ns
    o4 = o4.reshape(4, piece, ew).astype(F32)
    w = d // ndev
    gbs = lax.dynamic_slice_in_dim(gbo, (h * ns + s) * w, w, 1)
    return (
        lo_o,
        gt_o.astype(F32),
        o4[:3],
        o4[3].T,
        ou.reshape(piece, ff).astype(F32),
        od.reshape(piece, ff).astype(F32).T,
        gbs[:2],
        gbs[2:4],
    )


def solution(mesh):
    in_specs = (
        P("seq", "head"),
        P(),
        P("seq"),
        P(None, None, "head"),
        P("head", None),
        P(None, "head"),
        P("head", None),
        P(),
        P(),
        P("seq", "head"),
    )
    out_specs = (
        P("seq", "head"),
        P("seq", "head"),
        P(None, "seq", "head"),
        P("head", "seq"),
        P("seq", "head"),
        P("head", "seq"),
        P(None, ("head", "seq")),
        P(None, ("head", "seq")),
    )
    f = functools.partial(shards, mesh.shape["seq"], mesh.shape["head"])
    return jax.shard_map(f, mesh=mesh, in_specs=in_specs, out_specs=out_specs, check_vma=False)
```

```python
import functools
import math

import jax
import jax.numpy as jnp
from jax import lax
from jax.experimental import pallas as pl
from jax.experimental.pallas import tpu as pltpu
from jax.sharding import PartitionSpec as P

HD = 64
UNIT = 768
EPS = 1e-05
MESH = pl.DeviceIdType.MESH
BF = jnp.bfloat16
F32 = jnp.float32


def bit_orders(ns):
    m = ns.bit_length() - 1
    xs = list(range(1, 1 + (m - 1) // 2))
    ys = list(range(1 + (m - 1) // 2, m))
    return xs + ys, ys + xs


def bits_to(s, order):
    out = 0
    for j, b in enumerate(order):
        out = out + (((s >> b) & 1) << j)
    return out


def rcopy(src, dst, send, recv, dev):
    return pltpu.make_async_remote_copy(
        src_ref=src, dst_ref=dst, send_sem=send, recv_sem=recv, device_id=dev, device_id_type=MESH
    )


def enter(devs):
    bar = pltpu.get_barrier_semaphore()
    for d in devs:
        pl.semaphore_signal(bar, inc=1, device_id=d, device_id_type=MESH)
    pl.semaphore_wait(bar, len(devs))


def z_others(s, h, nz):
    return [(s, lax.rem(h + d, nz)) for d in range(1, nz)]


def run_waves(groups):
    live = []
    pending = list(groups)
    while pending or live:
        if pending:
            live.append(pending.pop(0))
        nxt = []
        for group in live:
            kept = []
            for gen in group:
                try:
                    next(gen)
                    kept.append(gen)
                except StopIteration:
                    pass
            if kept:
                nxt.append(kept)
        live = nxt


def gather_kernel(ns, nz, tok, cot, w4, wu, wd, x, co, w4g, wug, wdg, lsem, tsend, trecv, zsend, zrecv, psend, precv):
    s, h = lax.axis_index("seq"), lax.axis_index("head")
    o0, o1 = bit_orders(ns)
    orders = (o0 + [0], o1 + [0])
    m = len(orders[0])
    t = x.shape[0]
    ew = tok.shape[1]
    arrays = ((w4, w4g), (wu, wug), (wd, wdg))
    half = w4.shape[1] // 2
    r = half // ns
    zdev = z_others(s, h, nz)
    enter(zdev + [(jnp.bitwise_xor(s, 1 << b), h) for b in orders[0]])
    sends = []
    local = []

    def a2a(i, src, dst):
        for d, dev in enumerate(zdev):
            cp = rcopy(
                src.at[pl.ds(dev[1] * t, t), :],
                dst.at[:, pl.ds(h * ew, ew)],
                tsend.at[i * (nz - 1) + d],
                trecv.at[i * (nz - 1) + d],
                dev,
            )
            cp.start()
            sends.append((None, cp))
        lc = pltpu.make_async_copy(src.at[pl.ds(h * t, t), :], dst.at[:, pl.ds(h * ew, ew)], lsem.at[i])
        lc.start()
        local.append(lc)

    def a2a_wait(i, src, dst):
        for d in range(nz - 1):
            frm = lax.rem(h + nz - 1 - d, nz)
            rcopy(
                src.at[pl.ds(h * t, t), :],
                dst.at[:, pl.ds(frm * ew, ew)],
                tsend.at[i * (nz - 1) + d],
                trecv.at[i * (nz - 1) + d],
                (s, frm),
            ).wait_recv()

    pos = [bits_to(s, order) for order in orders]

    def zsem(a, f, k, d):
        return ((a * 2 + f) * (nz - 1) + k) * 2 + d

    def zcopy(a, f, k, d, origin, own):
        w, wg = arrays[a]
        rows = pl.ds(f * half + pos[f] * r, r)
        dst = wg.at[origin, :, rows, :]
        src = w.at[:, rows, :] if own else dst
        i = zsem(a, f, k, d)
        return rcopy(src, dst, zsend.at[i], zrecv.at[i], (s, h + 1 if d == 0 else h - 1))

    def zstart(a, f, k, d, origin, cond):
        cp = zcopy(a, f, k, d, origin, k == 0)
        pl.when(cond)(cp.start)
        sends.append((cond, cp))

    def piece(a, f, k, d):
        wg = arrays[a][1]
        origin = h - 1 - k if d == 0 else h + 1 + k
        valid = origin >= 0 if d == 0 else origin < nz
        pl.when(valid)(zcopy(a, f, k, d, origin, False).wait_recv)
        if k + 1 < nz - 1:
            more = valid & ((h + 1 < nz) if d == 0 else (h >= 1))
            zstart(a, f, k + 1, d, origin, more)
        for j, b in enumerate(orders[f]):
            n = r << j
            begin = (pos[f] >> j) << j
            other = jnp.bitwise_xor(begin, 1 << j)
            i = zsem(a, f, k, d) * m + j
            dev = (jnp.bitwise_xor(s, 1 << b), h)
            mine = wg.at[origin, :, pl.ds(f * half + begin * r, n), :]
            theirs = wg.at[origin, :, pl.ds(f * half + other * r, n), :]
            out = rcopy(mine, mine, psend.at[i], precv.at[i], dev)
            pl.when(valid)(out.start)
            sends.append((valid, out))
            yield
            pl.when(valid)(rcopy(theirs, theirs, psend.at[i], precv.at[i], dev).wait_recv)

    a2a(0, tok, x)
    for a in range(3):
        for f in range(2):
            zstart(a, f, 0, 0, h, h + 1 < nz)
            zstart(a, f, 0, 1, h, h >= 1)
        if a == 0:
            a2a(1, cot, co)
    for a, (w, wg) in enumerate(arrays):
        lc = pltpu.make_async_copy(w, wg.at[h], lsem.at[2 + a])
        lc.start()
        local.append(lc)
    groups = [[piece(a, f, k, d) for d in range(2) for f in range(2)] for a in range(3) for k in range(nz - 1)]
    run_waves(groups)
    a2a_wait(0, tok, x)
    a2a_wait(1, cot, co)
    for lc in local:
        lc.wait()
    for cond, cp in sends:
        if cond is None:
            cp.wait_send()
        else:
            pl.when(cond)(cp.wait_send)


def any_spec():
    return pl.BlockSpec(memory_space=pl.ANY)


def vmem_spec():
    return pl.BlockSpec(memory_space=pltpu.VMEM)


def smem_spec():
    return pl.BlockSpec(memory_space=pltpu.SMEM)


def gather_all(ns, nz, tok, cot, w4, wu, wd):
    t, d = tok.shape[0] // nz, w4.shape[1]
    m = ns.bit_length() - 1
    nzs = 3 * 2 * (nz - 1) * 2
    dma = pltpu.SemaphoreType.DMA
    return pl.pallas_call(
        functools.partial(gather_kernel, ns, nz),
        out_shape=(
            jax.ShapeDtypeStruct((t, d), BF),
            jax.ShapeDtypeStruct((t, d), BF),
            jax.ShapeDtypeStruct((nz,) + w4.shape, BF),
            jax.ShapeDtypeStruct((nz,) + wu.shape, BF),
            jax.ShapeDtypeStruct((nz,) + wd.shape, BF),
        ),
        in_specs=[any_spec()] * 5,
        out_specs=(any_spec(),) * 5,
        scratch_shapes=[
            dma((5,)),
            dma((2 * (nz - 1),)),
            dma((2 * (nz - 1),)),
            dma((nzs,)),
            dma((nzs,)),
            dma((nzs * m,)),
            dma((nzs * m,)),
        ],
        name="gather_all",
        compiler_params=pltpu.CompilerParams(collective_id=0, has_side_effects=True),
    )(tok, cot, w4, wu, wd)


def scan_kernel(ns, nz, wt, wp, wl, msg, out, r1, r2, tot, outb, s1, q1, s2, q2, s3, q3):
    s, h = lax.axis_index("seq"), lax.axis_index("head")
    zdev = z_others(s, h, nz)
    sdev = [(jnp.bitwise_xor(s, d), h) for d in range(1, ns)]
    enter(zdev + sdev)
    sends = []
    for d, dev in enumerate(zdev):
        cp = rcopy(msg.at[dev[1]], r1.at[h], s1.at[d], q1.at[d], dev)
        cp.start()
        sends.append(cp)
    r1[h] = msg[h]
    for d in range(nz - 1):
        frm = lax.rem(h + nz - 1 - d, nz)
        rcopy(r1.at[frm], r1.at[frm], s1.at[d], q1.at[d], (s, frm)).wait_recv()
    total = jnp.zeros(tot.shape, F32)
    for z in range(nz):
        total = total + wt[z] * r1[z].astype(F32)
    tot[...] = total.astype(BF)
    for d, dev in enumerate(sdev):
        cp = rcopy(tot, r2.at[s], s2.at[d], q2.at[d], dev)
        cp.start()
        sends.append(cp)
    r2[s] = tot[...]
    line = [sum(wl[z, k] * r1[k].astype(F32) for k in range(nz)) for z in range(nz)]
    for d in range(ns - 1):
        frm = jnp.bitwise_xor(s, d + 1)
        rcopy(r2.at[frm], r2.at[frm], s2.at[d], q2.at[d], (frm, h)).wait_recv()
    for k in range(ns):
        got = r2[k].astype(F32)
        line = [line[z] + wp[z, k] * got for z in range(nz)]
    for z in range(nz):
        outb[z] = line[z].astype(BF)
    for d, dev in enumerate(zdev):
        cp = rcopy(outb.at[dev[1]], out.at[h], s3.at[d], q3.at[d], dev)
        cp.start()
        sends.append(cp)
    out[h] = outb[h]
    for d in range(nz - 1):
        frm = lax.rem(h + nz - 1 - d, nz)
        rcopy(out.at[frm], out.at[frm], s3.at[d], q3.at[d], (s, frm)).wait_recv()
    for cp in sends:
        cp.wait_send()


def scan_states(ns, nz, cid, wt, wp, wl, msg):
    dma = pltpu.SemaphoreType.DMA
    one = msg.shape[1:]
    return pl.pallas_call(
        functools.partial(scan_kernel, ns, nz),
        out_shape=jax.ShapeDtypeStruct(msg.shape, BF),
        in_specs=[smem_spec()] * 3 + [vmem_spec()],
        out_specs=vmem_spec(),
        scratch_shapes=[
            pltpu.VMEM(msg.shape, BF),
            pltpu.VMEM((ns,) + one, BF),
            pltpu.VMEM(one, BF),
            pltpu.VMEM(msg.shape, BF),
            dma((nz - 1,)),
            dma((nz - 1,)),
            dma((ns - 1,)),
            dma((ns - 1,)),
            dma((nz - 1,)),
            dma((nz - 1,)),
        ],
        name="scan_states",
        compiler_params=pltpu.CompilerParams(collective_id=cid, has_side_effects=True),
    )(wt, wp, wl, msg)


def add_rows(dst, lead, start, src, src_lead, src_start, n):
    blk = min(n, 32)

    def step(i, _):
        a = dst[lead + (pl.ds(pl.multiple_of(start + i * blk, 16), blk), slice(None))]
        b = src[src_lead + (pl.ds(pl.multiple_of(src_start + i * blk, 16), blk), slice(None))]
        dst[lead + (pl.ds(pl.multiple_of(start + i * blk, 16), blk), slice(None))] = (
            a.astype(F32) + b.astype(F32)
        ).astype(BF)
        return 0

    lax.fori_loop(0, n // blk, step, 0)


def reduce_kernel(ns, nz, lo, gt, gb, *refs):
    s, h = lax.axis_index("seq"), lax.axis_index("head")
    o0, o1 = bit_orders(ns)
    orders = ([0] + o0, [0] + o1)
    m = len(orders[0])
    g = refs[:3]
    lo_out, gt_out, gbo = refs[3:6]
    outs = refs[6:9]
    sc = refs[9:]
    acc = sc[0:3]
    rec = [sc[3 + i * m : 3 + (i + 1) * m] for i in range(3)]
    base = 3 + 3 * m
    zl, zr = sc[base : base + 3], sc[base + 3 : base + 6]
    gcur, grec, gz = sc[base + 6 : base + 9]
    lsem, tsend, trecv, csend, crecv, zsend, zrecv, gsend, grecv = sc[base + 9 :]
    t = lo.shape[0]
    ew = lo_out.shape[1]
    unit = g[0].shape[3] // ns
    zdev = z_others(s, h, nz)
    enter(zdev + [(jnp.bitwise_xor(s, 1 << b), h) for b in orders[0]])
    sends = []
    local = []

    def a2a(i, src, dst):
        for d, dev in enumerate(zdev):
            cp = rcopy(
                src.at[:, pl.ds(dev[1] * ew, ew)],
                dst.at[pl.ds(h * t, t), :],
                tsend.at[i * (nz - 1) + d],
                trecv.at[i * (nz - 1) + d],
                dev,
            )
            cp.start()
            sends.append((None, cp))
        lc = pltpu.make_async_copy(src.at[:, pl.ds(h * ew, ew)], dst.at[pl.ds(h * t, t), :], lsem.at[i])
        lc.start()
        local.append(lc)

    def a2a_wait(i, src, dst):
        for d in range(nz - 1):
            frm = lax.rem(h + nz - 1 - d, nz)
            rcopy(
                src.at[:, pl.ds(h * ew, ew)],
                dst.at[pl.ds(frm * t, t), :],
                tsend.at[i * (nz - 1) + d],
                trecv.at[i * (nz - 1) + d],
                (s, frm),
            ).wait_recv()

    def item(a, tz):
        c = g[a].shape[1]
        idx = a * nz + tz
        pos = [0, 0]
        for j in range(m + 1):
            if j > 0:
                for f in range(2):
                    i = (idx * m + j - 1) * 2 + f
                    n = unit * (ns >> j)
                    buf = rec[a][j - 1].at[tz, :, f]
                    rcopy(buf, buf, csend.at[i], crecv.at[i], (s, h)).wait_recv()
                    if j == 1:
                        pltpu.make_async_copy(
                            acc[a].at[tz, :, f], acc[a].at[tz, :, f], lsem.at[2 + idx * 2 + f]
                        ).wait()
                    for cc in range(c):
                        add_rows(acc[a], (tz, cc, f), pos[f], rec[a][j - 1], (tz, cc, f), 0, n)
            if j < m:
                for f in range(2):
                    i = (idx * m + j) * 2 + f
                    n = unit * (ns >> (j + 1))
                    b = (s >> orders[f][j]) & 1
                    dev = (jnp.bitwise_xor(s, 1 << orders[f][j]), h)
                    if j == 0:
                        src = g[a].at[tz, :, f, pl.ds((1 - b) * n, n), :]
                        lc = pltpu.make_async_copy(
                            g[a].at[tz, :, f, pl.ds(b * n, n), :], acc[a].at[tz, :, f], lsem.at[2 + idx * 2 + f]
                        )
                        lc.start()
                    else:
                        src = acc[a].at[tz, :, f, pl.ds(pl.multiple_of(pos[f] + (1 - b) * n, 16), n), :]
                        pos[f] = pos[f] + b * n
                    cp = rcopy(src, rec[a][j].at[tz, :, f], csend.at[i], crecv.at[i], dev)
                    cp.start()
                    sends.append((None, cp))
            yield
        for d, (buf, cond, first, nb) in enumerate(
            ((zl, h < tz, h >= 1, h + 1), (zr, h > tz, h + 1 < nz, h - 1))
        ):
            for f in range(2):
                i = (idx * 2 + d) * 2 + f
                mine = acc[a].at[tz, :, f, pl.ds(pl.multiple_of(pos[f], 16), unit), :]
                cp = rcopy(mine, buf[a].at[tz, :, f], zsend.at[i], zrecv.at[i], (s, nb))

                def relay(cp=cp, f=f, d=d, buf=buf, first=first):
                    def more():
                        cp.wait_recv()
                        for cc in range(c):
                            add_rows(acc[a], (tz, cc, f), pos[f], buf[a], (tz, cc, f), 0, unit)

                    pl.when(first)(more)
                    cp.start()

                pl.when(cond)(relay)
                sends.append((cond, cp))
        yield

        def finish():
            for f in range(2):
                for d, (buf, there) in enumerate(((zl, tz > 0), (zr, tz < nz - 1))):
                    if there:
                        i = (idx * 2 + d) * 2 + f
                        rcopy(
                            buf[a].at[tz, :, f], buf[a].at[tz, :, f], zsend.at[i], zrecv.at[i], (s, h)
                        ).wait_recv()
                for cc in range(c):
                    v = acc[a][tz, cc, f, pl.ds(pl.multiple_of(pos[f], 16), unit), :].astype(F32)
                    if tz > 0:
                        v = v + zl[a][tz, cc, f].astype(F32)
                    if tz < nz - 1:
                        v = v + zr[a][tz, cc, f].astype(F32)
                    outs[a][cc, f] = v.astype(BF)

        pl.when(h == tz)(finish)

    def small():
        gcur[0] = gb[...]
        for j, b in enumerate(orders[0]):
            dev = (jnp.bitwise_xor(s, 1 << b), h)
            cp = rcopy(gcur.at[j], grec.at[j], gsend.at[j], grecv.at[j], dev)
            cp.start()
            sends.append((None, cp))
            yield
            cp.wait_recv()
            gcur[j + 1] = gcur[j] + grec[j]
        for d, dev in enumerate(zdev):
            cp = rcopy(gcur.at[m], gz.at[h], gsend.at[m + d], grecv.at[m + d], dev)
            cp.start()
            sends.append((None, cp))
        gz[h] = gcur[m]
        yield
        for d in range(nz - 1):
            frm = lax.rem(h + nz - 1 - d, nz)
            rcopy(gz.at[frm], gz.at[frm], gsend.at[m + d], grecv.at[m + d], (s, frm)).wait_recv()
        total = gz[0]
        for z in range(1, nz):
            total = total + gz[z]
        gbo[...] = total

    a2a(0, lo, lo_out)
    order = [2, 1, 0]
    groups = [[item(a, tz)] for a in order for tz in range(nz)]
    groups[1].append(small())
    a2a(1, gt, gt_out)
    run_waves(groups)
    a2a_wait(0, lo, lo_out)
    a2a_wait(1, gt, gt_out)
    for lc in local:
        lc.wait()
    for cond, cp in sends:
        if cond is None:
            cp.wait_send()
        else:
            pl.when(cond)(cp.wait_send)


def reduce_all(ns, nz, lo, gt, gb, g4, gu, gd):
    t, d = lo.shape
    m = ns.bit_length() - 1
    dma = pltpu.SemaphoreType.DMA
    gs = (g4, gu, gd)
    unit = g4.shape[3] // ns

    def bufs(div):
        return [pltpu.VMEM((nz, a.shape[1], 2, a.shape[3] // div, a.shape[4]), BF) for a in gs]

    rec = []
    for i in range(3):
        rec += [bufs(2 << j)[i] for j in range(m)]
    outs = tuple(jax.ShapeDtypeStruct((a.shape[1], 2, unit, a.shape[4]), BF) for a in gs)
    n_items = 3 * nz
    return pl.pallas_call(
        functools.partial(reduce_kernel, ns, nz),
        out_shape=(
            jax.ShapeDtypeStruct((t * nz, d // nz), BF),
            jax.ShapeDtypeStruct((t * nz, d // nz), BF),
            jax.ShapeDtypeStruct(gb.shape, F32),
        )
        + outs,
        in_specs=[any_spec()] * 2 + [vmem_spec()] + [any_spec()] * 3,
        out_specs=(any_spec(),) * 2 + (vmem_spec(),) * 4,
        scratch_shapes=bufs(2)
        + rec
        + bufs(ns)
        + bufs(ns)
        + [
            pltpu.VMEM((m + 1,) + gb.shape, F32),
            pltpu.VMEM((m,) + gb.shape, F32),
            pltpu.VMEM((nz,) + gb.shape, F32),
            dma((2 + 2 * n_items,)),
            dma((2 * (nz - 1),)),
            dma((2 * (nz - 1),)),
            dma((n_items * m * 2,)),
            dma((n_items * m * 2,)),
            dma((n_items * 4,)),
            dma((n_items * 4,)),
            dma((m + nz - 1,)),
            dma((m + nz - 1,)),
        ],
        name="reduce_all",
        compiler_params=pltpu.CompilerParams(
            collective_id=3, has_side_effects=True, vmem_limit_bytes=58 * 2**20
        ),
    )(lo, gt, gb, g4, gu, gd)


def dot(a, b):
    return lax.dot_general(a, b, (((1,), (0,)), ((), ())), preferred_element_type=F32)


def dot_t(a, b):
    return lax.dot_general(a, b, (((1,), (1,)), ((), ())), preferred_element_type=F32)


def t_dot(a, b):
    return lax.dot_general(a, b, (((0,), (0,)), ((), ())), preferred_element_type=F32)


def lane_low(shape):
    return lax.broadcasted_iota(jnp.int32, shape, 1) < HD


def row_low(shape):
    return lax.broadcasted_iota(jnp.int32, shape, 0) < HD


def row_block(t):
    return 96 if t % 96 == 0 else 32


def over_rows(t, body):
    rb = row_block(t)

    def step(i, _):
        body(pl.ds(pl.multiple_of(i * rb, 32), rb))
        return 0

    lax.fori_loop(0, t // rb, step, 0)


def normed(v):
    mean = jnp.mean(v, axis=1, keepdims=True)
    c = v - mean
    w = lax.rsqrt(jnp.mean(c * c, axis=1, keepdims=True) + EPS)
    return c * w, w


def norm_forward(src, gain, bias, dst):
    def body(rows):
        xh, _ = normed(src[rows, :].astype(F32))
        dst[rows, :] = (xh * gain[...] + bias[...]).astype(BF)

    over_rows(src.shape[0], body)


def norm_backward(e_ref, src, gain, add, emit, sums):
    sums[0] = jnp.zeros(sums.shape[1:], F32)
    sums[1] = jnp.zeros(sums.shape[1:], F32)

    def body(rows):
        e = e_ref[rows, :]
        xh, w = normed(src[rows, :].astype(F32))
        eg = e * gain[...]
        m1 = jnp.mean(eg, axis=1, keepdims=True)
        m2 = jnp.mean(eg * xh, axis=1, keepdims=True)
        emit(rows, add[rows, :].astype(F32) + w * (eg - m1 - xh * m2))
        n = e.shape[0]
        sums[0] += jnp.sum((e * xh).reshape(n // 8, 8, -1), axis=0)
        sums[1] += jnp.sum(e.reshape(n // 8, 8, -1), axis=0)

    over_rows(src.shape[0], body)


def transpose_perm(ns, src, dst):
    d = dst.shape[0]
    u = d // (2 * ns)
    o0, o1 = bit_orders(ns)
    m = ns.bit_length() - 1
    orders = ([0] + o0, [0] + o1)
    for j in range(d // 128):
        tr = src[:, j * 128 : (j + 1) * 128].T
        for i in range(128 // u):
            g = j * (128 // u) + i
            dev, f = g // 2, g % 2
            q = sum(((dev >> b) & 1) << (m - 1 - k) for k, b in enumerate(orders[f]))
            row = f * (d // 2) + q * u
            dst[row : row + u, :] = tr[i * u : (i + 1) * u, :]


def phi(y):
    return jnp.where(y > 0, y + 1.0, jnp.exp(jnp.minimum(y, 0.0)))


def cols(i, n):
    return pl.ds(pl.multiple_of(i * n, 128), n)


def project(a1, wg, g, pad, fq, fk, vb):
    ew = wg.shape[3]
    c = cols(g, ew)
    fq[:, c] = phi(dot(a1[...], wg[g, 0])).astype(BF)
    fk[:, c] = (pad[...] * phi(dot(a1[...], wg[g, 1]))).astype(BF)
    vb[:, c] = dot(a1[...], wg[g, 2]).astype(BF)


def with_ones(v2):
    one = jnp.ones_like(v2)
    low = lane_low(v2.shape)
    return jnp.where(low, v2, one), jnp.where(low, one, v2)


def chunk_sums(p, blk, nb, fk, vb, inc):
    for n in range(nb):
        rows = pl.ds(n * blk, blk)
        k2, v2 = fk[rows, cols(p, 128)], vb[rows, cols(p, 128)]
        r = t_dot(k2, jnp.concatenate(with_ones(v2), axis=1))
        inc[n, p] = jnp.where(row_low((128, 128)), r[:, :128], r[:, 128:])


def causal_mask(blk):
    return lax.broadcasted_iota(jnp.int32, (blk, blk), 0) >= lax.broadcasted_iota(jnp.int32, (blk, blk), 1)


def masked_scores(a2, b2, keep):
    low = lane_low(b2.shape)
    zero = jnp.zeros_like(b2)
    return [
        jnp.where(keep, dot_t(a2, b), 0.0).astype(BF)
        for b in (jnp.where(low, b2, zero), jnp.where(low, zero, b2))
    ]


def split_state(st):
    low = row_low(st.shape)
    zero = jnp.zeros_like(st)
    return jnp.concatenate([jnp.where(low, st, zero), jnp.where(low, zero, st)], axis=1)


def attend(p, n, blk, fq, fk, vb, st):
    rows = pl.ds(n * blk, blk)
    c = cols(p, 128)
    q2, k2, v2 = fq[rows, c], fk[rows, c], vb[rows, c]
    s0, s1 = masked_scores(q2, k2, causal_mask(blk))
    g0, g1 = with_ones(v2)
    r = dot(q2, split_state(st))
    return dot(s0, g0) + r[:, :128], dot(s1, g1) + r[:, 128:]


def attend_store(p, n, blk, r0, r1, att, rden):
    rows = pl.ds(n * blk, blk)
    low = lane_low(r0.shape)
    num = jnp.where(low, r0, r1)
    den = 1.0 + pltpu.roll(jnp.where(low, r1, r0), HD, 1)
    rd = 1.0 / den
    att[rows, cols(p, 128)] = (num * rd).astype(BF)
    rden[rows, cols(p, 128)] = rd


def attend_gradient(p, n, blk, datt, att, rden, dr0, dr1):
    rows = pl.ds(n * blk, blk)
    c = cols(p, 128)
    e = datt[rows, c]
    rd = rden[rows, c]
    low = lane_low(e.shape)
    lane = lax.broadcasted_iota(jnp.int32, e.shape, 1)
    dn = e * rd
    w = dn * att[rows, c].astype(F32)
    d0 = -jnp.sum(jnp.where(low, w, 0.0), axis=1, keepdims=True)
    d1 = -jnp.sum(jnp.where(low, 0.0, w), axis=1, keepdims=True)

    def parts(dd, first):
        hi = dd.astype(BF).astype(F32)
        return jnp.where(lane == first, hi, jnp.where(lane == first + 1, dd - hi, 0.0))

    dr0[rows, c] = jnp.where(low, dn, parts(d0, HD)).astype(BF)
    dr1[rows, c] = jnp.where(low, parts(d1, 0), dn).astype(BF)


def chunk_gradients(p, blk, nb, fq, dr0, dr1, ginc):
    for n in range(nb):
        rows = pl.ds(n * blk, blk)
        c = cols(p, 128)
        r = t_dot(fq[rows, c], jnp.concatenate([dr0[rows, c], dr1[rows, c]], axis=1))
        ginc[n, p] = jnp.where(row_low((128, 128)), r[:, :128], r[:, 128:])


def attend_backward(p, n, blk, fq, fk, vb, dr0, dr1, st, dst, dq, dk, dv):
    rows = pl.ds(n * blk, blk)
    c = cols(p, 128)
    q2, k2, v2, e0, e1 = fq[rows, c], fk[rows, c], vb[rows, c], dr0[rows, c], dr1[rows, c]
    g0, g1 = with_ones(v2)
    keep = causal_mask(blk)
    keep_t = lax.broadcasted_iota(jnp.int32, (blk, blk), 0) <= lax.broadcasted_iota(jnp.int32, (blk, blk), 1)
    low = lane_low(q2.shape)

    def pick(a, b):
        return jnp.where(low, a, b)

    ds0 = jnp.where(keep, dot_t(e0, g0), 0.0).astype(BF)
    ds1 = jnp.where(keep, dot_t(e1, g1), 0.0).astype(BF)
    dfq = pick(dot(ds0, k2), dot(ds1, k2)) + dot_t(jnp.concatenate([e0, e1], axis=1), split_state(st))
    dq[rows, c] = (dfq * jnp.minimum(q2.astype(F32), 1.0)).astype(BF)
    dt0 = jnp.where(keep_t, dot_t(g0, e0), 0.0).astype(BF)
    dt1 = jnp.where(keep_t, dot_t(g1, e1), 0.0).astype(BF)
    dfk = pick(dot(dt0, q2), dot(dt1, q2)) + dot_t(jnp.concatenate([g0, g1], axis=1), split_state(dst))
    dk[rows, c] = (dfk * jnp.minimum(k2.astype(F32), 1.0)).astype(BF)
    st0, st1 = masked_scores(k2, q2, keep_t)
    own = jnp.where(row_low((128, 128)) == lane_low((128, 128)), dst, jnp.zeros_like(dst))
    dv[rows, c] = (pick(dot(st0, e0), dot(st1, e1)) + dot(k2, own)).astype(BF)


def gelu_parts(s):
    c0 = math.sqrt(2.0 / math.pi)
    s2 = s * s
    th = jnp.tanh(c0 * (s + 0.044715 * s * s2))
    h = 0.5 * (1.0 + th)
    slope = h + 0.5 * s * (1.0 - th * th) * (c0 * (1.0 + 3 * 0.044715 * s2))
    return s * h, slope


def loop_pairs(n, body):
    def step(p, _):
        body(p)
        return 0

    lax.fori_loop(0, n, step, 0)


def front_kernel(nb, cflag, x, wg, gain, bias, pad, fq, fk, vb, inc, msg, a1):
    t, d = x.shape
    blk = t // nb
    norm_forward(x, gain, bias, a1)
    for g in range(wg.shape[0]):
        project(a1, wg, g, pad, fq, fk, vb)
    pg = msg.shape[1] // 128

    def pair(p):
        chunk_sums(p, blk, nb, fk, vb, inc)
        cur = inc[0, p]
        for n in range(1, nb):
            cur = cflag[n] * cur + inc[n, p]
        msg[p // pg, pl.ds(pl.multiple_of(lax.rem(p, pg) * 128, 128), 128), :] = cur.astype(BF)

    loop_pairs(d // 128, pair)


def middle_kernel(nb, cflag, sin, inc, fq, fk, vb, x, wot, gain, bias, att, rden, states, mid, a2):
    t, d = x.shape
    blk = t // nb
    pg = sin.shape[1] // 128

    def pair(p):
        cur = sin[p // pg, pl.ds(pl.multiple_of(lax.rem(p, pg) * 128, 128), 128), :].astype(F32)
        for n in range(nb):
            used = cflag[n] * cur
            st = used.astype(BF)
            states[n, p] = st
            cur = used + inc[n, p]
            r0, r1 = attend(p, n, blk, fq, fk, vb, st)
            attend_store(p, n, blk, r0, r1, att, rden)

    loop_pairs(d // 128, pair)
    ew = wot.shape[2]
    mid[...] = x[...].astype(F32)
    for g in range(wot.shape[0]):
        mid[...] += dot_t(att[:, g * ew : (g + 1) * ew], wot[g])
    norm_forward(mid, gain, bias, a2)


def ffn_kernel(ns, mid, a2, co, wu, wd, lo, da2, gu, gd, a2t, cot, acc, wub, wdb, gub, gdb, isem, osem):
    nz, d, ff = wu.shape
    tile = wub.shape[2]
    per = ff // tile
    steps = nz * per

    def fetch(i, slot):
        g, j = i // per, lax.rem(i, per)
        c = pl.ds(pl.multiple_of(j * tile, 128), tile)
        return (
            pltpu.make_async_copy(wu.at[g, :, c], wub.at[slot], isem.at[slot, 0]),
            pltpu.make_async_copy(wd.at[g, c, :], wdb.at[slot], isem.at[slot, 1]),
        )

    def flush(i, slot):
        g, j = i // per, lax.rem(i, per)
        c = pl.ds(pl.multiple_of(j * tile, 128), tile)
        return (
            pltpu.make_async_copy(gub.at[slot], gu.at[g, :, c], osem.at[slot, 0]),
            pltpu.make_async_copy(gdb.at[slot], gd.at[g, :, c], osem.at[slot, 1]),
        )

    for cp in fetch(0, 0):
        cp.start()
    transpose_perm(ns, a2, a2t)
    transpose_perm(ns, co, cot)
    acc[...] = mid[...]
    da2[...] = jnp.zeros_like(da2)

    def step(i, _):
        slot = lax.rem(i, 2)

        @pl.when(i + 1 < steps)
        def _():
            for cp in fetch(i + 1, 1 - slot):
                cp.start()

        for cp in fetch(i, slot):
            cp.wait()

        @pl.when(i >= 2)
        def _():
            for cp in flush(i - 2, slot):
                cp.wait()

        up = dot(a2[...], wub[slot])
        hidf, slope = gelu_parts(up)
        hid = hidf.astype(BF)
        acc[...] += dot(hid, wdb[slot])
        gdb[slot] = dot(cot[...], hid).astype(BF)
        dup = (slope * dot_t(co[...], wdb[slot])).astype(BF)
        da2[...] += dot_t(dup, wub[slot])
        gub[slot] = dot(a2t[...], dup).astype(BF)
        for cp in flush(i, slot):
            cp.start()
        return 0

    lax.fori_loop(0, steps, step, 0)
    for i in range(max(0, steps - 2), steps):
        for cp in flush(i, i % 2):
            cp.wait()
    lo[...] = acc[...].astype(BF)


def turn_kernel(nb, cflag, da2, mid, co, gain, wot, fq, att, rden, dmid, dml, dr0, dr1, ginc, msg, sums, datt):
    t, d = mid.shape
    blk = t // nb
    pg = msg.shape[1] // 128

    def emit(rows, v):
        dmid[rows, :] = v
        dml[rows, :] = v.astype(BF)

    norm_backward(da2, mid, gain, co, emit, sums)
    ew = wot.shape[2]
    for g in range(wot.shape[0]):
        datt[:, g * ew : (g + 1) * ew] = dot(dml[...], wot[g])

    def pair(p):
        for n in range(nb):
            attend_gradient(p, n, blk, datt, att, rden, dr0, dr1)
        chunk_gradients(p, blk, nb, fq, dr0, dr1, ginc)
        cur = cflag[nb - 1] * ginc[nb - 1, p]
        for n in range(nb - 2, -1, -1):
            cur = cflag[n] * (cur + ginc[n, p])
        msg[p // pg, pl.ds(pl.multiple_of(lax.rem(p, pg) * 128, 128), 128), :] = cur.astype(BF)

    loop_pairs(d // 128, pair)


def back_kernel(nb, cflag, gin, ginc, states, fq, fk, vb, dr0, dr1, dq, dk, dv):
    t, d = fq.shape
    blk = t // nb
    pg = gin.shape[1] // 128

    def pair(p):
        cur = gin[p // pg, pl.ds(pl.multiple_of(lax.rem(p, pg) * 128, 128), 128), :].astype(F32)
        for n in range(nb - 1, -1, -1):
            attend_backward(p, n, blk, fq, fk, vb, dr0, dr1, states[n, p], cur.astype(BF), dq, dk, dv)
            cur = cflag[n] * (cur + ginc[n, p])

    loop_pairs(d // 128, pair)


def last_kernel(ns, x, gain, bias, dmid, dml, att, dq, dk, dv, wg, gt, g4, sums, a1, a1t, dmt, da1):
    nz, _, d, ew = wg.shape
    norm_forward(x, gain, bias, a1)
    transpose_perm(ns, a1, a1t)
    transpose_perm(ns, dml, dmt)
    for g in range(nz):
        c = slice(g * ew, (g + 1) * ew)
        for k, r in enumerate((dq, dk, dv)):
            g4[g, k] = dot(a1t[...], r[:, c]).astype(BF)
            if g == 0 and k == 0:
                da1[...] = dot_t(r[:, c], wg[g, k])
            else:
                da1[...] += dot_t(r[:, c], wg[g, k])
        g4[g, 3] = dot(dmt[...], att[:, c]).astype(BF)

    def emit(rows, v):
        gt[rows, :] = v.astype(BF)

    norm_backward(da1, x, gain, dmid, emit, sums)


def on_core(name, kernel, outs, scratch, *args, hbm=(), smem=(), hbm_out=()):
    ins = [any_spec() if i in hbm else smem_spec() if i in smem else vmem_spec() for i in range(len(args))]
    return pl.pallas_call(
        kernel,
        out_shape=tuple(jax.ShapeDtypeStruct(s, dt) for s, dt in outs),
        in_specs=ins,
        out_specs=tuple(any_spec() if i in hbm_out else vmem_spec() for i in range(len(outs))),
        scratch_shapes=scratch,
        name=name,
        compiler_params=pltpu.CompilerParams(vmem_limit_bytes=58 * 2**20),
    )(*args)


def group_order(nz):
    out = []
    for h in range(nz):
        seq = [h]
        for k in range(nz - 1):
            for o in (h - 1 - k, h + 1 + k):
                if 0 <= o < nz:
                    seq.append(o)
        out.append(seq)
    return out


def pick_group(order, h, i):
    out = 0
    for hh, seq in enumerate(order):
        for ii, g in enumerate(seq):
            if isinstance(i, int):
                if ii == i:
                    out = out + jnp.where(h == hh, g, 0)
            else:
                out = out + jnp.where((h == hh) & (i == ii), g, 0)
    return out


class Places:
    def __init__(self, ns, nz):
        self.ns, self.nz = ns, nz
        self.s, self.h = lax.axis_index("seq"), lax.axis_index("head")
        self.o0, self.o1 = bit_orders(ns)
        self.m = ns.bit_length() - 1
        self.zdev = z_others(self.s, self.h, nz)
        self.zfrom = [(self.s, lax.rem(self.h + nz - 1 - d, nz)) for d in range(nz - 1)]
        self.sdev = [(jnp.bitwise_xor(self.s, d), self.h) for d in range(1, ns)]
        self.bit = [(jnp.bitwise_xor(self.s, 1 << b), self.h) for b in range(self.m)]
        self.left, self.right = (self.s, self.h - 1), (self.s, self.h + 1)


class Gather:
    def __init__(self, pl_, buf, zs, zr, ps, pr, base):
        self.p, self.buf, self.base = pl_, buf, base
        self.sems = (zs, zr, ps, pr)
        self.orders = (pl_.o0 + [0], pl_.o1 + [0])
        self.half = buf.shape[2] // 2
        self.r = self.half // pl_.ns
        pos = [bits_to(pl_.s, o) for o in self.orders]
        self.zrow = [f * self.half + pos[f] * self.r for f in range(2)]
        self.mine = [
            [f * self.half + ((pos[f] >> j) << j) * self.r for j in range(pl_.m)] for f in range(2)
        ]
        self.theirs = [
            [f * self.half + jnp.bitwise_xor((pos[f] >> j) << j, 1 << j) * self.r for j in range(pl_.m)]
            for f in range(2)
        ]
        h, nz = pl_.h, pl_.nz
        self.origin = [(h - 1 - k, h + 1 + k) for k in range(nz - 1)]
        self.valid = [(h - 1 - k >= 0, h + 1 + k < nz) for k in range(nz - 1)]
        self.more = [((h - 1 - k >= 0) & (h + 1 < nz), (h + 1 + k < nz) & (h >= 1)) for k in range(nz - 1)]

    def rows(self, start, n):
        return pl.ds(pl.multiple_of(start, 16), n)

    def zcopy(self, f, k, d, origin):
        ref = self.buf.at[origin, :, self.rows(self.zrow[f], self.r), :]
        i = ((self.base * 2 + f) * (self.p.nz - 1) + k) * 2 + d
        return rcopy(ref, ref, self.sems[0].at[i], self.sems[1].at[i], self.p.right if d == 0 else self.p.left)

    def pcopy(self, f, k, d, j, starts):
        n = self.r << j
        ref = self.buf.at[self.origin[k][d], :, self.rows(starts[f][j], n), :]
        i = (((self.base * 2 + f) * (self.p.nz - 1) + k) * 2 + d) * self.p.m + j
        return rcopy(ref, ref, self.sems[2].at[i], self.sems[3].at[i], self.p.bit[self.orders[f][j]])

    def begin(self):
        for d, cond in enumerate((self.p.h + 1 < self.p.nz, self.p.h >= 1)):

            @pl.when(cond)
            def _(d=d):
                for f in range(2):
                    self.zcopy(f, 0, d, self.p.h).start()

    def advance(self, k, st):
        for d in range(2):

            @pl.when(self.valid[k][d])
            def _(d=d):
                for f in range(2):
                    if st == 0:
                        self.zcopy(f, k, d, self.origin[k][d]).wait_recv()
                    else:
                        self.pcopy(f, k, d, st - 1, self.theirs).wait_recv()
                if st == 0 and k + 1 < self.p.nz - 1:

                    @pl.when(self.more[k][d])
                    def _():
                        for f in range(2):
                            self.zcopy(f, k + 1, d, self.origin[k][d]).start()

                if st < self.p.m:
                    for f in range(2):
                        self.pcopy(f, k, d, st, self.mine).start()

    def drain(self):
        for d, cond in enumerate((self.p.h + 1 < self.p.nz, self.p.h >= 1)):

            @pl.when(cond)
            def _(d=d):
                for f in range(2):
                    self.zcopy(f, 0, d, self.p.h).wait_send()

        for k in range(self.p.nz - 1):
            for d in range(2):

                @pl.when(self.valid[k][d])
                def _(d=d, k=k):
                    for f in range(2):
                        for j in range(self.p.m):
                            self.pcopy(f, k, d, j, self.mine).wait_send()
                    if k + 1 < self.p.nz - 1:

                        @pl.when(self.more[k][d])
                        def _():
                            for f in range(2):
                                self.zcopy(f, k + 1, d, self.origin[k][d]).wait_send()


class RowsIn:
    def __init__(self, pl_, src, dst, ssem, rsem, lsem, base):
        self.p, self.src, self.dst, self.sems, self.base = pl_, src, dst, (ssem, rsem, lsem), base
        self.t, self.ew = dst.shape[0], src.shape[1]

    def copy(self, d, dev, col):
        i = self.base * (self.p.nz - 1) + d
        return rcopy(
            self.src.at[pl.ds(pl.multiple_of(dev[1] * self.t, 16), self.t), :],
            self.dst.at[:, pl.ds(pl.multiple_of(col * self.ew, 128), self.ew)],
            self.sems[0].at[i],
            self.sems[1].at[i],
            dev,
        )

    def own(self):
        h = self.p.h
        return pltpu.make_async_copy(
            self.src.at[pl.ds(pl.multiple_of(h * self.t, 16), self.t), :],
            self.dst.at[:, pl.ds(pl.multiple_of(h * self.ew, 128), self.ew)],
            self.sems[2].at[self.base],
        )

    def begin(self):
        for d, dev in enumerate(self.p.zdev):
            self.copy(d, dev, self.p.h).start()
        self.own().start()

    def finish(self):
        for d, frm in enumerate(self.p.zfrom):
            self.copy(d, frm, frm[1]).wait_recv()
        self.own().wait()

    def drain(self):
        for d, dev in enumerate(self.p.zdev):
            self.copy(d, dev, self.p.h).wait_send()


class Scan:
    def __init__(self, pl_, wt, wp, wl, msg, r1, r2, tot, outb, got, sems):
        self.p, self.w, self.msg, self.r1, self.r2 = pl_, (wt, wp, wl), msg, r1, r2
        self.tot, self.outb, self.got, self.sems = tot, outb, got, sems

    def c1(self, d, dev, slot):
        return rcopy(self.msg.at[dev[1]], self.r1.at[slot], self.sems[0].at[d], self.sems[1].at[d], dev)

    def c2(self, d, dev, slot):
        return rcopy(self.tot, self.r2.at[slot], self.sems[2].at[d], self.sems[3].at[d], dev)

    def c3(self, d, dev, slot):
        return rcopy(self.outb.at[dev[1]], self.got.at[slot], self.sems[4].at[d], self.sems[5].at[d], dev)

    def phase1(self):
        for d, dev in enumerate(self.p.zdev):
            self.c1(d, dev, self.p.h).start()
        self.r1[self.p.h] = self.msg[self.p.h]

    def phase2(self):
        for d, frm in enumerate(self.p.zfrom):
            self.c1(d, frm, frm[1]).wait_recv()
        wt = self.w[0]
        self.tot[...] = sum(wt[z] * self.r1[z].astype(F32) for z in range(self.p.nz)).astype(BF)
        for d, dev in enumerate(self.p.sdev):
            self.c2(d, dev, self.p.s).start()
        self.r2[self.p.s] = self.tot[...]

    def phase3(self):
        for d, dev in enumerate(self.p.sdev):
            self.c2(d, dev, dev[0]).wait_recv()
        _, wp, wl = self.w
        for z in range(self.p.nz):
            v = sum(wl[z, k] * self.r1[k].astype(F32) for k in range(self.p.nz))
            v = v + sum(wp[z, k] * self.r2[k].astype(F32) for k in range(self.p.ns))
            self.outb[z] = v.astype(BF)
        for d, dev in enumerate(self.p.zdev):
            self.c3(d, dev, self.p.h).start()
        self.got[self.p.h] = self.outb[self.p.h]

    def finish(self):
        for d, frm in enumerate(self.p.zfrom):
            self.c3(d, frm, frm[1]).wait_recv()

    def drain(self):
        for d, dev in enumerate(self.p.zdev):
            self.c1(d, dev, self.p.h).wait_send()
            self.c3(d, dev, self.p.h).wait_send()
        for d, dev in enumerate(self.p.sdev):
            self.c2(d, dev, self.p.s).wait_send()


def state_part(p, n, blk, fq, vals, st):
    rows = pl.ds(n * blk, blk)
    r = dot(fq[rows, cols(p, 128)], split_state(st))
    low = lane_low((blk, 128))
    num = jnp.where(low, r[:, :128], r[:, 128:])
    den = pltpu.roll(jnp.where(low, r[:, 128:], r[:, :128]), HD, 1)
    return num, den


def fore_kernel(ns, nz, nb, *refs):
    cflag, wt, wp, wl = refs[:4]
    tok, cot, wq, wo, wu, wd, gains, biases, pad = refs[4:13]
    xo, coo, fqo, fko, vbo, atto, rdeno, stateso, mido, w4o, lo, da2o, gu, gd = refs[13:27]
    (xv, cov, av, fq, fk, vb, att, a2t, ct, rden, mid, acc, da2, inc, states,
     w4v, wuv, wdv, gub, gdb, msg, r1, r2, tot, outb, got,
     lsem, tsend, trecv, zsend, zrecv, psend, precv, wsem, ysem, osem,
     c1s, c1r, c2s, c2r, c3s, c3r) = refs[27:]
    P_ = Places(ns, nz)
    t, d = xv.shape
    blk = t // nb
    ew = wq.shape[2]
    ff = wu.shape[2]
    h = P_.h
    m = P_.m
    np_ = d // 128
    pg = msg.shape[1] // 128
    order = group_order(nz)
    gidx = [pick_group(order, h, i) for i in range(nz)]
    W = Gather(P_, w4v, zsend, zrecv, psend, precv, 0)
    U = Gather(P_, wuv, zsend, zrecv, psend, precv, 1)
    V = Gather(P_, wdv, zsend, zrecv, psend, precv, 2)
    X = RowsIn(P_, tok, xv, tsend, trecv, lsem, 0)
    C = RowsIn(P_, cot, cov, tsend, trecv, lsem, 1)
    scan = Scan(P_, wt, wp, wl, msg, r1, r2, tot, outb, got, (c1s, c1r, c2s, c2r, c3s, c3r))
    own = [
        pltpu.make_async_copy(wq, w4v.at[h, 0:3], wsem.at[0]),
        pltpu.make_async_copy(wo, w4v.at[h, 3:4], wsem.at[1]),
        pltpu.make_async_copy(wu, wuv.at[h], wsem.at[2]),
        pltpu.make_async_copy(wd, wdv.at[h], wsem.at[3]),
    ]
    for cp in own:
        cp.start()
    enter(P_.zdev + P_.sdev)
    X.begin()
    own[0].wait()
    own[1].wait()
    W.begin()
    outs = []

    def keep(src, dst):
        cp = pltpu.make_async_copy(src, dst, ysem.at[len(outs)])
        outs.append(cp)
        cp.start()

    parts = [(a, k) for k in range(nz - 1) for a in (U, V)]
    waves = []
    for w in range(len(parts) - 1 + 2 * m + 1):
        waves.append([(a, k, (w - i) // 2) for i, (a, k) in enumerate(parts) if 0 <= w - i <= 2 * m and (w - i) % 2 == 0])
    done_at = [len(parts[: 2 * k + 2]) - 1 + 2 * m for k in range(nz - 1)]
    state = {"w": 0}

    def tick(upto=None):
        upto = state["w"] if upto is None else upto
        while state["w"] <= upto and state["w"] < len(waves):
            for a, k, st in waves[state["w"]]:
                a.advance(k, st)
            state["w"] += 1

    W.advance(0, 0)
    X.finish()
    own[2].wait()
    own[3].wait()
    U.begin()
    V.begin()
    norm_forward(xv, gains.at[0:1], biases.at[0:1], av)
    keep(xv, xo)
    project(av, w4v, gidx[0], pad, fq, fk, vb)
    for w in range(1, nz - 1 + m):
        for k in range(nz - 1):
            if 0 <= w - k <= m:
                W.advance(k, w - k)
                if w - k == m:
                    project(av, w4v, gidx[k + 1], pad, fq, fk, vb)
        if w == nz - 2:
            C.begin()
    keep(w4v, w4o)
    keep(fq, fqo)
    keep(fk, fko)
    keep(vb, vbo)
    tick()

    def sums_of(p):
        chunk_sums(p, blk, nb, fk, vb, inc)
        cur = inc[0, p]
        for n in range(1, nb):
            cur = cflag[n] * cur + inc[n, p]
        msg[p // pg, pl.ds(pl.multiple_of(lax.rem(p, pg) * 128, 128), 128), :] = cur.astype(BF)

    loop_pairs(np_, sums_of)
    scan.phase1()
    tick()

    def local_of(p):
        for n in range(nb):
            rows = pl.ds(n * blk, blk)
            c = cols(p, 128)
            q2, k2, v2 = fq[rows, c], fk[rows, c], vb[rows, c]
            s0, s1 = masked_scores(q2, k2, causal_mask(blk))
            g0, g1 = with_ones(v2)
            x0, x1 = dot(s0, g0), dot(s1, g1)
            low = lane_low(x0.shape)
            acc[rows, c] = jnp.where(low, x0, x1)
            rden[rows, c] = pltpu.roll(jnp.where(low, x1, x0), HD, 1)

    hp = np_ // 2
    loop_pairs(hp, local_of)
    scan.phase2()
    tick()
    loop_pairs(np_ - hp, lambda p: local_of(p + hp))
    scan.phase3()
    tick()
    scan.finish()

    def state_of(p):
        cur = got[p // pg, pl.ds(pl.multiple_of(lax.rem(p, pg) * 128, 128), 128), :].astype(F32)
        for n in range(nb):
            rows = pl.ds(n * blk, blk)
            c = cols(p, 128)
            used = cflag[n] * cur
            st = used.astype(BF)
            states[n, p] = st
            cur = used + inc[n, p]
            num, den = state_part(p, n, blk, fq, None, st)
            rd = 1.0 / (1.0 + rden[rows, c] + den)
            att[rows, c] = ((acc[rows, c] + num) * rd).astype(BF)
            rden[rows, c] = rd

    loop_pairs(np_, state_of)
    keep(att, atto)
    keep(rden, rdeno)
    keep(states, stateso)
    tick()
    mid[...] = xv[...].astype(F32)
    for g in range(nz):
        mid[...] += dot_t(att[:, g * ew : (g + 1) * ew], w4v[g, 3])
        if g % 2 == 1:
            tick()
    norm_forward(mid, gains.at[1:2], biases.at[1:2], av)
    keep(mid, mido)
    C.finish()
    keep(cov, coo)
    transpose_perm(ns, av, a2t)
    transpose_perm(ns, cov, ct)
    acc[...] = mid[...]
    da2[...] = jnp.zeros_like(da2)
    tile = gub.shape[2]
    per = ff // tile
    steps = nz * per

    def place(i):
        g = pick_group(order, h, i // per)
        return g, pl.ds(pl.multiple_of(lax.rem(i, per) * tile, 128), tile)

    def flush(i, slot):
        g, c = place(i)
        return (
            pltpu.make_async_copy(gub.at[slot], gu.at[g, :, c], osem.at[slot, 0]),
            pltpu.make_async_copy(gdb.at[slot], gd.at[g, :, c], osem.at[slot, 1]),
        )

    def step(i, _):
        slot = lax.rem(i, 2)
        for k in range(nz - 1):

            @pl.when(i == (k + 1) * per)
            def _(k=k):
                tick(done_at[k])

        @pl.when(i >= 2)
        def _():
            for cp in flush(i - 2, slot):
                cp.wait()

        g, c = place(i)
        wub, wdb = wuv[g, 0, :, c], wdv[g, 0, c, :]
        up = dot(av[...], wub)
        hidf, slope = gelu_parts(up)
        hid = hidf.astype(BF)
        acc[...] += dot(hid, wdb)
        gdb[slot] = dot(ct[...], hid).astype(BF)
        dup = (slope * dot_t(cov[...], wdb)).astype(BF)
        da2[...] += dot_t(dup, wub)
        gub[slot] = dot(a2t[...], dup).astype(BF)
        for cp in flush(i, slot):
            cp.start()
        return 0

    lax.fori_loop(0, steps, step, 0)
    tick(len(waves))
    keep(da2, da2o)
    av[...] = acc[...].astype(BF)
    keep(av, lo)
    for i in range(max(0, steps - 2), steps):
        for cp in flush(i, i % 2):
            cp.wait()
    for cp in outs:
        cp.wait()
    X.drain()
    C.drain()
    scan.drain()
    for a in (W, U, V):
        a.drain()


def fore(ns, nz, nb, tables, tok, cot, wq, wo, wu, wd, gains, biases, pad):
    t, d = tok.shape[0] // nz, wq.shape[1]
    ew, ff = wq.shape[2], wu.shape[2]
    np_ = d // 128
    m = ns.bit_length() - 1
    dma = pltpu.SemaphoreType.DMA
    vm = pltpu.VMEM
    tile = 512 if ff % 512 == 0 else ff
    one = ((ew // 128) * 128, 128)
    nzs = 3 * 2 * (nz - 1) * 2
    td, tdf = ((t, d), BF), ((t, d), F32)
    outs = [td, td, td, td, td, td, tdf, ((nb, np_, 128, 128), BF), tdf, ((nz, 4, d, ew), BF), td, tdf,
            ((nz, d, ff), BF), ((nz, d, ff), BF)]
    args = tables + (tok, cot, wq, wo, wu, wd, gains, biases, pad)
    return pl.pallas_call(
        functools.partial(fore_kernel, ns, nz, nb),
        out_shape=tuple(jax.ShapeDtypeStruct(s, dt) for s, dt in outs),
        in_specs=[smem_spec()] * 4 + [any_spec()] * 6 + [vmem_spec()] * 3,
        out_specs=(any_spec(),) * len(outs),
        scratch_shapes=[vm((t, d), BF)] * 7
        + [vm((d, t), BF)] * 2
        + [vm((t, d), F32)] * 4
        + [
            vm((nb, np_, 128, 128), F32),
            vm((nb, np_, 128, 128), BF),
            vm((nz, 4, d, ew), BF),
            vm((nz, 1, d, ff), BF),
            vm((nz, 1, ff, d), BF),
            vm((2, d, tile), BF),
            vm((2, d, tile), BF),
            vm((nz,) + one, BF),
            vm((nz,) + one, BF),
            vm((ns,) + one, BF),
            vm(one, BF),
            vm((nz,) + one, BF),
            vm((nz,) + one, BF),
            dma((2,)),
            dma((2 * (nz - 1),)),
            dma((2 * (nz - 1),)),
            dma((nzs,)),
            dma((nzs,)),
            dma((nzs * m,)),
            dma((nzs * m,)),
            dma((4,)),
            dma((16,)),
            dma((2, 2)),
        ]
        + [dma((nz - 1,)), dma((nz - 1,)), dma((ns - 1,)), dma((ns - 1,)), dma((nz - 1,)), dma((nz - 1,))],
        name="fore",
        compiler_params=pltpu.CompilerParams(collective_id=0, has_side_effects=True, vmem_limit_bytes=62 * 2**20),
    )(*args)


def shards(ns, nz, tokens, lengths, pad_mask, w_qkv, w_out, w_up, w_down, norm_gains, norm_biases, out_cotangent):
    rows = tokens.shape[0]
    t = rows // nz
    d = w_qkv.shape[1]
    ff = w_up.shape[1]
    ew = d // nz
    np_ = d // 128
    blk = math.gcd(t, UNIT)
    nb = t // blk
    s, h = lax.axis_index("seq"), lax.axis_index("head")

    ends = jnp.cumsum(lengths)

    def item_at(p):
        return jnp.sum((p[..., None] >= ends).astype(jnp.int32), axis=-1)

    ndev = ns * nz
    last = item_at((jnp.arange(ndev, dtype=jnp.int32) + 1) * t - 1)
    before = jnp.concatenate([jnp.full((1,), -1, jnp.int32), last[:-1]])
    me = s * nz + h
    chunk = item_at(me * t + jnp.arange(nb, dtype=jnp.int32) * blk)
    prior = lax.dynamic_slice_in_dim(before, me, 1)
    cflag = (chunk == jnp.concatenate([prior, chunk[:-1]])).astype(F32)
    last2, before2 = last.reshape(ns, nz), before.reshape(ns, nz)
    my_last, my_before = last2[s], before2[s]
    sidx, zidx = jnp.arange(ns), jnp.arange(nz)
    fwt = (my_last == my_last[-1]).astype(F32)
    fwp = ((sidx[None, :] < s) & (last2[None, :, -1] == my_before[:, None])).astype(F32)
    fwl = ((zidx[None, :] < zidx[:, None]) & (my_last[None, :] == my_before[:, None])).astype(F32)
    bwt = (my_before == my_before[0]).astype(F32)
    bwp = ((sidx[None, :] > s) & (before2[None, :, 0] == my_last[:, None])).astype(F32)
    bwl = ((zidx[None, :] > zidx[:, None]) & (my_before[None, :] == my_last[:, None])).astype(F32)

    pad = lax.dynamic_slice_in_dim(pad_mask, h * t, t).astype(F32)[:, None]
    gains = [norm_gains[i : i + 1] for i in range(2)]
    biases = [norm_biases[i : i + 1] for i in range(2)]
    td, tdf = ((t, d), BF), ((t, d), F32)
    msgs = ((nz, (ew // 128) * 128, 128), BF)
    incs = ((nb, np_, 128, 128), F32)
    sums = ((2, 8, d), F32)
    vm = pltpu.VMEM
    x, co, fq, fk, vb, att, rden, states, mid, w4g, lo, da2, gu, gd = fore(
        ns, nz, nb, (cflag, fwt, fwp, fwl), tokens, out_cotangent, w_qkv, w_out.T[None], w_up[None], w_down[None],
        norm_gains, norm_biases, pad,
    )
    wot = w4g[:, 3]
    dmid, dml, dr0, dr1, ginc, gmsg, sums2 = on_core(
        "turn",
        functools.partial(turn_kernel, nb),
        (tdf, td, td, td, incs, msgs, sums),
        [vm((t, d), F32)],
        cflag, da2, mid, co, gains[1], wot, fq, att, rden,
        smem=(0,),
    )
    gin = scan_states(ns, nz, 2, bwt, bwp, bwl, gmsg)
    dq, dk, dv = on_core(
        "back",
        functools.partial(back_kernel, nb),
        (td, td, td),
        [],
        cflag, gin, ginc, states, fq, fk, vb, dr0, dr1,
        smem=(0,),
    )
    gt, g4, sums1 = on_core(
        "last",
        functools.partial(last_kernel, ns),
        (td, ((nz, 4, d, ew), BF), sums),
        [vm((t, d), BF), vm((d, t), BF), vm((d, t), BF), vm((t, d), F32)],
        x, gains[0], biases[0], dmid, dml, att, dq, dk, dv, w4g,
    )
    s1, s2 = jnp.sum(sums1, axis=1), jnp.sum(sums2, axis=1)
    gb = jnp.concatenate([jnp.stack([s1[0], s2[0], s1[1], s2[1]]), jnp.zeros((4, d), F32)])
    lo_o, gt_o, gbo, o4, ou, od = reduce_all(
        ns, nz, lo, gt, gb,
        g4.reshape(nz, 4, 2, d // 2, ew),
        gu.reshape(nz, 1, 2, d // 2, ff),
        gd.reshape(nz, 1, 2, d // 2, ff),
    )
    piece = d // ns
    o4 = o4.reshape(4, piece, ew).astype(F32)
    w = d // ndev
    gbs = lax.dynamic_slice_in_dim(gbo, (h * ns + s) * w, w, 1)
    return (
        lo_o,
        gt_o.astype(F32),
        o4[:3],
        o4[3].T,
        ou.reshape(piece, ff).astype(F32),
        od.reshape(piece, ff).astype(F32).T,
        gbs[:2],
        gbs[2:4],
    )


def solution(mesh):
    in_specs = (
        P("seq", "head"),
        P(),
        P("seq"),
        P(None, None, "head"),
        P("head", None),
        P(None, "head"),
        P("head", None),
        P(),
        P(),
        P("seq", "head"),
    )
    out_specs = (
        P("seq", "head"),
        P("seq", "head"),
        P(None, "seq", "head"),
        P("head", "seq"),
        P("seq", "head"),
        P("head", "seq"),
        P(None, ("head", "seq")),
        P(None, ("head", "seq")),
    )
    f = functools.partial(shards, mesh.shape["seq"], mesh.shape["head"])
    return jax.shard_map(f, mesh=mesh, in_specs=in_specs, out_specs=out_specs, check_vma=False)
```

```python
import functools
import math

import jax
import jax.numpy as jnp
from jax import lax
from jax.experimental import pallas as pl
from jax.experimental.pallas import tpu as pltpu
from jax.sharding import PartitionSpec as P

HD = 64
UNIT = 768
EPS = 1e-05
MESH = pl.DeviceIdType.MESH
BF = jnp.bfloat16
F32 = jnp.float32


def bit_orders(ns):
    m = ns.bit_length() - 1
    xs = list(range(1, 1 + (m - 1) // 2))
    ys = list(range(1 + (m - 1) // 2, m))
    return xs + ys, ys + xs


def bits_to(s, order):
    out = 0
    for j, b in enumerate(order):
        out = out + (((s >> b) & 1) << j)
    return out


def rcopy(src, dst, send, recv, dev):
    return pltpu.make_async_remote_copy(
        src_ref=src, dst_ref=dst, send_sem=send, recv_sem=recv, device_id=dev, device_id_type=MESH
    )


def enter(devs):
    bar = pltpu.get_barrier_semaphore()
    for d in devs:
        pl.semaphore_signal(bar, inc=1, device_id=d, device_id_type=MESH)
    pl.semaphore_wait(bar, len(devs))


def z_others(s, h, nz):
    return [(s, lax.rem(h + d, nz)) for d in range(1, nz)]


def any_spec():
    return pl.BlockSpec(memory_space=pl.ANY)


def vmem_spec():
    return pl.BlockSpec(memory_space=pltpu.VMEM)


def smem_spec():
    return pl.BlockSpec(memory_space=pltpu.SMEM)


def dot(a, b):
    return lax.dot_general(a, b, (((1,), (0,)), ((), ())), preferred_element_type=F32)


def dot_t(a, b):
    return lax.dot_general(a, b, (((1,), (1,)), ((), ())), preferred_element_type=F32)


def t_dot(a, b):
    return lax.dot_general(a, b, (((0,), (0,)), ((), ())), preferred_element_type=F32)


def lane_low(shape):
    return lax.broadcasted_iota(jnp.int32, shape, 1) < HD


def row_low(shape):
    return lax.broadcasted_iota(jnp.int32, shape, 0) < HD


def row_block(t):
    return 96 if t % 96 == 0 else 32


def over_rows(t, body):
    rb = row_block(t)

    def step(i, _):
        body(pl.ds(pl.multiple_of(i * rb, 32), rb))
        return 0

    lax.fori_loop(0, t // rb, step, 0)


def normed(v):
    mean = jnp.mean(v, axis=1, keepdims=True)
    c = v - mean
    w = lax.rsqrt(jnp.mean(c * c, axis=1, keepdims=True) + EPS)
    return c * w, w


def norm_forward(src, gain, bias, dst):
    def body(rows):
        xh, _ = normed(src[rows, :].astype(F32))
        dst[rows, :] = (xh * gain[...] + bias[...]).astype(BF)

    over_rows(src.shape[0], body)


def norm_backward(e_ref, src, gain, add, emit, sums):
    sums[0] = jnp.zeros(sums.shape[1:], F32)
    sums[1] = jnp.zeros(sums.shape[1:], F32)

    def body(rows):
        e = e_ref[rows, :]
        xh, w = normed(src[rows, :].astype(F32))
        eg = e * gain[...]
        m1 = jnp.mean(eg, axis=1, keepdims=True)
        m2 = jnp.mean(eg * xh, axis=1, keepdims=True)
        emit(rows, add[rows, :].astype(F32) + w * (eg - m1 - xh * m2))
        n = e.shape[0]
        sums[0] += jnp.sum((e * xh).reshape(n // 8, 8, -1), axis=0)
        sums[1] += jnp.sum(e.reshape(n // 8, 8, -1), axis=0)

    over_rows(src.shape[0], body)


def transpose_perm(ns, src, dst):
    d = dst.shape[0]
    u = d // (2 * ns)
    o0, o1 = bit_orders(ns)
    m = ns.bit_length() - 1
    orders = ([0] + o0, [0] + o1)
    for j in range(d // 128):
        tr = src[:, j * 128 : (j + 1) * 128].T
        for i in range(128 // u):
            g = j * (128 // u) + i
            dev, f = g // 2, g % 2
            q = sum(((dev >> b) & 1) << (m - 1 - k) for k, b in enumerate(orders[f]))
            row = f * (d // 2) + q * u
            dst[row : row + u, :] = tr[i * u : (i + 1) * u, :]


def phi(y):
    return jnp.where(y > 0, y + 1.0, jnp.exp(jnp.minimum(y, 0.0)))


def cols(i, n):
    return pl.ds(pl.multiple_of(i * n, 128), n)


def project(a1, wg, g, pad, fq, fk, vb):
    ew = wg.shape[3]
    c = cols(g, ew)
    fq[:, c] = phi(dot(a1[...], wg[g, 0])).astype(BF)
    fk[:, c] = (pad[...] * phi(dot(a1[...], wg[g, 1]))).astype(BF)
    vb[:, c] = dot(a1[...], wg[g, 2]).astype(BF)


def with_ones(v2):
    one = jnp.ones_like(v2)
    low = lane_low(v2.shape)
    return jnp.where(low, v2, one), jnp.where(low, one, v2)


def chunk_sums(p, blk, nb, fk, vb, inc):
    for n in range(nb):
        rows = pl.ds(n * blk, blk)
        k2, v2 = fk[rows, cols(p, 128)], vb[rows, cols(p, 128)]
        r = t_dot(k2, jnp.concatenate(with_ones(v2), axis=1))
        inc[n, p] = jnp.where(row_low((128, 128)), r[:, :128], r[:, 128:])


def causal_mask(blk):
    return lax.broadcasted_iota(jnp.int32, (blk, blk), 0) >= lax.broadcasted_iota(jnp.int32, (blk, blk), 1)


def masked_scores(a2, b2, keep):
    low = lane_low(b2.shape)
    zero = jnp.zeros_like(b2)
    return [
        jnp.where(keep, dot_t(a2, b), 0.0).astype(BF)
        for b in (jnp.where(low, b2, zero), jnp.where(low, zero, b2))
    ]


def split_state(st):
    low = row_low(st.shape)
    zero = jnp.zeros_like(st)
    return jnp.concatenate([jnp.where(low, st, zero), jnp.where(low, zero, st)], axis=1)


def attend_gradient(p, n, blk, datt, att, rden, dr0, dr1):
    rows = pl.ds(n * blk, blk)
    c = cols(p, 128)
    e = datt[rows, c]
    rd = rden[rows, c]
    low = lane_low(e.shape)
    lane = lax.broadcasted_iota(jnp.int32, e.shape, 1)
    dn = e * rd
    w = dn * att[rows, c].astype(F32)
    d0 = -jnp.sum(jnp.where(low, w, 0.0), axis=1, keepdims=True)
    d1 = -jnp.sum(jnp.where(low, 0.0, w), axis=1, keepdims=True)

    def parts(dd, first):
        hi = dd.astype(BF).astype(F32)
        return jnp.where(lane == first, hi, jnp.where(lane == first + 1, dd - hi, 0.0))

    dr0[rows, c] = jnp.where(low, dn, parts(d0, HD)).astype(BF)
    dr1[rows, c] = jnp.where(low, parts(d1, 0), dn).astype(BF)


def chunk_gradients(p, blk, nb, fq, dr0, dr1, ginc):
    for n in range(nb):
        rows = pl.ds(n * blk, blk)
        c = cols(p, 128)
        r = t_dot(fq[rows, c], jnp.concatenate([dr0[rows, c], dr1[rows, c]], axis=1))
        ginc[n, p] = jnp.where(row_low((128, 128)), r[:, :128], r[:, 128:])


def gelu_parts(s):
    c0 = math.sqrt(2.0 / math.pi)
    s2 = s * s
    th = jnp.tanh(c0 * (s + 0.044715 * s * s2))
    h = 0.5 * (1.0 + th)
    slope = h + 0.5 * s * (1.0 - th * th) * (c0 * (1.0 + 3 * 0.044715 * s2))
    return s * h, slope


def loop_pairs(n, body):
    def step(p, _):
        body(p)
        return 0

    lax.fori_loop(0, n, step, 0)


def group_order(nz):
    out = []
    for h in range(nz):
        seq = [h]
        for k in range(nz - 1):
            for o in (h - 1 - k, h + 1 + k):
                if 0 <= o < nz:
                    seq.append(o)
        out.append(seq)
    return out


def pick_group(order, h, i):
    out = 0
    for hh, seq in enumerate(order):
        for ii, g in enumerate(seq):
            if isinstance(i, int):
                if ii == i:
                    out = out + jnp.where(h == hh, g, 0)
            else:
                out = out + jnp.where((h == hh) & (i == ii), g, 0)
    return out


class Places:
    def __init__(self, ns, nz):
        self.ns, self.nz = ns, nz
        self.s, self.h = lax.axis_index("seq"), lax.axis_index("head")
        self.o0, self.o1 = bit_orders(ns)
        self.m = ns.bit_length() - 1
        self.zdev = z_others(self.s, self.h, nz)
        self.zfrom = [(self.s, lax.rem(self.h + nz - 1 - d, nz)) for d in range(nz - 1)]
        self.sdev = [(jnp.bitwise_xor(self.s, d), self.h) for d in range(1, ns)]
        self.bit = [(jnp.bitwise_xor(self.s, 1 << b), self.h) for b in range(self.m)]
        self.left, self.right = (self.s, self.h - 1), (self.s, self.h + 1)


class Gather:
    def __init__(self, pl_, buf, zs, zr, ps, pr, base):
        self.p, self.buf, self.base = pl_, buf, base
        self.sems = (zs, zr, ps, pr)
        self.orders = (pl_.o0 + [0], pl_.o1 + [0])
        self.half = buf.shape[2] // 2
        self.r = self.half // pl_.ns
        pos = [bits_to(pl_.s, o) for o in self.orders]
        self.zrow = [f * self.half + pos[f] * self.r for f in range(2)]
        self.mine = [
            [f * self.half + ((pos[f] >> j) << j) * self.r for j in range(pl_.m)] for f in range(2)
        ]
        self.theirs = [
            [f * self.half + jnp.bitwise_xor((pos[f] >> j) << j, 1 << j) * self.r for j in range(pl_.m)]
            for f in range(2)
        ]
        h, nz = pl_.h, pl_.nz
        self.origin = [(h - 1 - k, h + 1 + k) for k in range(nz - 1)]
        self.valid = [(h - 1 - k >= 0, h + 1 + k < nz) for k in range(nz - 1)]
        self.more = [((h - 1 - k >= 0) & (h + 1 < nz), (h + 1 + k < nz) & (h >= 1)) for k in range(nz - 1)]

    def rows(self, start, n):
        return pl.ds(pl.multiple_of(start, 16), n)

    def zcopy(self, f, k, d, origin):
        ref = self.buf.at[origin, :, self.rows(self.zrow[f], self.r), :]
        i = ((self.base * 2 + f) * (self.p.nz - 1) + k) * 2 + d
        return rcopy(ref, ref, self.sems[0].at[i], self.sems[1].at[i], self.p.right if d == 0 else self.p.left)

    def pcopy(self, f, k, d, j, starts):
        n = self.r << j
        ref = self.buf.at[self.origin[k][d], :, self.rows(starts[f][j], n), :]
        i = (((self.base * 2 + f) * (self.p.nz - 1) + k) * 2 + d) * self.p.m + j
        return rcopy(ref, ref, self.sems[2].at[i], self.sems[3].at[i], self.p.bit[self.orders[f][j]])

    def begin(self):
        for d, cond in enumerate((self.p.h + 1 < self.p.nz, self.p.h >= 1)):

            @pl.when(cond)
            def _(d=d):
                for f in range(2):
                    self.zcopy(f, 0, d, self.p.h).start()

    def forward(self, k):
        if k + 1 < self.p.nz - 1:
            for d in range(2):

                @pl.when(self.more[k][d])
                def _(d=d):
                    for f in range(2):
                        self.zcopy(f, k + 1, d, self.origin[k][d]).start()

    def advance(self, k, st):
        for d in range(2):

            @pl.when(self.valid[k][d])
            def _(d=d):
                for f in range(2):
                    if st == 0:
                        self.zcopy(f, k, d, self.origin[k][d]).wait_recv()
                    else:
                        self.pcopy(f, k, d, st - 1, self.theirs).wait_recv()
                if st < self.p.m:
                    for f in range(2):
                        self.pcopy(f, k, d, st, self.mine).start()

    def drain(self):
        for d, cond in enumerate((self.p.h + 1 < self.p.nz, self.p.h >= 1)):

            @pl.when(cond)
            def _(d=d):
                for f in range(2):
                    self.zcopy(f, 0, d, self.p.h).wait_send()

        for k in range(self.p.nz - 1):
            for d in range(2):

                @pl.when(self.valid[k][d])
                def _(d=d, k=k):
                    for f in range(2):
                        for j in range(self.p.m):
                            self.pcopy(f, k, d, j, self.mine).wait_send()
                    if k + 1 < self.p.nz - 1:

                        @pl.when(self.more[k][d])
                        def _():
                            for f in range(2):
                                self.zcopy(f, k + 1, d, self.origin[k][d]).wait_send()


def parts_of(t):
    return t // 144 if t % 144 == 0 else 1


class RowsIn:
    def __init__(self, pl_, src, dst, ssem, rsem, lsem, base):
        self.p, self.src, self.dst, self.sems, self.base = pl_, src, dst, (ssem, rsem, lsem), base
        self.t, self.ew = dst.shape[0], src.shape[1]
        self.parts = parts_of(self.t)
        self.n = self.t // self.parts

    def copy(self, r, d, dev, col):
        i = (self.base * (self.p.nz - 1) + d) * self.parts + r
        return rcopy(
            self.src.at[pl.ds(pl.multiple_of(dev[1] * self.t + r * self.n, 16), self.n), :],
            self.dst.at[pl.ds(r * self.n, self.n), pl.ds(pl.multiple_of(col * self.ew, 128), self.ew)],
            self.sems[0].at[i],
            self.sems[1].at[i],
            dev,
        )

    def own(self):
        h = self.p.h
        return pltpu.make_async_copy(
            self.src.at[pl.ds(pl.multiple_of(h * self.t, 16), self.t), :],
            self.dst.at[:, pl.ds(pl.multiple_of(h * self.ew, 128), self.ew)],
            self.sems[2].at[self.base],
        )

    def begin(self, lo, hi):
        for r in range(lo, min(hi, self.parts)):
            if r == 0:
                self.own().start()
            for d, dev in enumerate(self.p.zdev):
                self.copy(r, d, dev, self.p.h).start()

    def finish(self):
        for r in range(self.parts):
            for d, frm in enumerate(self.p.zfrom):
                self.copy(r, d, frm, frm[1]).wait_recv()
        self.own().wait()

    def drain(self):
        for r in range(self.parts):
            for d, dev in enumerate(self.p.zdev):
                self.copy(r, d, dev, self.p.h).wait_send()


class Scan:
    def __init__(self, pl_, wt, wp, wl, msg, r1, r2, tot, outb, got, sems):
        self.p, self.w, self.msg, self.r1, self.r2 = pl_, (wt, wp, wl), msg, r1, r2
        self.tot, self.outb, self.got, self.sems = tot, outb, got, sems

    def c1(self, d, dev, slot):
        return rcopy(self.msg.at[dev[1]], self.r1.at[slot], self.sems[0].at[d], self.sems[1].at[d], dev)

    def c2(self, d, dev, slot):
        return rcopy(self.tot, self.r2.at[slot], self.sems[2].at[d], self.sems[3].at[d], dev)

    def c3(self, d, dev, slot):
        return rcopy(self.outb.at[dev[1]], self.got.at[slot], self.sems[4].at[d], self.sems[5].at[d], dev)

    def phase1(self):
        for d, dev in enumerate(self.p.zdev):
            self.c1(d, dev, self.p.h).start()
        self.r1[self.p.h] = self.msg[self.p.h]

    def phase2(self):
        for d, frm in enumerate(self.p.zfrom):
            self.c1(d, frm, frm[1]).wait_recv()
        wt = self.w[0]
        self.tot[...] = sum(wt[z] * self.r1[z].astype(F32) for z in range(self.p.nz)).astype(BF)
        for d, dev in enumerate(self.p.sdev):
            self.c2(d, dev, self.p.s).start()
        self.r2[self.p.s] = self.tot[...]

    def phase3(self):
        for d, dev in enumerate(self.p.sdev):
            self.c2(d, dev, dev[0]).wait_recv()
        _, wp, wl = self.w
        for z in range(self.p.nz):
            v = sum(wl[z, k] * self.r1[k].astype(F32) for k in range(self.p.nz))
            v = v + sum(wp[z, k] * self.r2[k].astype(F32) for k in range(self.p.ns))
            self.outb[z] = v.astype(BF)
        for d, dev in enumerate(self.p.zdev):
            self.c3(d, dev, self.p.h).start()
        self.got[self.p.h] = self.outb[self.p.h]

    def finish(self):
        for d, frm in enumerate(self.p.zfrom):
            self.c3(d, frm, frm[1]).wait_recv()

    def drain(self):
        for d, dev in enumerate(self.p.zdev):
            self.c1(d, dev, self.p.h).wait_send()
            self.c3(d, dev, self.p.h).wait_send()
        for d, dev in enumerate(self.p.sdev):
            self.c2(d, dev, self.p.s).wait_send()


ZROWS = 16
MSG = HD + ZROWS


def msg_rows(p, pg):
    return p // pg, pl.ds(pl.multiple_of(lax.rem(p, pg) * MSG, 16), MSG)


def is_own(shape=(128, 128)):
    return row_low(shape) == lane_low(shape)


def pack_state(sa, lanes):
    own = is_own()
    state = jnp.where(lane_low((HD, 128)), sa[:HD], sa[HD:])
    z = jnp.where(own, 0.0, sa)
    hi = z.astype(BF)
    lo = (z - hi.astype(F32)).astype(BF)
    lane = lax.broadcasted_iota(jnp.int32, (ZROWS, 128), 1)
    row = lax.broadcasted_iota(jnp.int32, (ZROWS, 128), 0)
    sel = jnp.where((lane % HD) < lanes, 1.0, 0.0).astype(BF)
    zr = jnp.where(row == 0, dot_t(sel, hi), jnp.where(row == 1, dot_t(sel, lo), 0.0))
    return jnp.concatenate([state, zr], axis=0).astype(BF)


def unpack_state(msg, every):
    st = msg[:HD].astype(F32)
    z = t_dot(msg[HD:], jnp.ones((ZROWS, 128), BF))
    if not every:
        lane = lax.broadcasted_iota(jnp.int32, (128, 128), 1)
        z = jnp.where(lane % HD == 0, z, 0.0)
    return jnp.where(is_own(), jnp.concatenate([st, st], axis=0), z)


def state_part(p, n, blk, fq, vals, st):
    rows = pl.ds(n * blk, blk)
    r = dot(fq[rows, cols(p, 128)], split_state(st))
    low = lane_low((blk, 128))
    num = jnp.where(low, r[:, :128], r[:, 128:])
    den = pltpu.roll(jnp.where(low, r[:, 128:], r[:, :128]), HD, 1)
    return num, den


def fore_kernel(ns, nz, nb, *refs):
    cflag, wt, wp, wl = refs[:4]
    tok, cot, wq, wo, wu, wd, gains, biases, pad = refs[4:13]
    xo, coo, fqo, fko, vbo, atto, rdeno, stateso, mido, w4o, lo, da2o, gu, gd = refs[13:27]
    (xv, cov, av, fq, fk, vb, att, a2t, ct, rden, mid, acc, da2, inc, states,
     w4v, wuv, wdv, gub, gdb, msg, r1, r2, tot, outb, got,
     lsem, tsend, trecv, zsend, zrecv, psend, precv, wsem, ysem, osem,
     c1s, c1r, c2s, c2r, c3s, c3r) = refs[27:]
    P_ = Places(ns, nz)
    t, d = xv.shape
    blk = t // nb
    ew = wq.shape[2]
    ff = wu.shape[2]
    h = P_.h
    m = P_.m
    np_ = d // 128
    pg = msg.shape[1] // MSG
    order = group_order(nz)
    gidx = [pick_group(order, h, i) for i in range(nz)]
    W = Gather(P_, w4v, zsend, zrecv, psend, precv, 0)
    U = Gather(P_, wuv, zsend, zrecv, psend, precv, 1)
    V = Gather(P_, wdv, zsend, zrecv, psend, precv, 2)
    X = RowsIn(P_, tok, xv, tsend, trecv, lsem, 0)
    C = RowsIn(P_, cot, cov, tsend, trecv, lsem, 1)
    scan = Scan(P_, wt, wp, wl, msg, r1, r2, tot, outb, got, (c1s, c1r, c2s, c2r, c3s, c3r))
    own = [
        pltpu.make_async_copy(wq, w4v.at[h, 0:3], wsem.at[0]),
        pltpu.make_async_copy(wo, w4v.at[h, 3:4], wsem.at[1]),
        pltpu.make_async_copy(wu, wuv.at[h], wsem.at[2]),
        pltpu.make_async_copy(wd, wdv.at[h], wsem.at[3]),
    ]
    for cp in own:
        cp.start()
    outs = []

    def keep(src, dst):
        cp = pltpu.make_async_copy(src, dst, ysem.at[len(outs)])
        outs.append(cp)
        cp.start()

    def both(k, st):
        U.advance(k, st)
        V.advance(k, st)

    far = nz - 1
    enter(P_.zdev + P_.sdev)
    own[0].wait()
    own[1].wait()
    W.begin()
    X.begin(0, 1)
    wsteps = sorted((2 * k + st, k, st) for k in range(far) for st in range(m + 1))
    early = [x for x in wsteps if x[0] <= 2 * (far - 1)]
    for _, k, st in early:
        W.advance(k, st)
        if st == 0:
            W.forward(k)
            if k + 1 < far:
                X.begin(k + 1, k + 2 if k + 2 < far else X.parts)
    own[2].wait()
    own[3].wait()
    U.begin()
    V.begin()
    X.finish()
    norm_forward(xv, gains.at[0:1], biases.at[0:1], av)
    keep(xv, xo)
    project(av, w4v, gidx[0], pad, fq, fk, vb)
    for _, k, st in early:
        if st == m:
            project(av, w4v, gidx[k + 1], pad, fq, fk, vb)
    for _, k, st in wsteps[len(early) :]:
        W.advance(k, st)
        if st == m:
            project(av, w4v, gidx[k + 1], pad, fq, fk, vb)
    keep(w4v, w4o)
    keep(fq, fqo)
    keep(fk, fko)
    keep(vb, vbo)

    def sums_of(p):
        chunk_sums(p, blk, nb, fk, vb, inc)
        cur = inc[0, p]
        for n in range(1, nb):
            cur = cflag[n] * cur + inc[n, p]
        g, rr = msg_rows(p, pg)
        msg[g, rr, :] = pack_state(cur, 1)

    loop_pairs(np_, sums_of)
    scan.phase1()
    C.begin(0, 1)
    both(0, 0)

    def local_of(p):
        for n in range(nb):
            rows = pl.ds(n * blk, blk)
            c = cols(p, 128)
            q2, k2, v2 = fq[rows, c], fk[rows, c], vb[rows, c]
            s0, s1 = masked_scores(q2, k2, causal_mask(blk))
            g0, g1 = with_ones(v2)
            x0, x1 = dot(s0, g0), dot(s1, g1)
            low = lane_low(x0.shape)
            acc[rows, c] = jnp.where(low, x0, x1)
            rden[rows, c] = pltpu.roll(jnp.where(low, x1, x0), HD, 1)

    hp = np_ // 2
    loop_pairs(hp, local_of)
    scan.phase2()
    both(0, 1)
    loop_pairs(np_ - hp, lambda p: local_of(p + hp))
    scan.phase3()
    C.begin(1, C.parts)
    U.forward(0)
    V.forward(0)
    both(0, 2)
    scan.finish()

    def state_of(p):
        g, rr = msg_rows(p, pg)
        cur = unpack_state(got[g, rr, :], True)
        for n in range(nb):
            rows = pl.ds(n * blk, blk)
            c = cols(p, 128)
            used = cflag[n] * cur
            st = used.astype(BF)
            states[n, p] = st
            cur = used + inc[n, p]
            num, den = state_part(p, n, blk, fq, None, st)
            rd = 1.0 / (1.0 + rden[rows, c] + den)
            att[rows, c] = ((acc[rows, c] + num) * rd).astype(BF)
            rden[rows, c] = rd

    loop_pairs(np_, state_of)
    keep(att, atto)
    keep(rden, rdeno)
    keep(states, stateso)
    for st in range(3, m + 1):
        both(0, st)
    mid[...] = xv[...].astype(F32)
    for g in range(nz):
        mid[...] += dot_t(att[:, g * ew : (g + 1) * ew], w4v[g, 3])
    norm_forward(mid, gains.at[1:2], biases.at[1:2], av)
    keep(mid, mido)
    C.finish()
    keep(cov, coo)
    transpose_perm(ns, av, a2t)
    transpose_perm(ns, cov, ct)
    acc[...] = mid[...]
    da2[...] = jnp.zeros_like(da2)
    tile = gub.shape[2]
    per = ff // tile
    steps = nz * per

    def place(i):
        g = pick_group(order, h, i // per)
        return g, pl.ds(pl.multiple_of(lax.rem(i, per) * tile, 128), tile)

    def flush(i, slot):
        g, c = place(i)
        return (
            pltpu.make_async_copy(gub.at[slot], gu.at[g, :, c], osem.at[slot, 0]),
            pltpu.make_async_copy(gdb.at[slot], gd.at[g, :, c], osem.at[slot, 1]),
        )

    def step(i, _):
        slot = lax.rem(i, 2)
        for j in range(steps):
            due = [(k, st) for k in range(1, far) for st in range(m + 1) if max(0, (k + 1) * per - (m - st)) == j]
            if due:

                @pl.when(i == j)
                def _(due=due):
                    for k, st in due:
                        both(k, st)
                        if st == 0:
                            U.forward(k)
                            V.forward(k)

        @pl.when(i >= 2)
        def _():
            for cp in flush(i - 2, slot):
                cp.wait()

        g, c = place(i)
        wub, wdb = wuv[g, 0, :, c], wdv[g, 0, c, :]
        up = dot(av[...], wub)
        hidf, slope = gelu_parts(up)
        hid = hidf.astype(BF)
        acc[...] += dot(hid, wdb)
        gdb[slot] = dot(ct[...], hid).astype(BF)
        dup = (slope * dot_t(cov[...], wdb)).astype(BF)
        da2[...] += dot_t(dup, wub)
        gub[slot] = dot(a2t[...], dup).astype(BF)
        for cp in flush(i, slot):
            cp.start()
        return 0

    lax.fori_loop(0, steps, step, 0)
    keep(da2, da2o)
    av[...] = acc[...].astype(BF)
    keep(av, lo)
    for i in range(max(0, steps - 2), steps):
        for cp in flush(i, i % 2):
            cp.wait()
    for cp in outs:
        cp.wait()
    X.drain()
    C.drain()
    scan.drain()
    for a in (W, U, V):
        a.drain()


def fore(ns, nz, nb, tables, tok, cot, wq, wo, wu, wd, gains, biases, pad):
    t, d = tok.shape[0] // nz, wq.shape[1]
    ew, ff = wq.shape[2], wu.shape[2]
    np_ = d // 128
    m = ns.bit_length() - 1
    dma = pltpu.SemaphoreType.DMA
    vm = pltpu.VMEM
    tile = 512 if ff % 512 == 0 else ff
    one = ((ew // 128) * MSG, 128)
    nzs = 3 * 2 * (nz - 1) * 2
    td, tdf = ((t, d), BF), ((t, d), F32)
    outs = [td, td, td, td, td, td, tdf, ((nb, np_, 128, 128), BF), tdf, ((nz, 4, d, ew), BF), td, tdf,
            ((nz, d, ff), BF), ((nz, d, ff), BF)]
    args = tables + (tok, cot, wq, wo, wu, wd, gains, biases, pad)
    return pl.pallas_call(
        functools.partial(fore_kernel, ns, nz, nb),
        out_shape=tuple(jax.ShapeDtypeStruct(s, dt) for s, dt in outs),
        in_specs=[smem_spec()] * 4 + [any_spec()] * 6 + [vmem_spec()] * 3,
        out_specs=(any_spec(),) * len(outs),
        scratch_shapes=[vm((t, d), BF)] * 7
        + [vm((d, t), BF)] * 2
        + [vm((t, d), F32)] * 4
        + [
            vm((nb, np_, 128, 128), F32),
            vm((nb, np_, 128, 128), BF),
            vm((nz, 4, d, ew), BF),
            vm((nz, 1, d, ff), BF),
            vm((nz, 1, ff, d), BF),
            vm((2, d, tile), BF),
            vm((2, d, tile), BF),
            vm((nz,) + one, BF),
            vm((nz,) + one, BF),
            vm((ns,) + one, BF),
            vm(one, BF),
            vm((nz,) + one, BF),
            vm((nz,) + one, BF),
            dma((2,)),
            dma((2 * (nz - 1) * parts_of(t),)),
            dma((2 * (nz - 1) * parts_of(t),)),
            dma((nzs,)),
            dma((nzs,)),
            dma((nzs * m,)),
            dma((nzs * m,)),
            dma((4,)),
            dma((16,)),
            dma((2, 2)),
        ]
        + [dma((nz - 1,)), dma((nz - 1,)), dma((ns - 1,)), dma((ns - 1,)), dma((nz - 1,)), dma((nz - 1,))],
        name="fore",
        compiler_params=pltpu.CompilerParams(collective_id=0, has_side_effects=True, vmem_limit_bytes=62 * 2**20),
    )(*args)


def add_block(dst, dlead, dstart, src, slead, n):
    blk = min(n, 64)

    def step(i, _):
        a = dst[dlead + (pl.ds(pl.multiple_of(dstart + i * blk, 16), blk), slice(None))]
        b = src[slead + (pl.ds(pl.multiple_of(i * blk, 16), blk), slice(None))]
        dst[dlead + (pl.ds(pl.multiple_of(dstart + i * blk, 16), blk), slice(None))] = (
            a.astype(F32) + b.astype(F32)
        ).astype(BF)
        return 0

    lax.fori_loop(0, n // blk, step, 0)


class Reduce:
    def __init__(self, p, idx, tz, acc, lead, src, own, rec, zbuf, zslot, zx, xslot, sems, out):
        self.p, self.idx, self.tz = p, idx, tz
        self.acc, self.lead, self.src, self.own, self.rec = acc, lead, src, own, rec
        self.zbuf, self.zslot, self.zx, self.xslot, self.out = zbuf, zslot, zx, xslot, out
        self.cs, self.cr, self.zs, self.zr, self.ls = sems
        orders = ([0] + p.o0, [0] + p.o1)
        self.orders = orders
        self.units = rec[0].shape[2] * 2 // p.ns
        self.bit = [[(p.s >> orders[f][j]) & 1 for j in range(p.m)] for f in range(2)]
        self.pos = []
        for f in range(2):
            pos, seq = 0, []
            for j in range(1, p.m):
                seq.append(pos)
                pos = pos + self.bit[f][j] * self.size(j)
            self.pos.append(seq + [pos])

    def size(self, j):
        return self.units * (self.p.ns >> (j + 1))

    def step(self, f, j):
        i = (self.idx * self.p.m + j) * 2 + f
        b = self.bit[f][j]
        n = self.size(j)
        if j == 0:
            src = self.src(f, 1 - b)
        else:
            at = self.pos[f][j - 1] + (1 - b) * n
            src = self.acc.at[self.lead(f) + (pl.ds(pl.multiple_of(at, 16), n), slice(None))]
        dst = self.rec[j].at[self.rslot(j), f]
        return rcopy(src, dst, self.cs.at[i], self.cr.at[i], self.p.bit[self.orders[f][j]])

    def rslot(self, j):
        return self.idx

    def load(self, f):
        return pltpu.make_async_copy(
            self.src(f, self.bit[f][0]), self.acc.at[self.lead(f)], self.ls.at[self.idx * 2 + f]
        )

    def route(self, hh):
        nz, tz = self.p.nz, self.tz
        q, count, inward = (hh, tz, 1) if hh < tz else (nz - 1 - hh, nz - 1 - tz, -1)
        if q % 2 == 0 and q + 1 < count:
            return False, hh + inward, 0
        return q % 2 == 1, tz, q // 2 + (0 if hh < tz else (tz + 1) // 2)

    def landing(self, f, slot):
        return self.zbuf.at[self.zslot, f] if slot == 0 else self.zx.at[self.xslot, slot - 1, f]

    def zcopy(self, f, to, slot):
        i = self.idx * 2 + f
        mine = self.acc.at[self.lead(f) + (pl.ds(pl.multiple_of(self.pos[f][-1], 16), self.units), slice(None))]
        r = (self.idx * (self.p.nz // 2) + slot) * 2 + f
        return rcopy(mine, self.landing(f, slot), self.zs.at[i], self.zr.at[r], (self.p.s, to))

    def advance(self, st):
        m, tz, nz = self.p.m, self.tz, self.p.nz
        if st <= m:
            for f in range(2):
                if st > 0:
                    self.step(f, st - 1).wait_recv()
                    if st == 1 and self.own:
                        self.load(f).wait()
                    add_block(self.acc, self.lead(f), self.pos[f][st - 1], self.rec[st - 1], (self.rslot(st - 1), f), self.size(st - 1))
                elif self.own:
                    self.load(f).start()
                if st < m:
                    self.step(f, st).start()
        if st == m or st == m + 1:
            for hh in range(nz):
                inner, to, slot = self.route(hh) if hh != tz else (None, 0, 0)
                if inner is None or inner != (st == m + 1):
                    continue

                @pl.when(self.p.h == hh)
                def _(inner=inner, to=to, slot=slot):
                    for f in range(2):
                        if inner:
                            self.zcopy(f, to, 0).wait_recv()
                            add_block(self.acc, self.lead(f), self.pos[f][-1], self.zbuf, (self.zslot, f), self.units)
                        self.zcopy(f, to, slot).start()

        if st == m + 2:

            @pl.when(self.p.h == tz)
            def _():
                for f in range(2):
                    v = self.acc[self.lead(f) + (pl.ds(pl.multiple_of(self.pos[f][-1], 16), self.units), slice(None))]
                    v = v.astype(F32)
                    for slot in range((tz + 1) // 2 + (nz - tz) // 2):
                        self.zcopy(f, tz, slot).wait_recv()
                        ref = self.landing(f, slot)
                        v = v + ref[...].astype(F32)
                    self.out[f] = v.astype(BF)

    def drain(self):
        for f in range(2):
            for j in range(self.p.m):
                self.step(f, j).wait_send()

        @pl.when(self.p.h != self.tz)
        def _():
            for f in range(2):
                self.zcopy(f, 0, 0).wait_send()


class RowsOut:
    def __init__(self, pl_, src, dst, ssem, rsem, lsem, base):
        self.p, self.src, self.dst, self.sems, self.base = pl_, src, dst, (ssem, rsem, lsem), base
        self.t, self.ew = src.shape[0], dst.shape[1]
        self.parts = parts_of(self.t)
        self.n = self.t // self.parts

    def copy(self, r, d, dev, row):
        i = (self.base * (self.p.nz - 1) + d) * self.parts + r
        return rcopy(
            self.src.at[pl.ds(r * self.n, self.n), pl.ds(pl.multiple_of(dev[1] * self.ew, 128), self.ew)],
            self.dst.at[pl.ds(pl.multiple_of(row * self.t + r * self.n, 16), self.n), :],
            self.sems[0].at[i],
            self.sems[1].at[i],
            dev,
        )

    def own(self):
        h = self.p.h
        return pltpu.make_async_copy(
            self.src.at[:, pl.ds(pl.multiple_of(h * self.ew, 128), self.ew)],
            self.dst.at[pl.ds(pl.multiple_of(h * self.t, 16), self.t), :],
            self.sems[2].at[self.base],
        )

    def begin(self, lo, hi):
        for r in range(lo, min(hi, self.parts)):
            if r == 0:
                self.own().start()
            for d, dev in enumerate(self.p.zdev):
                self.copy(r, d, dev, self.p.h).start()

    def finish(self):
        for r in range(self.parts):
            for d, frm in enumerate(self.p.zfrom):
                self.copy(r, d, frm, frm[1]).wait_recv()
            for d, dev in enumerate(self.p.zdev):
                self.copy(r, d, dev, self.p.h).wait_send()
        self.own().wait()


class Small:
    def __init__(self, pl_, cur, rec, gz, ssem, rsem, out):
        self.p, self.cur, self.rec, self.gz, self.sems, self.out = pl_, cur, rec, gz, (ssem, rsem), out

    def hop(self, j):
        return rcopy(self.cur.at[j], self.rec.at[j], self.sems[0].at[j], self.sems[1].at[j], self.p.bit[j])

    def zhop(self, d, dev, slot):
        i = self.p.m + d
        return rcopy(self.cur.at[self.p.m], self.gz.at[slot], self.sems[0].at[i], self.sems[1].at[i], dev)

    def advance(self, st):
        m = self.p.m
        if 0 < st <= m:
            self.hop(st - 1).wait_recv()
            self.cur[st] = self.cur[st - 1] + self.rec[st - 1]
        if st < m:
            self.hop(st).start()
        if st == m:
            for d, dev in enumerate(self.p.zdev):
                self.zhop(d, dev, self.p.h).start()
            self.gz[self.p.h] = self.cur[m]
        if st == m + 1:
            for d, frm in enumerate(self.p.zfrom):
                self.zhop(d, frm, frm[1]).wait_recv()
            total = self.gz[0]
            for z in range(1, self.p.nz):
                total = total + self.gz[z]
            self.out[...] = total
            for j in range(m):
                self.hop(j).wait_send()
            for d, dev in enumerate(self.p.zdev):
                self.zhop(d, dev, self.p.h).wait_send()


def back_queries(p, n, blk, fk, vb, fq, dr0, dr1, st, dq):
    rows = pl.ds(n * blk, blk)
    c = cols(p, 128)
    q2, k2, v2, e0, e1 = fq[rows, c], fk[rows, c], vb[rows, c], dr0[rows, c], dr1[rows, c]
    g0, g1 = with_ones(v2)
    keep = causal_mask(blk)
    ds0 = jnp.where(keep, dot_t(e0, g0), 0.0).astype(BF)
    ds1 = jnp.where(keep, dot_t(e1, g1), 0.0).astype(BF)
    dfq = jnp.where(lane_low(q2.shape), dot(ds0, k2), dot(ds1, k2))
    dfq = dfq + dot_t(jnp.concatenate([e0, e1], axis=1), split_state(st))
    dq[rows, c] = (dfq * jnp.minimum(q2.astype(F32), 1.0)).astype(BF)


def back_keys(p, n, blk, fk, vb, fq, dr0, dr1, dst):
    rows = pl.ds(n * blk, blk)
    c = cols(p, 128)
    q2, k2, v2, e0, e1 = fq[rows, c], fk[rows, c], vb[rows, c], dr0[rows, c], dr1[rows, c]
    g0, g1 = with_ones(v2)
    keep_t = lax.broadcasted_iota(jnp.int32, (blk, blk), 0) <= lax.broadcasted_iota(jnp.int32, (blk, blk), 1)
    low = lane_low(q2.shape)
    dt0 = jnp.where(keep_t, dot_t(g0, e0), 0.0).astype(BF)
    dt1 = jnp.where(keep_t, dot_t(g1, e1), 0.0).astype(BF)
    dfk = jnp.where(low, dot(dt0, q2), dot(dt1, q2))
    dfk = dfk + dot_t(jnp.concatenate([g0, g1], axis=1), split_state(dst))
    st0, st1 = masked_scores(k2, q2, keep_t)
    own = jnp.where(row_low((128, 128)) == lane_low((128, 128)), dst, jnp.zeros_like(dst))
    dvv = jnp.where(low, dot(st0, e0), dot(st1, e1)) + dot(k2, own)
    fk[rows, c] = (dfk * jnp.minimum(k2.astype(F32), 1.0)).astype(BF)
    vb[rows, c] = dvv.astype(BF)


def aft_kernel(ns, nz, nb, *refs):
    cflag, wt, wp, wl = refs[:4]
    x, co, fqi, fki, vbi, atti, rdeni, statesi, midi, w4, lo, da2i, gu, gd, gains, biases = refs[4:20]
    lo_o, gt_o, gbo, o4, ou, od = refs[20:26]
    (fq, fk, vb, dr0, dr1, att, dml, dq, a1t, dmt, datt, mid, dmid, rden, ginc, states, ring, sums2, sums1,
     pool, rec0, *more) = refs[26:]
    m = ns.bit_length() - 1
    rec = [rec0] + list(more[: m - 1])
    (zbuf, zx, msg, r1, r2, tot, outb, got, gcur, grec, gz,
     lsem, rsem, asem, tsend, trecv, tl, csend, crecv, zsend, zrecv, gsend, grecv,
     c1s, c1r, c2s, c2r, c3s, c3r) = more[m - 1 :]
    P_ = Places(ns, nz)
    t, d = fq.shape
    blk = t // nb
    ew = lo_o.shape[1]
    np_ = d // 128
    pg = msg.shape[1] // MSG
    quarter = d // 4
    scan = Scan(P_, wt, wp, wl, msg, r1, r2, tot, outb, got, (c1s, c1r, c2s, c2r, c3s, c3r))
    lo_a = RowsOut(P_, lo, lo_o, tsend, trecv, tl, 0)
    gt_a = RowsOut(P_, dml, gt_o, tsend, trecv, tl, 1)
    small = Small(P_, gcur, grec, gz, gsend, grecv, gbo)
    sems = (csend, crecv, zsend, zrecv, asem)
    ends_first = [z for pair in zip(range(nz // 2), range(nz - 1, nz // 2 - 1, -1)) for z in pair]
    ffn, attn = [], []
    for a, (g, out) in enumerate(((gd, od), (gu, ou))):
        for i, tz in enumerate(ends_first):
            idx = a * nz + i
            ffn.append(
                Reduce(
                    P_, idx, tz, pool, lambda f, idx=idx: (idx, f),
                    lambda f, b, g=g, tz=tz: g.at[tz, f, pl.ds(pl.multiple_of(b * quarter, 16), quarter), :],
                    True, rec, zbuf, idx, zx, a, sems, out,
                )
            )
    top = [[(P_.s >> o[0]) & 1 for o in ([0] + P_.o0, [0] + P_.o1)][f] for f in range(2)]
    for i, tz in enumerate(ends_first):
        idx = 2 * nz + i
        attn.append(
            Reduce(
                P_, idx, tz, rec0, lambda f, tz=tz: (2 * tz + f, top[f]),
                lambda f, b, tz=tz: rec0.at[2 * tz + f, b],
                False, rec, zbuf, idx, zx, 2, sems, o4,
            )
        )
    loads = {}

    def load(name, src, dst):
        i = len(loads)
        loads[name] = (src, dst, i)
        pltpu.make_async_copy(src, dst, lsem.at[i]).start()

    def ready(*names):
        for name in names:
            src, dst, i = loads[name]
            pltpu.make_async_copy(src, dst, lsem.at[i]).wait()

    uses = [(g, 3) for g in range(nz)] + [(g, c) for g in ends_first for c in range(3)]
    depth = ring.shape[0]

    def ring_copy(i):
        g, c = uses[i]
        return pltpu.make_async_copy(w4.at[g, c], ring.at[i % depth], rsem.at[i % depth])

    load("da2", da2i, datt)
    load("mid", midi, mid)
    load("co", co, dr0)
    for i in range(depth):
        ring_copy(i).start()
    load("att", atti, att)
    load("rden", rdeni, rden)
    load("fq", fqi, fq)
    enter(P_.zdev + P_.sdev)
    for it in ffn:
        it.advance(0)
    lo_a.begin(0, lo_a.parts - 1)
    load("fk", fki, fk)
    load("vb", vbi, vb)
    load("states", statesi, states)
    last = m + 2
    half_n = len(ffn) // 2
    gaps = [0] + [half_n + 0.5] * (m - 1) + [3, 3]
    at = [sum(gaps[:st]) for st in range(1, last + 1)]
    steps = sorted((i + at[st - 1], i, st) for i in range(len(ffn)) for st in range(1, last + 1))
    state = {"w": 0}

    def tick(n=1):
        for _ in range(n):
            if state["w"] < len(steps):
                _, i, st = steps[state["w"]]
                ffn[i].advance(st)
                state["w"] += 1

    n_first = 1 + max(j for j, x in enumerate(steps) if x[2] == 1)
    ready("da2", "mid", "co")

    def emit(rows, v):
        dmid[rows, :] = v
        dml[rows, :] = v.astype(BF)

    norm_backward(datt, mid, gains.at[1:2], dr0, emit, sums2)
    tick(max(1, half_n - 2))
    for i in range(nz):
        ring_copy(i).wait()
        datt[:, i * ew : (i + 1) * ew] = dot(dml[...], ring[i % depth])
        if i + depth < len(uses):
            ring_copy(i + depth).start()
    tick()
    ready("att", "rden", "fq")

    def turn(p):
        for n in range(nb):
            attend_gradient(p, n, blk, datt, att, rden, dr0, dr1)
        chunk_gradients(p, blk, nb, fq, dr0, dr1, ginc)
        cur = cflag[nb - 1] * ginc[nb - 1, p]
        for n in range(nb - 2, -1, -1):
            cur = cflag[n] * (cur + ginc[n, p])
        g, rr = msg_rows(p, pg)
        msg[g, rr, :] = pack_state(cur, 2)

    def in_parts(body, n, between):
        per = np_ // n
        for i in range(n):
            loop_pairs(per, lambda p, i=i: body(p + i * per))
            between(i)

    in_parts(turn, 4, lambda i: tick() if i == 1 else None)
    scan.phase1()
    lo_a.begin(lo_a.parts - 1, lo_a.parts)
    transpose_perm(ns, dml, dmt)
    load("x", x, dml)
    scan.phase2()
    tick(3)
    ready("fk", "vb", "states")

    def queries(p):
        for n in range(nb):
            back_queries(p, n, blk, fk, vb, fq, dr0, dr1, states[n, p], dq)

    def between(i):
        tick(max(0, n_first - state["w"]) if i == 1 else 2)
        if i == 1:
            scan.phase3()

    in_parts(queries, 4, between)
    ready("x")
    norm_forward(dml, gains.at[0:1], biases.at[0:1], dml)
    transpose_perm(ns, dml, a1t)
    load("x2", x, dml)
    scan.finish()

    def keys(p):
        g, rr = msg_rows(p, pg)
        cur = unpack_state(got[g, rr, :], False)
        for n in range(nb - 1, -1, -1):
            back_keys(p, n, blk, fk, vb, fq, dr0, dr1, cur.astype(BF))
            cur = cflag[n] * (cur + ginc[n, p])

    in_parts(keys, 4, lambda i: tick(3))
    awaves = []
    for w in range(len(attn) + last):
        awaves.append([(it, w - i) for i, it in enumerate(attn) if 0 <= w - i <= last])
    da1 = mid

    def put(tz, c, v):
        v = v.astype(BF)
        for f in range(2):
            for b in range(2):
                r = (2 * f + b) * quarter
                rec0[2 * tz + f, b, :, c * ew : (c + 1) * ew] = v[r : r + quarter, :]

    for i, tz in enumerate(ends_first):
        c0 = slice(tz * ew, (tz + 1) * ew)
        put(tz, 3, dot(dmt[...], att[:, c0]))
        for k, r in enumerate((dq, fk, vb)):
            put(tz, k, dot(a1t[...], r[:, c0]))
        for it, st in awaves[i]:
            it.advance(st)
        for k, r in enumerate((dq, fk, vb)):
            j = nz + i * 3 + k
            ring_copy(j).wait()
            v = dot_t(r[:, c0], ring[j % depth])
            if i == 0 and k == 0:
                da1[...] = v
            else:
                da1[...] += v
            if j + depth < len(uses):
                ring_copy(j + depth).start()
        tick(2)
    ready("x2")

    def emit1(rows, v):
        dml[rows, :] = v.astype(BF)

    norm_backward(da1, dml, gains.at[0:1], dmid, emit1, sums1)
    gt_a.begin(0, gt_a.parts)
    gcur[0] = jnp.zeros(gcur.shape[1:], F32)
    for i, (ref, k) in enumerate(((sums1, 0), (sums2, 0), (sums1, 1), (sums2, 1))):
        gcur[0, i : i + 1, :] = jnp.sum(ref[k], axis=0, keepdims=True)
    tick(len(steps))
    for w in range(len(attn), len(awaves)):
        small.advance(w - len(attn))
        for it, st in awaves[w]:
            it.advance(st)
    for st in range(len(awaves) - len(attn), m + 2):
        small.advance(st)
    lo_a.finish()
    gt_a.finish()
    for it in ffn + attn:
        it.drain()
    scan.drain()


def aft(ns, nz, nb, tables, x, co, fq, fk, vb, att, rden, states, mid, w4g, lo, da2, gu, gd, gains, biases):
    t, d = x.shape
    ew, ff = w4g.shape[3], gu.shape[3]
    m = ns.bit_length() - 1
    np_ = d // 128
    dma = pltpu.SemaphoreType.DMA
    vm = pltpu.VMEM
    one = ((ew // 128) * MSG, 128)
    unit = d // (2 * ns)
    n_items = 3 * nz
    depth = 4
    args = tables + (x, co, fq, fk, vb, att, rden, states, mid, w4g, lo, da2, gu, gd, gains, biases)
    piece = jax.ShapeDtypeStruct((2, unit, ff), BF)
    rows = jax.ShapeDtypeStruct((t * nz, ew), BF)
    return pl.pallas_call(
        functools.partial(aft_kernel, ns, nz, nb),
        out_shape=(rows, rows, jax.ShapeDtypeStruct((8, d), F32), piece, piece, piece),
        in_specs=[smem_spec()] * 4 + [any_spec()] * 14 + [vmem_spec()] * 2,
        out_specs=(any_spec(),) * 2 + (vmem_spec(),) * 4,
        scratch_shapes=[vm((t, d), BF)] * 8
        + [vm((d, t), BF)] * 2
        + [vm((t, d), F32)] * 4
        + [
            vm((nb, np_, 128, 128), F32),
            vm((nb, np_, 128, 128), BF),
            vm((depth, d, ew), BF),
            vm((2, 8, d), F32),
            vm((2, 8, d), F32),
            vm((2 * nz, 2, d // 4, ff), BF),
        ]
        + [vm((n_items, 2, d // 4 >> j, ff), BF) for j in range(m)]
        + [
            vm((n_items, 2, unit, ff), BF),
            vm((3, max(1, nz // 2 - 1), 2, unit, ff), BF),
            vm((nz,) + one, BF),
            vm((nz,) + one, BF),
            vm((ns,) + one, BF),
            vm(one, BF),
            vm((nz,) + one, BF),
            vm((nz,) + one, BF),
            vm((m + 1, 8, d), F32),
            vm((m, 8, d), F32),
            vm((nz, 8, d), F32),
            dma((16,)),
            dma((depth,)),
            dma((2 * n_items,)),
            dma((2 * (nz - 1) * parts_of(t),)),
            dma((2 * (nz - 1) * parts_of(t),)),
            dma((2,)),
            dma((n_items * m * 2,)),
            dma((n_items * m * 2,)),
            dma((n_items * 2,)),
            dma((n_items * nz,)),
            dma((m + nz - 1,)),
            dma((m + nz - 1,)),
        ]
        + [dma((nz - 1,)), dma((nz - 1,)), dma((ns - 1,)), dma((ns - 1,)), dma((nz - 1,)), dma((nz - 1,))],
        name="aft",
        compiler_params=pltpu.CompilerParams(collective_id=1, has_side_effects=True, vmem_limit_bytes=63 * 2**20),
    )(*args)


def shards(ns, nz, tokens, lengths, pad_mask, w_qkv, w_out, w_up, w_down, norm_gains, norm_biases, out_cotangent):
    rows = tokens.shape[0]
    t = rows // nz
    d = w_qkv.shape[1]
    ff = w_up.shape[1]
    ew = d // nz
    blk = math.gcd(t, UNIT)
    nb = t // blk
    s, h = lax.axis_index("seq"), lax.axis_index("head")

    ends = jnp.cumsum(lengths)

    def item_at(p):
        return jnp.sum((p[..., None] >= ends).astype(jnp.int32), axis=-1)

    ndev = ns * nz
    last = item_at((jnp.arange(ndev, dtype=jnp.int32) + 1) * t - 1)
    before = jnp.concatenate([jnp.full((1,), -1, jnp.int32), last[:-1]])
    me = s * nz + h
    chunk = item_at(me * t + jnp.arange(nb, dtype=jnp.int32) * blk)
    prior = lax.dynamic_slice_in_dim(before, me, 1)
    cflag = (chunk == jnp.concatenate([prior, chunk[:-1]])).astype(F32)
    last2, before2 = last.reshape(ns, nz), before.reshape(ns, nz)
    my_last, my_before = last2[s], before2[s]
    sidx, zidx = jnp.arange(ns), jnp.arange(nz)
    fwt = (my_last == my_last[-1]).astype(F32)
    fwp = ((sidx[None, :] < s) & (last2[None, :, -1] == my_before[:, None])).astype(F32)
    fwl = ((zidx[None, :] < zidx[:, None]) & (my_last[None, :] == my_before[:, None])).astype(F32)
    bwt = (my_before == my_before[0]).astype(F32)
    bwp = ((sidx[None, :] > s) & (before2[None, :, 0] == my_last[:, None])).astype(F32)
    bwl = ((zidx[None, :] > zidx[:, None]) & (my_before[None, :] == my_last[:, None])).astype(F32)

    pad = lax.dynamic_slice_in_dim(pad_mask, h * t, t).astype(F32)[:, None]
    x, co, fq, fk, vb, att, rden, states, mid, w4g, lo, da2, gu, gd = fore(
        ns, nz, nb, (cflag, fwt, fwp, fwl), tokens, out_cotangent, w_qkv, w_out.T[None], w_up[None], w_down[None],
        norm_gains, norm_biases, pad,
    )
    half = (nz, 2, d // 2, ff)
    lo_o, gt_o, gbo, o4, ou, od = aft(
        ns, nz, nb, (cflag, bwt, bwp, bwl), x, co, fq, fk, vb, att, rden, states, mid, w4g, lo, da2,
        gu.reshape(half), gd.reshape(half), norm_gains, norm_biases,
    )
    piece = d // ns
    o4 = o4.reshape(piece, 4, ew).transpose(1, 0, 2).astype(F32)
    w = d // ndev
    gbs = lax.dynamic_slice_in_dim(gbo, (h * ns + s) * w, w, 1)
    return (
        lo_o,
        gt_o.astype(F32),
        o4[:3],
        o4[3].T,
        ou.reshape(piece, ff).astype(F32),
        od.reshape(piece, ff).astype(F32).T,
        gbs[:2],
        gbs[2:4],
    )


def solution(mesh):
    in_specs = (
        P("seq", "head"),
        P(),
        P("seq"),
        P(None, None, "head"),
        P("head", None),
        P(None, "head"),
        P("head", None),
        P(),
        P(),
        P("seq", "head"),
    )
    out_specs = (
        P("seq", "head"),
        P("seq", "head"),
        P(None, "seq", "head"),
        P("head", "seq"),
        P("seq", "head"),
        P("head", "seq"),
        P(None, ("head", "seq")),
        P(None, ("head", "seq")),
    )
    f = functools.partial(shards, mesh.shape["seq"], mesh.shape["head"])
    return jax.shard_map(f, mesh=mesh, in_specs=in_specs, out_specs=out_specs, check_vma=False)
```

```python
import functools
import math

import jax
import jax.numpy as jnp
from jax import lax
from jax.experimental import pallas as pl
from jax.experimental.pallas import tpu as pltpu
from jax.sharding import PartitionSpec as P

HD = 64
UNIT = 768
EPS = 1e-05
MESH = pl.DeviceIdType.MESH
BF = jnp.bfloat16
F32 = jnp.float32


def bit_orders(ns):
    m = ns.bit_length() - 1
    xs = list(range(1, 1 + (m - 1) // 2))
    ys = list(range(1 + (m - 1) // 2, m))
    return xs + ys, ys + xs


def bits_to(s, order):
    out = 0
    for j, b in enumerate(order):
        out = out + (((s >> b) & 1) << j)
    return out


def rcopy(src, dst, send, recv, dev):
    return pltpu.make_async_remote_copy(
        src_ref=src, dst_ref=dst, send_sem=send, recv_sem=recv, device_id=dev, device_id_type=MESH
    )


def greet(devs):
    bar = pltpu.get_barrier_semaphore()
    for d in devs:
        pl.semaphore_signal(bar, inc=1, device_id=d, device_id_type=MESH)


def greeted(devs):
    pl.semaphore_wait(pltpu.get_barrier_semaphore(), len(devs))


def z_others(s, h, nz):
    return [(s, lax.rem(h + d, nz)) for d in range(1, nz)]


def any_spec():
    return pl.BlockSpec(memory_space=pl.ANY)


def vmem_spec():
    return pl.BlockSpec(memory_space=pltpu.VMEM)


def smem_spec():
    return pl.BlockSpec(memory_space=pltpu.SMEM)


def dot(a, b):
    return lax.dot_general(a, b, (((1,), (0,)), ((), ())), preferred_element_type=F32)


def dot_t(a, b):
    return lax.dot_general(a, b, (((1,), (1,)), ((), ())), preferred_element_type=F32)


def t_dot(a, b):
    return lax.dot_general(a, b, (((0,), (0,)), ((), ())), preferred_element_type=F32)


def lane_low(shape):
    return lax.broadcasted_iota(jnp.int32, shape, 1) < HD


def row_low(shape):
    return lax.broadcasted_iota(jnp.int32, shape, 0) < HD


def row_block(t):
    return 96 if t % 96 == 0 else 32


def over_rows(t, body):
    rb = row_block(t)

    def step(i, _):
        body(pl.ds(pl.multiple_of(i * rb, 32), rb))
        return 0

    lax.fori_loop(0, t // rb, step, 0)


def normed(v):
    mean = jnp.mean(v, axis=1, keepdims=True)
    c = v - mean
    w = lax.rsqrt(jnp.mean(c * c, axis=1, keepdims=True) + EPS)
    return c * w, w


def norm_forward(src, gain, bias, dst):
    def body(rows):
        xh, _ = normed(src[rows, :].astype(F32))
        dst[rows, :] = (xh * gain[...] + bias[...]).astype(BF)

    over_rows(src.shape[0], body)


def norm_backward(e_ref, src, gain, add, emit, sums):
    sums[0] = jnp.zeros(sums.shape[1:], F32)
    sums[1] = jnp.zeros(sums.shape[1:], F32)

    def body(rows):
        e = e_ref[rows, :]
        xh, w = normed(src[rows, :].astype(F32))
        eg = e * gain[...]
        m1 = jnp.mean(eg, axis=1, keepdims=True)
        m2 = jnp.mean(eg * xh, axis=1, keepdims=True)
        emit(rows, add[rows, :].astype(F32) + w * (eg - m1 - xh * m2))
        n = e.shape[0]
        sums[0] += jnp.sum((e * xh).reshape(n // 8, 8, -1), axis=0)
        sums[1] += jnp.sum(e.reshape(n // 8, 8, -1), axis=0)

    over_rows(src.shape[0], body)


def transpose_perm(ns, src, dst):
    d = dst.shape[0]
    u = d // (2 * ns)
    o0, o1 = bit_orders(ns)
    m = ns.bit_length() - 1
    orders = ([0] + o0, [0] + o1)
    for j in range(d // 128):
        tr = src[:, j * 128 : (j + 1) * 128].T
        for i in range(128 // u):
            g = j * (128 // u) + i
            dev, f = g // 2, g % 2
            q = sum(((dev >> b) & 1) << (m - 1 - k) for k, b in enumerate(orders[f]))
            row = f * (d // 2) + q * u
            dst[row : row + u, :] = tr[i * u : (i + 1) * u, :]


def phi(y):
    return jnp.where(y > 0, y + 1.0, jnp.exp(jnp.minimum(y, 0.0)))


def cols(i, n):
    return pl.ds(pl.multiple_of(i * n, 128), n)


def project(a1, wg, g, pad, fq, fk, vb):
    ew = wg.shape[3]
    c = cols(g, ew)
    fq[:, c] = phi(dot(a1[...], wg[g, 0])).astype(BF)
    mask = jnp.concatenate([pad[...]] * (ew // 128), axis=1)
    fk[:, c] = (mask * phi(dot(a1[...], wg[g, 1]))).astype(BF)
    vb[:, c] = dot(a1[...], wg[g, 2]).astype(BF)


def with_ones(v2):
    one = jnp.ones_like(v2)
    low = lane_low(v2.shape)
    return jnp.where(low, v2, one), jnp.where(low, one, v2)


def chunk_sums(p, blk, nb, fk, vb, inc):
    for n in range(nb):
        rows = pl.ds(n * blk, blk)
        k2, v2 = fk[rows, cols(p, 128)], vb[rows, cols(p, 128)]
        r = t_dot(k2, jnp.concatenate(with_ones(v2), axis=1))
        inc[n, p] = jnp.where(row_low((128, 128)), r[:, :128], r[:, 128:])


def causal_mask(blk):
    return lax.broadcasted_iota(jnp.int32, (blk, blk), 0) >= lax.broadcasted_iota(jnp.int32, (blk, blk), 1)


def masked_scores(a2, b2, keep):
    low = lane_low(b2.shape)
    zero = jnp.zeros_like(b2)
    return [
        jnp.where(keep, dot_t(a2, b), 0.0).astype(BF)
        for b in (jnp.where(low, b2, zero), jnp.where(low, zero, b2))
    ]


def split_state(st):
    low = row_low(st.shape)
    zero = jnp.zeros_like(st)
    return jnp.concatenate([jnp.where(low, st, zero), jnp.where(low, zero, st)], axis=1)


def attend_gradient(p, n, blk, datt, att, rden, dr0, dr1):
    rows = pl.ds(n * blk, blk)
    c = cols(p, 128)
    e = datt[rows, c]
    rd = rden[rows, c]
    low = lane_low(e.shape)
    lane = lax.broadcasted_iota(jnp.int32, e.shape, 1)
    dn = e * rd
    w = dn * att[rows, c].astype(F32)
    d0 = -jnp.sum(jnp.where(low, w, 0.0), axis=1, keepdims=True)
    d1 = -jnp.sum(jnp.where(low, 0.0, w), axis=1, keepdims=True)

    def parts(dd, first):
        hi = dd.astype(BF).astype(F32)
        return jnp.where(lane == first, hi, jnp.where(lane == first + 1, dd - hi, 0.0))

    dr0[rows, c] = jnp.where(low, dn, parts(d0, HD)).astype(BF)
    dr1[rows, c] = jnp.where(low, parts(d1, 0), dn).astype(BF)


def chunk_gradients(p, blk, nb, fq, dr0, dr1, ginc):
    for n in range(nb):
        rows = pl.ds(n * blk, blk)
        c = cols(p, 128)
        r = t_dot(fq[rows, c], jnp.concatenate([dr0[rows, c], dr1[rows, c]], axis=1))
        ginc[n, p] = jnp.where(row_low((128, 128)), r[:, :128], r[:, 128:])


def gelu_parts(s):
    c0 = math.sqrt(2.0 / math.pi)
    s2 = s * s
    th = jnp.tanh(c0 * (s + 0.044715 * s * s2))
    h = 0.5 * (1.0 + th)
    slope = h + 0.5 * s * (1.0 - th * th) * (c0 * (1.0 + 3 * 0.044715 * s2))
    return s * h, slope


def loop_pairs(n, body):
    def step(p, _):
        body(p)
        return 0

    lax.fori_loop(0, n, step, 0)


def group_order(nz):
    out = []
    for h in range(nz):
        seq = [h]
        for k in range(nz - 1):
            for o in (h - 1 - k, h + 1 + k):
                if 0 <= o < nz:
                    seq.append(o)
        out.append(seq)
    return out


def pick_group(order, h, i):
    out = 0
    for hh, seq in enumerate(order):
        for ii, g in enumerate(seq):
            if isinstance(i, int):
                if ii == i:
                    out = out + jnp.where(h == hh, g, 0)
            else:
                out = out + jnp.where((h == hh) & (i == ii), g, 0)
    return out


class Places:
    def __init__(self, ns, nz):
        self.ns, self.nz = ns, nz
        self.s, self.h = lax.axis_index("seq"), lax.axis_index("head")
        self.o0, self.o1 = bit_orders(ns)
        self.m = ns.bit_length() - 1
        self.zdev = z_others(self.s, self.h, nz)
        self.zfrom = [(self.s, lax.rem(self.h + nz - 1 - d, nz)) for d in range(nz - 1)]
        self.sdev = [(jnp.bitwise_xor(self.s, d), self.h) for d in range(1, ns)]
        self.bit = [(jnp.bitwise_xor(self.s, 1 << b), self.h) for b in range(self.m)]
        self.left, self.right = (self.s, self.h - 1), (self.s, self.h + 1)


class Gather:
    def __init__(self, pl_, buf, zs, zr, ps, pr, base):
        self.p, self.buf, self.base = pl_, buf, base
        self.sems = (zs, zr, ps, pr)
        self.orders = (pl_.o0 + [0], pl_.o1 + [0])
        self.half = buf.shape[2] // 2
        self.r = self.half // pl_.ns
        pos = [bits_to(pl_.s, o) for o in self.orders]
        self.zrow = [f * self.half + pos[f] * self.r for f in range(2)]
        self.mine = [
            [f * self.half + ((pos[f] >> j) << j) * self.r for j in range(pl_.m)] for f in range(2)
        ]
        self.theirs = [
            [f * self.half + jnp.bitwise_xor((pos[f] >> j) << j, 1 << j) * self.r for j in range(pl_.m)]
            for f in range(2)
        ]
        h, nz = pl_.h, pl_.nz
        self.origin = [(h - 1 - k, h + 1 + k) for k in range(nz - 1)]
        self.valid = [(h - 1 - k >= 0, h + 1 + k < nz) for k in range(nz - 1)]
        self.more = [((h - 1 - k >= 0) & (h + 1 < nz), (h + 1 + k < nz) & (h >= 1)) for k in range(nz - 1)]

    def rows(self, start, n):
        return pl.ds(pl.multiple_of(start, 16), n)

    def zcopy(self, f, k, d, origin):
        ref = self.buf.at[origin, :, self.rows(self.zrow[f], self.r), :]
        i = ((self.base * 2 + f) * (self.p.nz - 1) + k) * 2 + d
        return rcopy(ref, ref, self.sems[0].at[i], self.sems[1].at[i], self.p.right if d == 0 else self.p.left)

    def pcopy(self, f, k, d, j, starts):
        n = self.r << j
        ref = self.buf.at[self.origin[k][d], :, self.rows(starts[f][j], n), :]
        i = (((self.base * 2 + f) * (self.p.nz - 1) + k) * 2 + d) * self.p.m + j
        return rcopy(ref, ref, self.sems[2].at[i], self.sems[3].at[i], self.p.bit[self.orders[f][j]])

    def begin(self):
        for d, cond in enumerate((self.p.h + 1 < self.p.nz, self.p.h >= 1)):

            @pl.when(cond)
            def _(d=d):
                for f in range(2):
                    self.zcopy(f, 0, d, self.p.h).start()

    def forward(self, k):
        if k + 1 < self.p.nz - 1:
            for d in range(2):

                @pl.when(self.more[k][d])
                def _(d=d):
                    for f in range(2):
                        self.zcopy(f, k + 1, d, self.origin[k][d]).start()

    def advance(self, k, st):
        for d in range(2):

            @pl.when(self.valid[k][d])
            def _(d=d):
                for f in range(2):
                    if st == 0:
                        self.zcopy(f, k, d, self.origin[k][d]).wait_recv()
                    else:
                        self.pcopy(f, k, d, st - 1, self.theirs).wait_recv()
                if st < self.p.m:
                    for f in range(2):
                        self.pcopy(f, k, d, st, self.mine).start()

    def drain(self):
        for d, cond in enumerate((self.p.h + 1 < self.p.nz, self.p.h >= 1)):

            @pl.when(cond)
            def _(d=d):
                for f in range(2):
                    self.zcopy(f, 0, d, self.p.h).wait_send()

        for k in range(self.p.nz - 1):
            for d in range(2):

                @pl.when(self.valid[k][d])
                def _(d=d, k=k):
                    for f in range(2):
                        for j in range(self.p.m):
                            self.pcopy(f, k, d, j, self.mine).wait_send()
                    if k + 1 < self.p.nz - 1:

                        @pl.when(self.more[k][d])
                        def _():
                            for f in range(2):
                                self.zcopy(f, k + 1, d, self.origin[k][d]).wait_send()


def parts_of(t):
    return t // 144 if t % 144 == 0 else 1


class RowsIn:
    def __init__(self, pl_, src, dst, ssem, rsem, lsem, base):
        self.p, self.src, self.dst, self.sems, self.base = pl_, src, dst, (ssem, rsem, lsem), base
        self.t, self.ew = dst.shape[0], src.shape[1]
        self.parts = parts_of(self.t)
        self.n = self.t // self.parts

    def copy(self, r, d, dev, col):
        i = (self.base * (self.p.nz - 1) + d) * self.parts + r
        return rcopy(
            self.src.at[pl.ds(pl.multiple_of(dev[1] * self.t + r * self.n, 16), self.n), :],
            self.dst.at[pl.ds(r * self.n, self.n), pl.ds(pl.multiple_of(col * self.ew, 128), self.ew)],
            self.sems[0].at[i],
            self.sems[1].at[i],
            dev,
        )

    def own(self):
        h = self.p.h
        return pltpu.make_async_copy(
            self.src.at[pl.ds(pl.multiple_of(h * self.t, 16), self.t), :],
            self.dst.at[:, pl.ds(pl.multiple_of(h * self.ew, 128), self.ew)],
            self.sems[2].at[self.base],
        )

    def begin(self, lo, hi):
        for r in range(lo, min(hi, self.parts)):
            if r == 0:
                self.own().start()
            for d, dev in enumerate(self.p.zdev):
                self.copy(r, d, dev, self.p.h).start()

    def finish(self):
        for r in range(self.parts):
            for d, frm in enumerate(self.p.zfrom):
                self.copy(r, d, frm, frm[1]).wait_recv()
        self.own().wait()

    def drain(self):
        for r in range(self.parts):
            for d, dev in enumerate(self.p.zdev):
                self.copy(r, d, dev, self.p.h).wait_send()


class Items:
    def __init__(self, p, lengths, t, nb):
        ns, nz, s, h = p.ns, p.nz, p.s, p.h
        ends, total = [], 0
        for i in range(lengths.shape[0]):
            total = total + lengths[i]
            ends.append(total)

        def item(pos):
            out = 0
            for e in ends:
                out = out + jnp.where(pos >= e, 1, 0)
            return out

        rows = nz * t
        first = s * rows
        me = first + h * t
        blk = t // nb

        def same(a, b):
            return jnp.where(a == b, 1.0, 0.0)

        line = [jnp.where(s == 0, -1, item(first - 1))] + [item(first + (z + 1) * t - 1) for z in range(nz)]
        before, last = line[:nz], line[1:]
        lines = [-1] + [item((k + 1) * rows - 1) for k in range(ns)]
        seq = [jnp.where(me == 0, -1, item(me - 1))] + [item(me + n * blk) for n in range(nb)]
        self.keep = [same(seq[n + 1], seq[n]) for n in range(nb)]
        zs, ks = range(nz), range(ns)
        zero = jnp.float32(0.0)
        self.fore = (
            [same(last[z], last[nz - 1]) for z in zs],
            [[jnp.where(k < s, same(lines[k + 1], before[z]), 0.0) for k in ks] for z in zs],
            [[same(last[k], before[z]) if k < z else zero for k in zs] for z in zs],
        )
        self.back = (
            [same(before[z], before[0]) for z in zs],
            [[jnp.where(k > s, same(lines[k], last[z]), 0.0) for k in ks] for z in zs],
            [[same(before[k], last[z]) if k > z else zero for k in zs] for z in zs],
        )


class Scan:
    def __init__(self, pl_, w, msg, r1, r2, tot, outb, got, sems):
        self.p, self.w, self.msg, self.r1, self.r2 = pl_, w, msg, r1, r2
        self.tot, self.outb, self.got, self.sems = tot, outb, got, sems

    def c1(self, d, dev, slot):
        return rcopy(self.msg.at[dev[1]], self.r1.at[slot], self.sems[0].at[d], self.sems[1].at[d], dev)

    def c2(self, d, dev, slot):
        return rcopy(self.tot, self.r2.at[slot], self.sems[2].at[d], self.sems[3].at[d], dev)

    def c3(self, d, dev, slot):
        return rcopy(self.outb.at[dev[1]], self.got.at[slot], self.sems[4].at[d], self.sems[5].at[d], dev)

    def phase1(self):
        for d, dev in enumerate(self.p.zdev):
            self.c1(d, dev, self.p.h).start()
        self.r1[self.p.h] = self.msg[self.p.h]

    def phase2(self):
        for d, frm in enumerate(self.p.zfrom):
            self.c1(d, frm, frm[1]).wait_recv()
        wt = self.w[0]
        self.tot[...] = sum(wt[z] * self.r1[z].astype(F32) for z in range(self.p.nz)).astype(BF)
        for d, dev in enumerate(self.p.sdev):
            self.c2(d, dev, self.p.s).start()
        self.r2[self.p.s] = self.tot[...]

    def phase3(self):
        for d, dev in enumerate(self.p.sdev):
            self.c2(d, dev, dev[0]).wait_recv()
        _, wp, wl = self.w
        for z in range(self.p.nz):
            v = sum(wl[z][k] * self.r1[k].astype(F32) for k in range(self.p.nz))
            v = v + sum(wp[z][k] * self.r2[k].astype(F32) for k in range(self.p.ns))
            self.outb[z] = v.astype(BF)
        for d, dev in enumerate(self.p.zdev):
            self.c3(d, dev, self.p.h).start()
        self.got[self.p.h] = self.outb[self.p.h]

    def finish(self):
        for d, frm in enumerate(self.p.zfrom):
            self.c3(d, frm, frm[1]).wait_recv()

    def drain(self):
        for d, dev in enumerate(self.p.zdev):
            self.c1(d, dev, self.p.h).wait_send()
            self.c3(d, dev, self.p.h).wait_send()
        for d, dev in enumerate(self.p.sdev):
            self.c2(d, dev, self.p.s).wait_send()


ZROWS = 16
MSG = HD + ZROWS


def msg_rows(p, pg):
    return p // pg, pl.ds(pl.multiple_of(lax.rem(p, pg) * MSG, 16), MSG)


def is_own(shape=(128, 128)):
    return row_low(shape) == lane_low(shape)


def pack_state(sa, lanes):
    own = is_own()
    state = jnp.where(lane_low((HD, 128)), sa[:HD], sa[HD:])
    z = jnp.where(own, 0.0, sa)
    hi = z.astype(BF)
    lo = (z - hi.astype(F32)).astype(BF)
    lane = lax.broadcasted_iota(jnp.int32, (ZROWS, 128), 1)
    row = lax.broadcasted_iota(jnp.int32, (ZROWS, 128), 0)
    sel = jnp.where((lane % HD) < lanes, 1.0, 0.0).astype(BF)
    zr = jnp.where(row == 0, dot_t(sel, hi), jnp.where(row == 1, dot_t(sel, lo), 0.0))
    return jnp.concatenate([state, zr], axis=0).astype(BF)


def unpack_state(msg, every):
    st = msg[:HD].astype(F32)
    z = t_dot(msg[HD:], jnp.ones((ZROWS, 128), BF))
    if not every:
        lane = lax.broadcasted_iota(jnp.int32, (128, 128), 1)
        z = jnp.where(lane % HD == 0, z, 0.0)
    return jnp.where(is_own(), jnp.concatenate([st, st], axis=0), z)


def state_part(p, n, blk, fq, st):
    rows = pl.ds(n * blk, blk)
    r = dot(fq[rows, cols(p, 128)], split_state(st))
    low = lane_low((blk, 128))
    num = jnp.where(low, r[:, :128], r[:, 128:])
    den = pltpu.roll(jnp.where(low, r[:, 128:], r[:, :128]), HD, 1)
    return num, den


FORE_ORDER = [
    ("Wb",), ("X", 2), ("W", 0, 0), ("Wf", 0), ("Vb",), ("W", 0, 1), ("Ub",), ("W", 1, 0), ("X", 3), ("Wf", 1),
    ("X", 1), ("V", 0, 0), ("X", 0), ("W", 1, 1), ("W", 2, 0), ("V", 0, 1), ("W", 0, 2), ("U", 0, 0), ("W", 2, 1),
    ("W", 1, 2), ("Vf", 0), ("ln1",), ("C", 0), ("W", 1, 3), ("Uf", 0), ("C", 2), ("V", 1, 0), ("pj", 0),
    ("W", 0, 3), ("pj", 1), ("Vf", 1), ("W", 2, 2), ("U", 0, 1), ("pj", 2), ("V", 1, 1), ("sums", 2), ("W", 2, 3),
    ("V", 0, 2), ("sums", 1), ("pj", 3), ("loc", 1), ("sums", 3), ("U", 1, 0), ("sums", 0), ("s1",), ("s2",),
    ("Uf", 1), ("C", 1), ("keep",), ("loc", 3), ("V", 1, 2), ("U", 1, 1), ("loc", 2), ("V", 2, 0), ("s3",),
    ("U", 2, 0), ("loc", 0), ("U", 1, 2), ("U", 0, 2), ("C", 3), ("sf",), ("state", 2), ("state", 0), ("state", 1),
    ("state", 3), ("U", 2, 1), ("Vf", 2), ("mid",), ("prep",), ("V", 1, 3), ("Uf", 2), ("F", 0), ("V", 0, 3),
    ("U", 2, 2), ("U", 1, 3), ("V", 2, 1), ("U", 0, 3), ("F", 1), ("F", 2), ("U", 2, 3), ("F", 3), ("Wf", 2),
    ("V", 2, 2), ("F", 4), ("F", 5), ("V", 2, 3), ("F", 6), ("F", 7),
]
AFT_ORDER = [
    ("S", 0, 1), ("lnb2",), ("datt",), ("S", 1, 1), ("lo", 3), ("t", 0), ("t", 1), ("S", 0, 2), ("t", 3),
    ("S", 6, 1), ("t", 2), ("s1",), ("S", 1, 2), ("q", 0), ("s2",), ("S", 7, 1), ("S", 6, 2), ("lo", 2), ("s3",),
    ("dmt",), ("q", 1), ("lo", 1), ("S", 4, 1), ("S", 7, 2), ("a1",), ("sf",), ("S", 0, 3), ("k", 1), ("S", 2, 1),
    ("q", 3), ("S", 1, 3), ("lo", 0), ("k", 3), ("q", 2), ("S", 5, 1), ("S", 7, 3), ("S", 3, 1), ("S", 6, 3),
    ("k", 0), ("k", 2), ("g", 0), ("o", 0), ("S", 0, 4), ("S", 1, 4), ("S", 4, 2), ("o", 2), ("g", 2), ("A", 0, 0),
    ("S", 5, 2), ("S", 2, 2), ("g", 1), ("S", 6, 4), ("g", 3), ("S", 7, 4), ("S", 3, 2), ("A", 2, 0), ("o", 3),
    ("S", 4, 3), ("S", 5, 3), ("d", 0), ("o", 1), ("d", 1), ("A", 3, 0), ("A", 2, 1), ("S", 4, 4), ("A", 1, 0),
    ("S", 5, 4), ("d", 2), ("S", 2, 3), ("A", 0, 1), ("S", 2, 4), ("A", 3, 1), ("d", 3), ("lnb1",), ("gt", 1),
    ("gt", 3), ("A", 1, 1), ("S", 3, 3), ("A", 0, 2), ("gt", 0), ("A", 1, 2), ("gt", 2), ("A", 0, 3), ("S", 5, 5),
    ("A", 2, 2), ("m", 0), ("S", 3, 4), ("A", 0, 4), ("S", 7, 5), ("S", 2, 5), ("S", 0, 5), ("A", 3, 2), ("S", 3, 5),
    ("S", 1, 5), ("S", 6, 5), ("A", 1, 3), ("A", 2, 3), ("m", 1), ("A", 3, 3), ("A", 1, 4), ("A", 2, 4), ("m", 2),
    ("m", 3), ("A", 3, 4), ("A", 3, 5), ("A", 0, 5), ("S", 4, 5), ("A", 2, 5), ("A", 1, 5), ("m", 4),
]


def fore_plan(nz, m, per, parts):
    if (nz, m, per, parts) == (4, 3, 2, 4):
        return FORE_ORDER
    far = nz - 1
    out = [("Wb",), ("X", 0)]
    ws = sorted((2 * k + st, k, st) for k in range(far) for st in range(m + 1))
    cut = 2 * (far - 1)
    x = 1
    for w, k, st in ws:
        if w <= cut:
            out.append(("W", k, st))
            if st == 0:
                out.append(("Wf", k))
                upto = parts if k + 2 >= far else min(parts, x + 1)
                out += [("X", r) for r in range(x, upto)]
                x = max(x, upto)
    out += [("Ub",), ("Vb",), ("ln1",), ("pj", 0)]
    out += [("sums", 0), ("loc", 0)]
    for w, k, st in ws:
        if w <= cut and st == m:
            out += [("pj", k + 1), ("sums", k + 1)]
    for w, k, st in ws:
        if w > cut:
            out.append(("W", k, st))
            if st == m:
                out += [("pj", k + 1), ("sums", k + 1)]
    out += [("s1",), ("keep",), ("C", 0), ("U", 0, 0), ("V", 0, 0)] + [("loc", i) for i in range(1, nz - 1)]
    out += [("s2",), ("U", 0, 1), ("V", 0, 1), ("loc", nz - 1), ("s3",)] + [("C", r) for r in range(1, parts)]
    out += [("Uf", 0), ("Vf", 0), ("U", 0, 2), ("V", 0, 2), ("sf",)] + [("state", i) for i in range(nz)]
    out += [(a, 0, st) for st in range(3, m + 1) for a in "UV"] + [("mid",), ("prep",)]
    for j in range(nz * per):
        for k in range(1, far):
            for st in range(m + 1):
                if max(0, (k + 1) * per - (m - st)) == j:
                    out += [("U", k, st), ("V", k, st)]
                    if st == 0:
                        out += [("Uf", k), ("Vf", k)]
        out.append(("F", j))
    return out


def fore_kernel(ns, nz, nb, *refs):
    lengths, tok, cot, wq, wo, wu, wd, gains, biases, pads = refs[:10]
    xo, coo, fqo, fko, vbo, atto, rdeno, stateso, mido, w4o, lo, da2o, gu, gd = refs[10:24]
    (xv, cov, av, fq, fk, vb, att, a2t, ct, rden, mid, acc, da2, inc, states,
     w4v, wuv, wdv, gub, gdb, msg, r1, r2, tot, outb, got,
     lsem, tsend, trecv, zsend, zrecv, psend, precv, wsem, ysem, osem,
     c1s, c1r, c2s, c2r, c3s, c3r, pad, wov) = refs[24:]
    P_ = Places(ns, nz)
    t, d = xv.shape
    blk = t // nb
    ew = wq.shape[2]
    ff = wu.shape[2]
    h = P_.h
    m = P_.m
    np_ = d // 128
    pg = msg.shape[1] // MSG
    order = group_order(nz)
    gidx = [pick_group(order, h, i) for i in range(nz)]
    W = Gather(P_, w4v, zsend, zrecv, psend, precv, 0)
    U = Gather(P_, wuv, zsend, zrecv, psend, precv, 1)
    V = Gather(P_, wdv, zsend, zrecv, psend, precv, 2)
    X = RowsIn(P_, tok, xv, tsend, trecv, lsem, 0)
    C = RowsIn(P_, cot, cov, tsend, trecv, lsem, 1)
    greet(P_.zdev + P_.sdev)
    items = Items(P_, lengths, t, nb)
    cflag = items.keep
    scan = Scan(P_, items.fore, msg, r1, r2, tot, outb, got, (c1s, c1r, c2s, c2r, c3s, c3r))
    own = [
        pltpu.make_async_copy(wq, w4v.at[h, 0:3], wsem.at[0]),
        pltpu.make_async_copy(wo, wov, wsem.at[1]),
        pltpu.make_async_copy(wu, wuv.at[h], wsem.at[2]),
        pltpu.make_async_copy(wd, wdv.at[h], wsem.at[3]),
    ]
    for cp in own:
        cp.start()
    outs = []

    def keep(src, dst):
        cp = pltpu.make_async_copy(src, dst, ysem.at[len(outs)])
        outs.append(cp)
        cp.start()

    far = nz - 1
    tile = gub.shape[2]
    per = ff // tile
    steps = nz * per

    def sums_of(p):
        chunk_sums(p, blk, nb, fk, vb, inc)
        cur = inc[0, p]
        for n in range(1, nb):
            cur = cflag[n] * cur + inc[n, p]
        g, rr = msg_rows(p, pg)
        msg[g, rr, :] = pack_state(cur, 1)

    def local_of(p):
        for n in range(nb):
            rows = pl.ds(n * blk, blk)
            c = cols(p, 128)
            q2, k2, v2 = fq[rows, c], fk[rows, c], vb[rows, c]
            s0, s1 = masked_scores(q2, k2, causal_mask(blk))
            g0, g1 = with_ones(v2)
            x0, x1 = dot(s0, g0), dot(s1, g1)
            low = lane_low(x0.shape)
            acc[rows, c] = jnp.where(low, x0, x1)
            rden[rows, c] = pltpu.roll(jnp.where(low, x1, x0), HD, 1)

    def state_of(p):
        g, rr = msg_rows(p, pg)
        cur = unpack_state(got[g, rr, :], True)
        for n in range(nb):
            rows = pl.ds(n * blk, blk)
            c = cols(p, 128)
            used = cflag[n] * cur
            st = used.astype(BF)
            states[n, p] = st
            cur = used + inc[n, p]
            num, den = state_part(p, n, blk, fq, st)
            rd = 1.0 / (1.0 + rden[rows, c] + den)
            att[rows, c] = ((acc[rows, c] + num) * rd).astype(BF)
            rden[rows, c] = rd

    def do_ln1():
        one_row = lax.broadcasted_iota(jnp.int32, pads.shape, 0) == h
        pad[...] = t_dot(jnp.where(one_row, pads[...], 0).astype(F32).astype(BF), jnp.ones((nz, 128), BF))
        X.finish()
        norm_forward(xv, gains.at[0:1], biases.at[0:1], av)
        keep(xv, xo)

    def do_project(i):
        project(av, w4v, gidx[i], pad, fq, fk, vb)

    def do_sums(i):
        loop_pairs(pg, lambda p: sums_of(p + gidx[i] * pg))

    def do_keep():
        keep(w4v, w4o)
        keep(fq, fqo)
        keep(fk, fko)
        keep(vb, vbo)

    def do_local(i):
        loop_pairs(pg, lambda p: local_of(p + gidx[i] * pg))

    def do_state(i):
        loop_pairs(pg, lambda p: state_of(p + i * pg))

    def do_mid():
        keep(att, atto)
        keep(rden, rdeno)
        keep(states, stateso)
        mid[...] = xv[...].astype(F32)
        for g in range(nz):
            mid[...] += dot_t(att[:, g * ew : (g + 1) * ew], w4v[g, 3])
        norm_forward(mid, gains.at[1:2], biases.at[1:2], av)
        keep(mid, mido)
        transpose_perm(ns, av, a2t)

    def do_prep():
        C.finish()
        keep(cov, coo)
        transpose_perm(ns, cov, ct)
        acc[...] = mid[...]
        da2[...] = jnp.zeros_like(da2)

    def begin_own(i, a):
        own[i].wait()
        a.begin()

    def place(i):
        g = pick_group(order, h, i // per)
        return g, pl.ds(pl.multiple_of(lax.rem(i, per) * tile, 128), tile)

    def flush(i, slot):
        g, c = place(i)
        return (
            pltpu.make_async_copy(gub.at[slot], gu.at[g, :, c], osem.at[slot, 0]),
            pltpu.make_async_copy(gdb.at[slot], gd.at[g, :, c], osem.at[slot, 1]),
        )

    todo = {
        "X": lambda r: X.begin(r, r + 1),
        "C": lambda r: C.begin(r, r + 1),
        "W": W.advance,
        "U": U.advance,
        "V": V.advance,
        "Wb": W.begin,
        "Ub": lambda: begin_own(2, U),
        "Vb": lambda: begin_own(3, V),
        "Wf": W.forward,
        "Uf": U.forward,
        "Vf": V.forward,
        "s1": scan.phase1,
        "s2": scan.phase2,
        "s3": scan.phase3,
        "sf": scan.finish,
        "ln1": do_ln1,
        "pj": do_project,
        "sums": do_sums,
        "keep": do_keep,
        "loc": do_local,
        "state": do_state,
        "mid": do_mid,
        "prep": do_prep,
    }
    plan = fore_plan(nz, m, per, X.parts)
    cuts = [[]]
    for tok_ in plan:
        if tok_[0] == "F":
            cuts.append([])
        else:
            cuts[-1].append(tok_)

    def run(tokens):
        for tok_ in tokens:
            todo[tok_[0]](*tok_[1:])

    own[1].wait()
    for j in range(d // 256):
        w4v[h, 3, j * 256 : (j + 1) * 256, :] = wov[:, j * 256 : (j + 1) * 256].T
    own[0].wait()
    greeted(P_.zdev + P_.sdev)
    run(cuts[0])

    def step(i, _):
        slot = lax.rem(i, 2)
        for j in range(1, steps):
            if cuts[j]:
                pl.when(i == j)(functools.partial(run, cuts[j]))

        @pl.when(i >= 2)
        def _():
            for cp in flush(i - 2, slot):
                cp.wait()

        g, c = place(i)
        wub, wdb = wuv[g, 0, :, c], wdv[g, 0, c, :]
        up = dot(av[...], wub)
        hidf, slope = gelu_parts(up)
        hid = hidf.astype(BF)
        acc[...] += dot(hid, wdb)
        gdb[slot] = dot(ct[...], hid).astype(BF)
        dup = (slope * dot_t(cov[...], wdb)).astype(BF)
        da2[...] += dot_t(dup, wub)
        gub[slot] = dot(a2t[...], dup).astype(BF)
        for cp in flush(i, slot):
            cp.start()
        return 0

    lax.fori_loop(0, steps, step, 0)
    run(cuts[steps])
    keep(da2, da2o)
    av[...] = acc[...].astype(BF)
    keep(av, lo)
    for i in range(max(0, steps - 2), steps):
        for cp in flush(i, i % 2):
            cp.wait()
    for cp in outs:
        cp.wait()
    X.drain()
    C.drain()
    scan.drain()
    for a in (W, U, V):
        a.drain()


def fore(ns, nz, nb, lengths, tok, cot, wq, wo, wu, wd, gains, biases, pad):
    t, d = tok.shape[0] // nz, wq.shape[1]
    ew, ff = wq.shape[2], wu.shape[2]
    np_ = d // 128
    m = ns.bit_length() - 1
    dma = pltpu.SemaphoreType.DMA
    vm = pltpu.VMEM
    tile = 512 if ff % 512 == 0 else ff
    one = ((ew // 128) * MSG, 128)
    nzs = 3 * 2 * (nz - 1) * 2
    td, tdf = ((t, d), BF), ((t, d), F32)
    outs = [td, td, td, td, td, td, tdf, ((nb, np_, 128, 128), BF), tdf, ((nz, 4, d, ew), BF), td, tdf,
            ((nz, d, ff), BF), ((nz, d, ff), BF)]
    args = (lengths, tok, cot, wq, wo, wu, wd, gains, biases, pad)
    return pl.pallas_call(
        functools.partial(fore_kernel, ns, nz, nb),
        out_shape=tuple(jax.ShapeDtypeStruct(s, dt) for s, dt in outs),
        in_specs=[smem_spec()] + [any_spec()] * 6 + [vmem_spec()] * 3,
        out_specs=(any_spec(),) * len(outs),
        scratch_shapes=[vm((t, d), BF)] * 7
        + [vm((d, t), BF)] * 2
        + [vm((t, d), F32)] * 4
        + [
            vm((nb, np_, 128, 128), F32),
            vm((nb, np_, 128, 128), BF),
            vm((nz, 4, d, ew), BF),
            vm((nz, 1, d, ff), BF),
            vm((nz, 1, ff, d), BF),
            vm((2, d, tile), BF),
            vm((2, d, tile), BF),
            vm((nz,) + one, BF),
            vm((nz,) + one, BF),
            vm((ns,) + one, BF),
            vm(one, BF),
            vm((nz,) + one, BF),
            vm((nz,) + one, BF),
            dma((2,)),
            dma((2 * (nz - 1) * parts_of(t),)),
            dma((2 * (nz - 1) * parts_of(t),)),
            dma((nzs,)),
            dma((nzs,)),
            dma((nzs * m,)),
            dma((nzs * m,)),
            dma((4,)),
            dma((16,)),
            dma((2, 2)),
        ]
        + [dma((nz - 1,)), dma((nz - 1,)), dma((ns - 1,)), dma((ns - 1,)), dma((nz - 1,)), dma((nz - 1,))]
        + [vm((t, 128), F32), vm((ew, d), BF)],
        name="fore",
        compiler_params=pltpu.CompilerParams(collective_id=0, has_side_effects=True, vmem_limit_bytes=62 * 2**20),
    )(*args)


def add_block(dst, dlead, dstart, src, slead, n):
    blk = min(n, 64)

    def step(i, _):
        a = dst[dlead + (pl.ds(pl.multiple_of(dstart + i * blk, 16), blk), slice(None))]
        b = src[slead + (pl.ds(pl.multiple_of(i * blk, 16), blk), slice(None))]
        dst[dlead + (pl.ds(pl.multiple_of(dstart + i * blk, 16), blk), slice(None))] = (
            a.astype(F32) + b.astype(F32)
        ).astype(BF)
        return 0

    lax.fori_loop(0, n // blk, step, 0)


class Reduce:
    def __init__(self, p, idx, tz, acc, lead, src, own, rec, zbuf, zslot, zx, xslot, sems, out):
        self.p, self.idx, self.tz = p, idx, tz
        self.acc, self.lead, self.src, self.own, self.rec = acc, lead, src, own, rec
        self.zbuf, self.zslot, self.zx, self.xslot, self.out = zbuf, zslot, zx, xslot, out
        self.cs, self.cr, self.zs, self.zr, self.ls = sems
        orders = ([0] + p.o0, [0] + p.o1)
        self.orders = orders
        self.units = rec[0].shape[2] * 2 // p.ns
        self.bit = [[(p.s >> orders[f][j]) & 1 for j in range(p.m)] for f in range(2)]
        self.pos = []
        for f in range(2):
            pos, seq = 0, []
            for j in range(1, p.m):
                seq.append(pos)
                pos = pos + self.bit[f][j] * self.size(j)
            self.pos.append(seq + [pos])

    def size(self, j):
        return self.units * (self.p.ns >> (j + 1))

    def step(self, f, j):
        i = (self.idx * self.p.m + j) * 2 + f
        b = self.bit[f][j]
        n = self.size(j)
        if j == 0:
            src = self.src(f, 1 - b)
        else:
            at = self.pos[f][j - 1] + (1 - b) * n
            src = self.acc.at[self.lead(f) + (pl.ds(pl.multiple_of(at, 16), n), slice(None))]
        dst = self.rec[j].at[self.rslot(j), f]
        return rcopy(src, dst, self.cs.at[i], self.cr.at[i], self.p.bit[self.orders[f][j]])

    def rslot(self, j):
        return self.idx

    def load(self, f):
        return pltpu.make_async_copy(
            self.src(f, self.bit[f][0]), self.acc.at[self.lead(f)], self.ls.at[self.idx * 2 + f]
        )

    def route(self, hh):
        nz, tz = self.p.nz, self.tz
        q, count, inward = (hh, tz, 1) if hh < tz else (nz - 1 - hh, nz - 1 - tz, -1)
        if q % 2 == 0 and q + 1 < count:
            return False, hh + inward, 0
        return q % 2 == 1, tz, q // 2 + (0 if hh < tz else (tz + 1) // 2)

    def landing(self, f, slot):
        return self.zbuf.at[self.zslot, f] if slot == 0 else self.zx.at[self.xslot, slot - 1, f]

    def zcopy(self, f, to, slot):
        i = self.idx * 2 + f
        mine = self.acc.at[self.lead(f) + (pl.ds(pl.multiple_of(self.pos[f][-1], 16), self.units), slice(None))]
        r = (self.idx * (self.p.nz // 2) + slot) * 2 + f
        return rcopy(mine, self.landing(f, slot), self.zs.at[i], self.zr.at[r], (self.p.s, to))

    def advance(self, st):
        m, tz, nz = self.p.m, self.tz, self.p.nz
        if st <= m:
            for f in range(2):
                if st > 0:
                    self.step(f, st - 1).wait_recv()
                    if st == 1 and self.own:
                        self.load(f).wait()
                    add_block(self.acc, self.lead(f), self.pos[f][st - 1], self.rec[st - 1], (self.rslot(st - 1), f), self.size(st - 1))
                elif self.own:
                    self.load(f).start()
                if st < m:
                    self.step(f, st).start()
        if st == m or st == m + 1:
            for hh in range(nz):
                inner, to, slot = self.route(hh) if hh != tz else (None, 0, 0)
                if inner is None or inner != (st == m + 1):
                    continue

                @pl.when(self.p.h == hh)
                def _(inner=inner, to=to, slot=slot):
                    for f in range(2):
                        if inner:
                            self.zcopy(f, to, 0).wait_recv()
                            add_block(self.acc, self.lead(f), self.pos[f][-1], self.zbuf, (self.zslot, f), self.units)
                        self.zcopy(f, to, slot).start()

        if st == m + 2:

            @pl.when(self.p.h == tz)
            def _():
                both = []
                for f in range(2):
                    v = self.acc[self.lead(f) + (pl.ds(pl.multiple_of(self.pos[f][-1], 16), self.units), slice(None))]
                    v = v.astype(F32)
                    for slot in range((tz + 1) // 2 + (nz - tz) // 2):
                        self.zcopy(f, tz, slot).wait_recv()
                        ref = self.landing(f, slot)
                        v = v + ref[...].astype(F32)
                    both.append(v)
                self.out(jnp.concatenate(both, axis=0))

    def drain(self):
        for f in range(2):
            for j in range(self.p.m):
                self.step(f, j).wait_send()

        @pl.when(self.p.h != self.tz)
        def _():
            for f in range(2):
                self.zcopy(f, 0, 0).wait_send()


class RowsOut:
    def __init__(self, pl_, src, dst, ssem, rsem, lsem, base):
        self.p, self.src, self.dst, self.sems, self.base = pl_, src, dst, (ssem, rsem, lsem), base
        self.t, self.ew = src.shape[0], dst.shape[1]
        self.parts = parts_of(self.t)
        self.n = self.t // self.parts

    def copy(self, r, d, dev, row):
        i = (self.base * (self.p.nz - 1) + d) * self.parts + r
        return rcopy(
            self.src.at[pl.ds(r * self.n, self.n), pl.ds(pl.multiple_of(dev[1] * self.ew, 128), self.ew)],
            self.dst.at[pl.ds(pl.multiple_of(row * self.t + r * self.n, 16), self.n), :],
            self.sems[0].at[i],
            self.sems[1].at[i],
            dev,
        )

    def own(self):
        h = self.p.h
        return pltpu.make_async_copy(
            self.src.at[:, pl.ds(pl.multiple_of(h * self.ew, 128), self.ew)],
            self.dst.at[pl.ds(pl.multiple_of(h * self.t, 16), self.t), :],
            self.sems[2].at[self.base],
        )

    def begin(self, lo, hi):
        for r in range(lo, min(hi, self.parts)):
            if r == 0:
                self.own().start()
            for d, dev in enumerate(self.p.zdev):
                self.copy(r, d, dev, self.p.h).start()

    def finish(self):
        for r in range(self.parts):
            for d, frm in enumerate(self.p.zfrom):
                self.copy(r, d, frm, frm[1]).wait_recv()
            for d, dev in enumerate(self.p.zdev):
                self.copy(r, d, dev, self.p.h).wait_send()
        self.own().wait()


class Small:
    def __init__(self, pl_, cur, rec, gz, ssem, rsem, out):
        self.p, self.cur, self.rec, self.gz, self.sems, self.out = pl_, cur, rec, gz, (ssem, rsem), out

    def hop(self, j):
        return rcopy(self.cur.at[j], self.rec.at[j], self.sems[0].at[j], self.sems[1].at[j], self.p.bit[j])

    def zhop(self, d, dev, slot):
        i = self.p.m + d
        return rcopy(self.cur.at[self.p.m], self.gz.at[slot], self.sems[0].at[i], self.sems[1].at[i], dev)

    def advance(self, st):
        m = self.p.m
        if 0 < st <= m:
            self.hop(st - 1).wait_recv()
            self.cur[st] = self.cur[st - 1] + self.rec[st - 1]
        if st < m:
            self.hop(st).start()
        if st == m:
            for d, dev in enumerate(self.p.zdev):
                self.zhop(d, dev, self.p.h).start()
            self.gz[self.p.h] = self.cur[m]
        if st == m + 1:
            for d, frm in enumerate(self.p.zfrom):
                self.zhop(d, frm, frm[1]).wait_recv()
            total = self.gz[0]
            for z in range(1, self.p.nz):
                total = total + self.gz[z]
            self.out[...] = total
            for j in range(m):
                self.hop(j).wait_send()
            for d, dev in enumerate(self.p.zdev):
                self.zhop(d, dev, self.p.h).wait_send()


def back_queries(p, n, blk, fk, vb, fq, dr0, dr1, st, dq):
    rows = pl.ds(n * blk, blk)
    c = cols(p, 128)
    q2, k2, v2, e0, e1 = fq[rows, c], fk[rows, c], vb[rows, c], dr0[rows, c], dr1[rows, c]
    g0, g1 = with_ones(v2)
    keep = causal_mask(blk)
    ds0 = jnp.where(keep, dot_t(e0, g0), 0.0).astype(BF)
    ds1 = jnp.where(keep, dot_t(e1, g1), 0.0).astype(BF)
    dfq = jnp.where(lane_low(q2.shape), dot(ds0, k2), dot(ds1, k2))
    dfq = dfq + dot_t(jnp.concatenate([e0, e1], axis=1), split_state(st))
    dq[rows, c] = (dfq * jnp.minimum(q2.astype(F32), 1.0)).astype(BF)


def back_keys(p, n, blk, fk, vb, fq, dr0, dr1, dst):
    rows = pl.ds(n * blk, blk)
    c = cols(p, 128)
    q2, k2, v2, e0, e1 = fq[rows, c], fk[rows, c], vb[rows, c], dr0[rows, c], dr1[rows, c]
    g0, g1 = with_ones(v2)
    keep_t = lax.broadcasted_iota(jnp.int32, (blk, blk), 0) <= lax.broadcasted_iota(jnp.int32, (blk, blk), 1)
    low = lane_low(q2.shape)
    dt0 = jnp.where(keep_t, dot_t(g0, e0), 0.0).astype(BF)
    dt1 = jnp.where(keep_t, dot_t(g1, e1), 0.0).astype(BF)
    dfk = jnp.where(low, dot(dt0, q2), dot(dt1, q2))
    dfk = dfk + dot_t(jnp.concatenate([g0, g1], axis=1), split_state(dst))
    st0, st1 = masked_scores(k2, q2, keep_t)
    own = jnp.where(row_low((128, 128)) == lane_low((128, 128)), dst, jnp.zeros_like(dst))
    dvv = jnp.where(low, dot(st0, e0), dot(st1, e1)) + dot(k2, own)
    fk[rows, c] = (dfk * jnp.minimum(k2.astype(F32), 1.0)).astype(BF)
    vb[rows, c] = dvv.astype(BF)


def aft_plan(nz, m, parts, quads):
    if (nz, m, parts, quads) == (4, 3, 4, 4):
        return AFT_ORDER
    n, last = 2 * nz, m + 2
    half = nz
    gaps = [half + 0.5] * (m - 1) + [3, 3]
    at = [sum(gaps[:st]) for st in range(last)]
    ffn = [("S", i, st) for _, i, st in sorted((i + at[st - 1], i, st) for i in range(n) for st in range(1, last + 1))]
    heads = 1 + max(j for j, x in enumerate(ffn) if x[2] == 1)
    out = []
    state = {"j": 0}

    def tick(k):
        out.extend(ffn[state["j"] : state["j"] + k])
        state["j"] = min(len(ffn), state["j"] + k)

    out += [("lo", r) for r in range(parts - 1)] + [("lnb2",)]
    tick(half - 2)
    out.append(("datt",))
    tick(1)
    for i in range(quads):
        out.append(("t", i))
        if i == 1:
            tick(1)
    out += [("s1",), ("lo", parts - 1), ("dmt",), ("s2",)]
    tick(3)
    for i in range(quads):
        out.append(("q", i))
        if i == min(1, quads - 1):
            tick(max(0, heads - state["j"]))
            out.append(("s3",))
        else:
            tick(1)
    out.append(("a1",))
    out += [("o", i) for i in range(nz)] + [("sf",)]
    for i in range(quads):
        out.append(("k", i))
        tick(1)
    attn = {w: [("A", i, w - i) for i in range(nz) if 0 <= w - i <= last] for w in range(nz + last)}
    for i in range(nz):
        out.append(("g", i))
        out += attn[i]
        out.append(("d", i))
        tick(1)
    out.append(("lnb1",))
    out += [("gt", r) for r in range(parts)]
    tick(len(ffn))
    for w in range(nz, nz + last):
        if w - nz <= m + 1:
            out.append(("m", w - nz))
        out += attn[w]
    out += [("m", st) for st in range(last, m + 2)]
    return out


def aft_kernel(ns, nz, nb, *refs):
    lengths, x, co, fqi, fki, vbi, atti, rdeni, statesi, midi, w4, lo, da2i, gu, gd, gains, biases = refs[:17]
    lo_o, gt_o, gbo, oq, oo, ou, od = refs[17:24]
    (fq, fk, vb, dr0, dr1, att, dml, dq, a1t, dmt, datt, mid, dmid, rden, ginc, states, ring, sums2, sums1,
     pool, rec0, *more) = refs[24:]
    m = ns.bit_length() - 1
    rec = [rec0] + list(more[: m - 1])
    (zbuf, zx, msg, r1, r2, tot, outb, got, gcur, grec, gz,
     lsem, rsem, asem, tsend, trecv, tl, csend, crecv, zsend, zrecv, gsend, grecv,
     c1s, c1r, c2s, c2r, c3s, c3r) = more[m - 1 :]
    P_ = Places(ns, nz)
    t, d = fq.shape
    blk = t // nb
    ew = lo_o.shape[1]
    np_ = d // 128
    pg = msg.shape[1] // MSG
    quarter = d // 4
    greet(P_.zdev + P_.sdev)
    items = Items(P_, lengths, t, nb)
    cflag = items.keep
    scan = Scan(P_, items.back, msg, r1, r2, tot, outb, got, (c1s, c1r, c2s, c2r, c3s, c3r))
    lo_a = RowsOut(P_, lo, lo_o, tsend, trecv, tl, 0)
    gt_a = RowsOut(P_, dml, gt_o, tsend, trecv, tl, 1)
    small = Small(P_, gcur, grec, gz, gsend, grecv, gbo)
    sems = (csend, crecv, zsend, zrecv, asem)
    ends_first = [z for pair in zip(range(nz // 2), range(nz - 1, nz // 2 - 1, -1)) for z in pair]
    ffn, attn = [], []

    def out_down(v):
        od[...] = v.T.astype(BF)

    def out_up(v):
        ou[...] = v.astype(BF)

    def out_attn(v):
        for c in range(3):
            oq[c] = v[:, c * ew : (c + 1) * ew].astype(BF)
        oo[...] = v[:, 3 * ew :].T.astype(BF)

    for a, (g, out) in enumerate(((gd, out_down), (gu, out_up))):
        for i, tz in enumerate(ends_first):
            idx = a * nz + i
            ffn.append(
                Reduce(
                    P_, idx, tz, pool, lambda f, idx=idx: (idx, f),
                    lambda f, b, g=g, tz=tz: g.at[tz, f, pl.ds(pl.multiple_of(b * quarter, 16), quarter), :],
                    True, rec, zbuf, idx, zx, a, sems, out,
                )
            )
    top = [[(P_.s >> o[0]) & 1 for o in ([0] + P_.o0, [0] + P_.o1)][f] for f in range(2)]
    for i, tz in enumerate(ends_first):
        idx = 2 * nz + i
        attn.append(
            Reduce(
                P_, idx, tz, rec0, lambda f, tz=tz: (2 * tz + f, top[f]),
                lambda f, b, tz=tz: rec0.at[2 * tz + f, b],
                False, rec, zbuf, idx, zx, 2, sems, out_attn,
            )
        )
    loads = {}

    def load(name, src, dst):
        i = len(loads)
        loads[name] = (src, dst, i)
        pltpu.make_async_copy(src, dst, lsem.at[i]).start()

    def ready(*names):
        for name in names:
            src, dst, i = loads[name]
            pltpu.make_async_copy(src, dst, lsem.at[i]).wait()

    uses = [(g, 3) for g in range(nz)] + [(g, c) for g in ends_first for c in range(3)]
    depth = ring.shape[0]

    def ring_copy(i):
        g, c = uses[i]
        return pltpu.make_async_copy(w4.at[g, c], ring.at[i % depth], rsem.at[i % depth])

    load("da2", da2i, datt)
    load("mid", midi, mid)
    load("co", co, dr0)
    for i in range(depth):
        ring_copy(i).start()
    load("att", atti, att)
    load("rden", rdeni, rden)
    load("fq", fqi, fq)
    greeted(P_.zdev + P_.sdev)
    for it in ffn:
        it.advance(0)
    load("fk", fki, fk)
    load("vb", vbi, vb)
    load("states", statesi, states)
    da1 = mid
    quads = 4 if np_ % 4 == 0 else 1

    def emit(rows, v):
        dmid[rows, :] = v
        dml[rows, :] = v.astype(BF)

    def do_lnb2():
        ready("da2", "mid", "co")
        norm_backward(datt, mid, gains.at[1:2], dr0, emit, sums2)

    def use_ring(i, body):
        ring_copy(i).wait()
        body(ring[i % depth])
        if i + depth < len(uses):
            ring_copy(i + depth).start()

    def do_datt():
        for i in range(nz):

            def body(w, i=i):
                datt[:, i * ew : (i + 1) * ew] = dot(dml[...], w)

            use_ring(i, body)

    def turn(p):
        for n in range(nb):
            attend_gradient(p, n, blk, datt, att, rden, dr0, dr1)
        chunk_gradients(p, blk, nb, fq, dr0, dr1, ginc)
        cur = cflag[nb - 1] * ginc[nb - 1, p]
        for n in range(nb - 2, -1, -1):
            cur = cflag[n] * (cur + ginc[n, p])
        g, rr = msg_rows(p, pg)
        msg[g, rr, :] = pack_state(cur, 2)

    def queries(p):
        for n in range(nb):
            back_queries(p, n, blk, fk, vb, fq, dr0, dr1, states[n, p], dq)

    def keys(p):
        g, rr = msg_rows(p, pg)
        cur = unpack_state(got[g, rr, :], False)
        for n in range(nb - 1, -1, -1):
            back_keys(p, n, blk, fk, vb, fq, dr0, dr1, cur.astype(BF))
            cur = cflag[n] * (cur + ginc[n, p])

    def pairs(body, i):
        n = np_ // quads
        loop_pairs(n, lambda p: body(p + i * n))

    def do_turn(i):
        if i == 0:
            ready("att", "rden", "fq")
        pairs(turn, i)

    def do_dmt():
        transpose_perm(ns, dml, dmt)
        load("x", x, dml)

    def do_queries(i):
        if i == 0:
            ready("fk", "vb", "states")
        pairs(queries, i)

    def do_a1():
        ready("x")
        norm_forward(dml, gains.at[0:1], biases.at[0:1], dml)
        transpose_perm(ns, dml, a1t)
        load("x2", x, dml)

    def do_keys_part(i):
        pairs(keys, i)

    def put(tz, c, v):
        v = v.astype(BF)
        for f in range(2):
            for b in range(2):
                r = (2 * f + b) * quarter
                rec0[2 * tz + f, b, :, c * ew : (c + 1) * ew] = v[r : r + quarter, :]

    def group(i):
        tz = ends_first[i]
        return tz, slice(tz * ew, (tz + 1) * ew)

    def do_out_grad(i):
        tz, c0 = group(i)
        put(tz, 3, dot(dmt[...], att[:, c0]))

    def do_grads(i):
        tz, c0 = group(i)
        for k, r in enumerate((dq, fk, vb)):
            put(tz, k, dot(a1t[...], r[:, c0]))

    def do_da1(i):
        tz, c0 = group(i)
        for k, r in enumerate((dq, fk, vb)):

            def body(w, k=k, r=r):
                v = dot_t(r[:, c0], w)
                if i == 0 and k == 0:
                    da1[...] = v
                else:
                    da1[...] += v

            use_ring(nz + i * 3 + k, body)

    def emit1(rows, v):
        dml[rows, :] = v.astype(BF)

    def do_lnb1():
        ready("x2")
        norm_backward(da1, dml, gains.at[0:1], dmid, emit1, sums1)
        gcur[0] = jnp.zeros(gcur.shape[1:], F32)
        for i, (ref, k) in enumerate(((sums1, 0), (sums2, 0), (sums1, 1), (sums2, 1))):
            gcur[0, i : i + 1, :] = jnp.sum(ref[k], axis=0, keepdims=True)

    todo = {
        "S": lambda i, st: ffn[i].advance(st),
        "A": lambda i, st: attn[i].advance(st),
        "lo": lambda r: lo_a.begin(r, r + 1),
        "gt": lambda r: gt_a.begin(r, r + 1),
        "m": small.advance,
        "s1": scan.phase1,
        "s2": scan.phase2,
        "s3": scan.phase3,
        "sf": scan.finish,
        "lnb2": do_lnb2,
        "datt": do_datt,
        "t": do_turn,
        "dmt": do_dmt,
        "q": do_queries,
        "a1": do_a1,
        "o": do_out_grad,
        "k": do_keys_part,
        "g": do_grads,
        "d": do_da1,
        "lnb1": do_lnb1,
    }
    for tok_ in aft_plan(nz, m, lo_a.parts, quads):
        todo[tok_[0]](*tok_[1:])
    lo_a.finish()
    gt_a.finish()
    for it in ffn + attn:
        it.drain()
    scan.drain()


def aft(ns, nz, nb, lengths, x, co, fq, fk, vb, att, rden, states, mid, w4g, lo, da2, gu, gd, gains, biases):
    t, d = x.shape
    ew, ff = w4g.shape[3], gu.shape[3]
    m = ns.bit_length() - 1
    np_ = d // 128
    dma = pltpu.SemaphoreType.DMA
    vm = pltpu.VMEM
    one = ((ew // 128) * MSG, 128)
    unit = d // (2 * ns)
    n_items = 3 * nz
    depth = 4
    args = (lengths, x, co, fq, fk, vb, att, rden, states, mid, w4g, lo, da2, gu, gd, gains, biases)
    pieces = [((3, 2 * unit, ew), BF), ((ew, 2 * unit), BF), ((2 * unit, ff), BF), ((ff, 2 * unit), BF)]
    rows = jax.ShapeDtypeStruct((t * nz, ew), BF)
    return pl.pallas_call(
        functools.partial(aft_kernel, ns, nz, nb),
        out_shape=(rows, rows, jax.ShapeDtypeStruct((8, d), F32)) + tuple(jax.ShapeDtypeStruct(*x) for x in pieces),
        in_specs=[smem_spec()] + [any_spec()] * 14 + [vmem_spec()] * 2,
        out_specs=(any_spec(),) * 2 + (vmem_spec(),) * 5,
        scratch_shapes=[vm((t, d), BF)] * 8
        + [vm((d, t), BF)] * 2
        + [vm((t, d), F32)] * 4
        + [
            vm((nb, np_, 128, 128), F32),
            vm((nb, np_, 128, 128), BF),
            vm((depth, d, ew), BF),
            vm((2, 8, d), F32),
            vm((2, 8, d), F32),
            vm((2 * nz, 2, d // 4, ff), BF),
        ]
        + [vm((n_items, 2, d // 4 >> j, ff), BF) for j in range(m)]
        + [
            vm((n_items, 2, unit, ff), BF),
            vm((3, max(1, nz // 2 - 1), 2, unit, ff), BF),
            vm((nz,) + one, BF),
            vm((nz,) + one, BF),
            vm((ns,) + one, BF),
            vm(one, BF),
            vm((nz,) + one, BF),
            vm((nz,) + one, BF),
            vm((m + 1, 8, d), F32),
            vm((m, 8, d), F32),
            vm((nz, 8, d), F32),
            dma((16,)),
            dma((depth,)),
            dma((2 * n_items,)),
            dma((2 * (nz - 1) * parts_of(t),)),
            dma((2 * (nz - 1) * parts_of(t),)),
            dma((2,)),
            dma((n_items * m * 2,)),
            dma((n_items * m * 2,)),
            dma((n_items * 2,)),
            dma((n_items * nz,)),
            dma((m + nz - 1,)),
            dma((m + nz - 1,)),
        ]
        + [dma((nz - 1,)), dma((nz - 1,)), dma((ns - 1,)), dma((ns - 1,)), dma((nz - 1,)), dma((nz - 1,))],
        name="aft",
        compiler_params=pltpu.CompilerParams(collective_id=1, has_side_effects=True, vmem_limit_bytes=63 * 2**20),
    )(*args)


def shards(ns, nz, tokens, lengths, pad_mask, w_qkv, w_out, w_up, w_down, norm_gains, norm_biases, out_cotangent):
    rows = tokens.shape[0]
    t = rows // nz
    d = w_qkv.shape[1]
    ff = w_up.shape[1]
    ew = d // nz
    blk = math.gcd(t, UNIT)
    nb = t // blk
    s, h = lax.axis_index("seq"), lax.axis_index("head")
    x, co, fq, fk, vb, att, rden, states, mid, w4g, lo, da2, gu, gd = fore(
        ns, nz, nb, lengths, tokens, out_cotangent, w_qkv, w_out, w_up[None], w_down[None],
        norm_gains, norm_biases, pad_mask.reshape(nz, t),
    )
    half = (nz, 2, d // 2, ff)
    lo_o, gt_o, gbo, oq, oo, ou, od = aft(
        ns, nz, nb, lengths, x, co, fq, fk, vb, att, rden, states, mid, w4g, lo, da2,
        gu.reshape(half), gd.reshape(half), norm_gains, norm_biases,
    )
    w = d // (ns * nz)
    gbs = lax.dynamic_slice_in_dim(gbo, (h * ns + s) * w, w, 1)
    return (
        lo_o,
        gt_o.astype(F32),
        oq.astype(F32),
        oo.astype(F32),
        ou.astype(F32),
        od.astype(F32),
        gbs[:2],
        gbs[2:4],
    )


def solution(mesh):
    in_specs = (
        P("seq", "head"),
        P(),
        P("seq"),
        P(None, None, "head"),
        P("head", None),
        P(None, "head"),
        P("head", None),
        P(),
        P(),
        P("seq", "head"),
    )
    out_specs = (
        P("seq", "head"),
        P("seq", "head"),
        P(None, "seq", "head"),
        P("head", "seq"),
        P("seq", "head"),
        P("head", "seq"),
        P(None, ("head", "seq")),
        P(None, ("head", "seq")),
    )
    f = functools.partial(shards, mesh.shape["seq"], mesh.shape["head"])
    return jax.shard_map(f, mesh=mesh, in_specs=in_specs, out_specs=out_specs, check_vma=False)
```

```python
import functools
import math

import jax
import jax.numpy as jnp
from jax import lax
from jax.experimental import pallas as pl
from jax.experimental.pallas import tpu as pltpu
from jax.sharding import PartitionSpec as P

HD = 64
UNIT = 768
EPS = 1e-05
MESH = pl.DeviceIdType.MESH
BF = jnp.bfloat16
F32 = jnp.float32


def bit_orders(ns):
    m = ns.bit_length() - 1
    xs = list(range(1, 1 + (m - 1) // 2))
    ys = list(range(1 + (m - 1) // 2, m))
    return xs + ys, ys + xs


def bits_to(s, order):
    out = 0
    for j, b in enumerate(order):
        out = out + (((s >> b) & 1) << j)
    return out


def rcopy(src, dst, send, recv, dev):
    return pltpu.make_async_remote_copy(
        src_ref=src, dst_ref=dst, send_sem=send, recv_sem=recv, device_id=dev, device_id_type=MESH
    )


def greet(devs):
    bar = pltpu.get_barrier_semaphore()
    for d in devs:
        pl.semaphore_signal(bar, inc=1, device_id=d, device_id_type=MESH)


def greeted(devs):
    pl.semaphore_wait(pltpu.get_barrier_semaphore(), len(devs))


def z_others(s, h, nz):
    return [(s, lax.rem(h + d, nz)) for d in range(1, nz)]


def any_spec():
    return pl.BlockSpec(memory_space=pl.ANY)


def vmem_spec():
    return pl.BlockSpec(memory_space=pltpu.VMEM)


def smem_spec():
    return pl.BlockSpec(memory_space=pltpu.SMEM)


def dot(a, b):
    return lax.dot_general(a, b, (((1,), (0,)), ((), ())), preferred_element_type=F32)


def dot_t(a, b):
    return lax.dot_general(a, b, (((1,), (1,)), ((), ())), preferred_element_type=F32)


def t_dot(a, b):
    return lax.dot_general(a, b, (((0,), (0,)), ((), ())), preferred_element_type=F32)


def lane_low(shape):
    return lax.broadcasted_iota(jnp.int32, shape, 1) < HD


def row_low(shape):
    return lax.broadcasted_iota(jnp.int32, shape, 0) < HD


def row_block(t):
    return 96 if t % 96 == 0 else 32


def over_rows(t, body, start=0):
    rb = row_block(t)

    def step(i, _):
        body(pl.ds(pl.multiple_of(start + i * rb, 32), rb))
        return 0

    lax.fori_loop(0, t // rb, step, 0)


def normed(v):
    mean = jnp.mean(v, axis=1, keepdims=True)
    c = v - mean
    w = lax.rsqrt(jnp.mean(c * c, axis=1, keepdims=True) + EPS)
    return c * w, w


def norm_forward(src, gain, bias, dst, start, n):
    def body(rows):
        xh, _ = normed(src[rows, :].astype(F32))
        dst[rows, :] = (xh * gain[...] + bias[...]).astype(BF)

    over_rows(n, body, start)


def norm_backward(e_ref, src, gain, add, emit, sums):
    sums[0] = jnp.zeros(sums.shape[1:], F32)
    sums[1] = jnp.zeros(sums.shape[1:], F32)

    def body(rows):
        e = e_ref[rows, :]
        xh, w = normed(src[rows, :].astype(F32))
        eg = e * gain[...]
        m1 = jnp.mean(eg, axis=1, keepdims=True)
        m2 = jnp.mean(eg * xh, axis=1, keepdims=True)
        emit(rows, add[rows, :].astype(F32) + w * (eg - m1 - xh * m2))
        n = e.shape[0]
        sums[0] += jnp.sum((e * xh).reshape(n // 8, 8, -1), axis=0)
        sums[1] += jnp.sum(e.reshape(n // 8, 8, -1), axis=0)

    over_rows(src.shape[0], body)


def transpose_perm(ns, src, dst):
    d = dst.shape[0]
    u = d // (2 * ns)
    o0, o1 = bit_orders(ns)
    m = ns.bit_length() - 1
    orders = ([0] + o0, [0] + o1)
    for j in range(d // 128):
        tr = src[:, j * 128 : (j + 1) * 128].T
        for i in range(128 // u):
            g = j * (128 // u) + i
            dev, f = g // 2, g % 2
            q = sum(((dev >> b) & 1) << (m - 1 - k) for k, b in enumerate(orders[f]))
            row = f * (d // 2) + q * u
            dst[row : row + u, :] = tr[i * u : (i + 1) * u, :]


def phi(y):
    return jnp.where(y > 0, y + 1.0, jnp.exp(jnp.minimum(y, 0.0)))


def cols(i, n):
    return pl.ds(pl.multiple_of(i * n, 128), n)


def project(a1, wg, g, pad, fq, fk, vb, rows):
    ew = wg.shape[3]
    c = cols(g, ew)
    a = a1[rows, :]
    mask = jnp.concatenate([pad[rows, :]] * (ew // 128), axis=1)
    fq[rows, c] = phi(dot(a, wg[g, 0])).astype(BF)
    fk[rows, c] = (mask * phi(dot(a, wg[g, 1]))).astype(BF)
    vb[rows, c] = dot(a, wg[g, 2]).astype(BF)


def with_ones(v2):
    one = jnp.ones_like(v2)
    low = lane_low(v2.shape)
    return jnp.where(low, v2, one), jnp.where(low, one, v2)


def chunk_sums(p, blk, n, fk, vb, inc):
    rows = pl.ds(n * blk, blk)
    k2, v2 = fk[rows, cols(p, 128)], vb[rows, cols(p, 128)]
    r = t_dot(k2, jnp.concatenate(with_ones(v2), axis=1))
    inc[n, p] = jnp.where(row_low((128, 128)), r[:, :128], r[:, 128:])


def causal_mask(blk):
    return lax.broadcasted_iota(jnp.int32, (blk, blk), 0) >= lax.broadcasted_iota(jnp.int32, (blk, blk), 1)


def masked_scores(a2, b2, keep):
    low = lane_low(b2.shape)
    zero = jnp.zeros_like(b2)
    return [
        jnp.where(keep, dot_t(a2, b), 0.0).astype(BF)
        for b in (jnp.where(low, b2, zero), jnp.where(low, zero, b2))
    ]


def split_state(st):
    low = row_low(st.shape)
    zero = jnp.zeros_like(st)
    return jnp.concatenate([jnp.where(low, st, zero), jnp.where(low, zero, st)], axis=1)


def attend_gradient(p, n, blk, datt, att, rden, dr0, dr1):
    rows = pl.ds(n * blk, blk)
    c = cols(p, 128)
    e = datt[rows, c]
    rd = rden[rows, c]
    low = lane_low(e.shape)
    lane = lax.broadcasted_iota(jnp.int32, e.shape, 1)
    dn = e * rd
    w = dn * att[rows, c].astype(F32)
    d0 = -jnp.sum(jnp.where(low, w, 0.0), axis=1, keepdims=True)
    d1 = -jnp.sum(jnp.where(low, 0.0, w), axis=1, keepdims=True)

    def parts(dd, first):
        hi = dd.astype(BF).astype(F32)
        return jnp.where(lane == first, hi, jnp.where(lane == first + 1, dd - hi, 0.0))

    dr0[rows, c] = jnp.where(low, dn, parts(d0, HD)).astype(BF)
    dr1[rows, c] = jnp.where(low, parts(d1, 0), dn).astype(BF)


def chunk_gradients(p, blk, nb, fq, dr0, dr1, ginc):
    for n in range(nb):
        rows = pl.ds(n * blk, blk)
        c = cols(p, 128)
        r = t_dot(fq[rows, c], jnp.concatenate([dr0[rows, c], dr1[rows, c]], axis=1))
        ginc[n, p] = jnp.where(row_low((128, 128)), r[:, :128], r[:, 128:])


def gelu_parts(s):
    c0 = math.sqrt(2.0 / math.pi)
    s2 = s * s
    th = jnp.tanh(c0 * (s + 0.044715 * s * s2))
    h = 0.5 * (1.0 + th)
    slope = h + 0.5 * s * (1.0 - th * th) * (c0 * (1.0 + 3 * 0.044715 * s2))
    return s * h, slope


def loop_pairs(n, body):
    def step(p, _):
        body(p)
        return 0

    lax.fori_loop(0, n, step, 0)


def group_order(nz):
    out = []
    for h in range(nz):
        seq = [h]
        for k in range(nz - 1):
            for o in (h - 1 - k, h + 1 + k):
                if 0 <= o < nz:
                    seq.append(o)
        out.append(seq)
    return out


def pick_group(order, h, i):
    out = 0
    for hh, seq in enumerate(order):
        for ii, g in enumerate(seq):
            if isinstance(i, int):
                if ii == i:
                    out = out + jnp.where(h == hh, g, 0)
            else:
                out = out + jnp.where((h == hh) & (i == ii), g, 0)
    return out


class Places:
    def __init__(self, ns, nz):
        self.ns, self.nz = ns, nz
        self.s, self.h = lax.axis_index("seq"), lax.axis_index("head")
        self.o0, self.o1 = bit_orders(ns)
        self.m = ns.bit_length() - 1
        self.zdev = z_others(self.s, self.h, nz)
        self.zfrom = [(self.s, lax.rem(self.h + nz - 1 - d, nz)) for d in range(nz - 1)]
        self.sdev = [(jnp.bitwise_xor(self.s, d), self.h) for d in range(1, ns)]
        self.bit = [(jnp.bitwise_xor(self.s, 1 << b), self.h) for b in range(self.m)]
        self.left, self.right = (self.s, self.h - 1), (self.s, self.h + 1)


class Gather:
    def __init__(self, pl_, buf, planes, zs, zr, ps, pr, base):
        self.p, self.buf, self.base = pl_, buf, base
        self.planes = pl.ds(*planes)
        self.sems = (zs, zr, ps, pr)
        self.orders = (pl_.o0 + [0], pl_.o1 + [0])
        self.half = buf.shape[2] // 2
        self.r = self.half // pl_.ns
        pos = [bits_to(pl_.s, o) for o in self.orders]
        self.zrow = [f * self.half + pos[f] * self.r for f in range(2)]
        self.mine = [
            [f * self.half + ((pos[f] >> j) << j) * self.r for j in range(pl_.m)] for f in range(2)
        ]
        self.theirs = [
            [f * self.half + jnp.bitwise_xor((pos[f] >> j) << j, 1 << j) * self.r for j in range(pl_.m)]
            for f in range(2)
        ]
        h, nz = pl_.h, pl_.nz
        self.origin = [(h - 1 - k, h + 1 + k) for k in range(nz - 1)]
        self.valid = [(h - 1 - k >= 0, h + 1 + k < nz) for k in range(nz - 1)]
        self.more = [((h - 1 - k >= 0) & (h + 1 < nz), (h + 1 + k < nz) & (h >= 1)) for k in range(nz - 1)]

    def rows(self, start, n):
        return pl.ds(pl.multiple_of(start, 16), n)

    def zcopy(self, f, k, d, origin):
        ref = self.buf.at[origin, self.planes, self.rows(self.zrow[f], self.r), :]
        i = ((self.base * 2 + f) * (self.p.nz - 1) + k) * 2 + d
        return rcopy(ref, ref, self.sems[0].at[i], self.sems[1].at[i], self.p.right if d == 0 else self.p.left)

    def pcopy(self, f, k, d, j, starts):
        n = self.r << j
        ref = self.buf.at[self.origin[k][d], self.planes, self.rows(starts[f][j], n), :]
        i = (((self.base * 2 + f) * (self.p.nz - 1) + k) * 2 + d) * self.p.m + j
        return rcopy(ref, ref, self.sems[2].at[i], self.sems[3].at[i], self.p.bit[self.orders[f][j]])

    def begin(self):
        for d, cond in enumerate((self.p.h + 1 < self.p.nz, self.p.h >= 1)):

            @pl.when(cond)
            def _(d=d):
                for f in range(2):
                    self.zcopy(f, 0, d, self.p.h).start()

    def forward(self, k):
        if k + 1 < self.p.nz - 1:
            for d in range(2):

                @pl.when(self.more[k][d])
                def _(d=d):
                    for f in range(2):
                        self.zcopy(f, k + 1, d, self.origin[k][d]).start()

    def advance(self, k, st):
        for d in range(2):

            @pl.when(self.valid[k][d])
            def _(d=d):
                for f in range(2):
                    if st == 0:
                        self.zcopy(f, k, d, self.origin[k][d]).wait_recv()
                    else:
                        self.pcopy(f, k, d, st - 1, self.theirs).wait_recv()
                if st < self.p.m:
                    for f in range(2):
                        self.pcopy(f, k, d, st, self.mine).start()

    def drain(self):
        for d, cond in enumerate((self.p.h + 1 < self.p.nz, self.p.h >= 1)):

            @pl.when(cond)
            def _(d=d):
                for f in range(2):
                    self.zcopy(f, 0, d, self.p.h).wait_send()

        for k in range(self.p.nz - 1):
            for d in range(2):

                @pl.when(self.valid[k][d])
                def _(d=d, k=k):
                    for f in range(2):
                        for j in range(self.p.m):
                            self.pcopy(f, k, d, j, self.mine).wait_send()
                    if k + 1 < self.p.nz - 1:

                        @pl.when(self.more[k][d])
                        def _():
                            for f in range(2):
                                self.zcopy(f, k + 1, d, self.origin[k][d]).wait_send()


def parts_of(t):
    return t // math.gcd(t, UNIT)


class RowsIn:
    def __init__(self, pl_, src, dst, ssem, rsem, lsem, base):
        self.p, self.src, self.dst, self.sems, self.base = pl_, src, dst, (ssem, rsem, lsem), base
        self.t, self.ew = dst.shape[0], src.shape[1]
        self.parts = parts_of(self.t)
        self.n = self.t // self.parts

    def copy(self, r, d, dev, col):
        i = (self.base * (self.p.nz - 1) + d) * self.parts + r
        return rcopy(
            self.src.at[pl.ds(pl.multiple_of(dev[1] * self.t + r * self.n, 16), self.n), :],
            self.dst.at[pl.ds(r * self.n, self.n), pl.ds(pl.multiple_of(col * self.ew, 128), self.ew)],
            self.sems[0].at[i],
            self.sems[1].at[i],
            dev,
        )

    def own(self):
        h = self.p.h
        return pltpu.make_async_copy(
            self.src.at[pl.ds(pl.multiple_of(h * self.t, 16), self.t), :],
            self.dst.at[:, pl.ds(pl.multiple_of(h * self.ew, 128), self.ew)],
            self.sems[2].at[self.base],
        )

    def begin(self, r):
        for d, dev in enumerate(self.p.zdev):
            self.copy(r, d, dev, self.p.h).start()

    def finish(self, r):
        for d, frm in enumerate(self.p.zfrom):
            self.copy(r, d, frm, frm[1]).wait_recv()

    def drain(self):
        for r in range(self.parts):
            for d, dev in enumerate(self.p.zdev):
                self.copy(r, d, dev, self.p.h).wait_send()


class Items:
    def __init__(self, p, lengths, t, nb):
        ns, nz, s, h = p.ns, p.nz, p.s, p.h
        ends, total = [], 0
        for i in range(lengths.shape[0]):
            total = total + lengths[i]
            ends.append(total)

        def item(pos):
            out = 0
            for e in ends:
                out = out + jnp.where(pos >= e, 1, 0)
            return out

        rows = nz * t
        first = s * rows
        me = first + h * t
        blk = t // nb

        def same(a, b):
            return jnp.where(a == b, 1.0, 0.0)

        line = [jnp.where(s == 0, -1, item(first - 1))] + [item(first + (z + 1) * t - 1) for z in range(nz)]
        before, last = line[:nz], line[1:]
        lines = [-1] + [item((k + 1) * rows - 1) for k in range(ns)]
        seq = [jnp.where(me == 0, -1, item(me - 1))] + [item(me + n * blk) for n in range(nb)]
        self.keep = [same(seq[n + 1], seq[n]) for n in range(nb)]
        zs, ks = range(nz), range(ns)
        zero = jnp.float32(0.0)
        self.fore = (
            [same(last[z], last[nz - 1]) for z in zs],
            [[jnp.where(k < s, same(lines[k + 1], before[z]), 0.0) for k in ks] for z in zs],
            [[same(last[k], before[z]) if k < z else zero for k in zs] for z in zs],
        )
        self.back = (
            [same(before[z], before[0]) for z in zs],
            [[jnp.where(k > s, same(lines[k], last[z]), 0.0) for k in ks] for z in zs],
            [[same(before[k], last[z]) if k > z else zero for k in zs] for z in zs],
        )


class Scan:
    def __init__(self, pl_, w, msg, r1, r2, tot, outb, got, sems):
        self.p, self.w, self.msg, self.r1, self.r2 = pl_, w, msg, r1, r2
        self.tot, self.outb, self.got, self.sems = tot, outb, got, sems

    def c1(self, d, dev, slot):
        return rcopy(self.msg.at[dev[1]], self.r1.at[slot], self.sems[0].at[d], self.sems[1].at[d], dev)

    def c2(self, d, dev, slot):
        return rcopy(self.tot, self.r2.at[slot], self.sems[2].at[d], self.sems[3].at[d], dev)

    def c3(self, d, dev, slot):
        return rcopy(self.outb.at[dev[1]], self.got.at[slot], self.sems[4].at[d], self.sems[5].at[d], dev)

    def phase1(self):
        for d, dev in enumerate(self.p.zdev):
            self.c1(d, dev, self.p.h).start()
        self.r1[self.p.h] = self.msg[self.p.h]

    def phase2(self):
        for d, frm in enumerate(self.p.zfrom):
            self.c1(d, frm, frm[1]).wait_recv()
        wt = self.w[0]
        self.tot[...] = sum(wt[z] * self.r1[z].astype(F32) for z in range(self.p.nz)).astype(BF)
        for d, dev in enumerate(self.p.sdev):
            self.c2(d, dev, self.p.s).start()
        self.r2[self.p.s] = self.tot[...]

    def phase3(self):
        for d, dev in enumerate(self.p.sdev):
            self.c2(d, dev, dev[0]).wait_recv()
        _, wp, wl = self.w
        for z in range(self.p.nz):
            v = sum(wl[z][k] * self.r1[k].astype(F32) for k in range(self.p.nz))
            v = v + sum(wp[z][k] * self.r2[k].astype(F32) for k in range(self.p.ns))
            self.outb[z] = v.astype(BF)
        for d, dev in enumerate(self.p.zdev):
            self.c3(d, dev, self.p.h).start()
        self.got[self.p.h] = self.outb[self.p.h]

    def finish(self):
        for d, frm in enumerate(self.p.zfrom):
            self.c3(d, frm, frm[1]).wait_recv()

    def drain(self):
        for d, dev in enumerate(self.p.zdev):
            self.c1(d, dev, self.p.h).wait_send()
            self.c3(d, dev, self.p.h).wait_send()
        for d, dev in enumerate(self.p.sdev):
            self.c2(d, dev, self.p.s).wait_send()


ZROWS = 16
MSG = HD + ZROWS


def msg_rows(p, pg):
    return p // pg, pl.ds(pl.multiple_of(lax.rem(p, pg) * MSG, 16), MSG)


def is_own(shape=(128, 128)):
    return row_low(shape) == lane_low(shape)


def pack_state(sa, lanes):
    own = is_own()
    state = jnp.where(lane_low((HD, 128)), sa[:HD], sa[HD:])
    z = jnp.where(own, 0.0, sa)
    hi = z.astype(BF)
    lo = (z - hi.astype(F32)).astype(BF)
    lane = lax.broadcasted_iota(jnp.int32, (ZROWS, 128), 1)
    row = lax.broadcasted_iota(jnp.int32, (ZROWS, 128), 0)
    sel = jnp.where((lane % HD) < lanes, 1.0, 0.0).astype(BF)
    zr = jnp.where(row == 0, dot_t(sel, hi), jnp.where(row == 1, dot_t(sel, lo), 0.0))
    return jnp.concatenate([state, zr], axis=0).astype(BF)


def unpack_state(msg, every):
    st = msg[:HD].astype(F32)
    z = t_dot(msg[HD:], jnp.ones((ZROWS, 128), BF))
    if not every:
        lane = lax.broadcasted_iota(jnp.int32, (128, 128), 1)
        z = jnp.where(lane % HD == 0, z, 0.0)
    return jnp.where(is_own(), jnp.concatenate([st, st], axis=0), z)


def state_part(p, n, blk, fq, st):
    rows = pl.ds(n * blk, blk)
    r = dot(fq[rows, cols(p, 128)], split_state(st))
    low = lane_low((blk, 128))
    num = jnp.where(low, r[:, :128], r[:, 128:])
    den = pltpu.roll(jnp.where(low, r[:, 128:], r[:, :128]), HD, 1)
    return num, den


FORE_ORDER = [
    ("Wb",), ("Ob",), ("Vb",), ("W", 0, 0), ("O", 0, 0), ("Wf", 0), ("X", 1), ("W", 0, 1), ("X", 0), ("W", 1, 0),
    ("Wf", 1), ("X", 2), ("W", 0, 2), ("W", 2, 0), ("W", 2, 1), ("V", 0, 0), ("Ub",), ("W", 0, 3), ("W", 1, 1),
    ("Of", 0), ("O", 0, 1), ("ln1", 0), ("pj", 1, 0), ("sums", 1, 0), ("ln1", 1), ("ln1", 2), ("W", 2, 2),
    ("W", 2, 3), ("loc", 1, 0), ("Vf", 0), ("W", 1, 2), ("U", 0, 0), ("W", 1, 3), ("pj", 3, 0), ("O", 1, 0),
    ("Of", 1), ("pj", 3, 2), ("O", 0, 2), ("O", 2, 0), ("Uf", 0), ("pj", 0, 1), ("sums", 0, 1), ("pj", 2, 0),
    ("loc", 2, 0), ("sums", 3, 2), ("Wf", 2), ("V", 1, 0), ("pj", 2, 1), ("loc", 2, 1), ("sums", 2, 1), ("Vf", 1),
    ("pj", 1, 1), ("sums", 2, 0), ("O", 1, 1), ("C", 0), ("pj", 3, 1), ("pj", 0, 2), ("V", 0, 1), ("sums", 0, 2),
    ("U", 1, 0), ("sums", 3, 0), ("loc", 1, 1), ("sums", 1, 1), ("sums", 3, 1), ("pj", 2, 2), ("pj", 1, 2),
    ("sums", 1, 2), ("pj", 0, 0), ("sums", 0, 0), ("sums", 2, 2), ("pack",), ("s1",), ("V", 2, 0), ("loc", 3, 2),
    ("loc", 0, 0), ("Uf", 1), ("loc", 1, 2), ("loc", 3, 1), ("loc", 2, 2), ("C", 2), ("Vf", 2), ("O", 2, 1), ("s2",),
    ("loc", 0, 1), ("U", 0, 1), ("loc", 3, 0), ("O", 2, 2), ("O", 0, 3), ("O", 2, 3), ("s3",), ("O", 1, 2),
    ("V", 0, 2), ("U", 2, 0), ("Of", 2), ("O", 1, 3), ("V", 1, 1), ("loc", 0, 2), ("keep",), ("U", 1, 1), ("C", 1),
    ("V", 0, 3), ("sf",), ("state", 0), ("state", 2), ("U", 0, 2), ("state", 3), ("state", 1), ("mid",), ("V", 1, 2),
    ("U", 2, 1), ("prep",), ("F", 0), ("U", 1, 2), ("F", 1), ("U", 2, 2), ("V", 2, 1), ("U", 0, 3), ("U", 1, 3),
    ("V", 1, 3), ("F", 2), ("F", 3), ("F", 4), ("V", 2, 2), ("U", 2, 3), ("F", 5), ("V", 2, 3), ("F", 6), ("Uf", 2),
    ("F", 7),
]
AFT_ORDER = [
    ("lnb2",), ("S", 0, 1), ("lo", 0), ("datt",), ("t", 0), ("t", 2), ("S", 0, 2), ("S", 5, 1), ("t", 3), ("t", 1),
    ("s1",), ("S", 6, 1), ("q", 1), ("s2",), ("S", 7, 1), ("S", 5, 2), ("lo", 2), ("S", 1, 1), ("q", 3), ("q", 0),
    ("s3",), ("q", 2), ("S", 6, 2), ("dmt",), ("S", 7, 2), ("S", 0, 3), ("lo", 1), ("sf",), ("k", 1), ("k", 3),
    ("S", 5, 3), ("S", 3, 1), ("k", 0), ("k", 2), ("S", 1, 2), ("d", 0), ("S", 6, 3), ("d", 1), ("S", 5, 4),
    ("S", 0, 4), ("d", 2), ("S", 4, 1), ("S", 7, 3), ("a1",), ("S", 2, 1), ("d", 3), ("o", 1), ("lnb1",), ("m", 0),
    ("gt", 1), ("S", 3, 2), ("o", 2), ("S", 6, 4), ("g", 3), ("o", 0), ("S", 1, 3), ("g", 1), ("A", 1, 0),
    ("S", 2, 2), ("S", 4, 2), ("gt", 2), ("g", 0), ("g", 2), ("S", 3, 3), ("A", 0, 0), ("A", 1, 1), ("S", 2, 3),
    ("S", 7, 4), ("A", 2, 0), ("o", 3), ("A", 2, 1), ("A", 0, 1), ("A", 2, 2), ("S", 0, 5), ("gt", 0), ("S", 4, 3),
    ("A", 3, 0), ("S", 1, 4), ("S", 2, 4), ("m", 1), ("A", 1, 2), ("A", 3, 1), ("m", 2), ("S", 4, 4), ("A", 2, 3),
    ("A", 2, 4), ("A", 0, 2), ("A", 1, 3), ("S", 3, 4), ("S", 5, 5), ("S", 2, 5), ("A", 1, 4), ("A", 3, 2), ("m", 3),
    ("A", 0, 3), ("S", 7, 5), ("S", 3, 5), ("S", 6, 5), ("A", 3, 3), ("S", 4, 5), ("A", 3, 4), ("A", 0, 4),
    ("A", 3, 5), ("A", 0, 5), ("m", 4), ("A", 1, 5), ("S", 1, 5), ("A", 2, 5),
]


def fore_plan(nz, m, per, parts):
    if (nz, m, per, parts) == (4, 3, 2, 3):
        return FORE_ORDER
    far = nz - 1
    out = [("Wb",)] + [("X", r) for r in range(parts)]
    for w, k, st in sorted((2 * k + st, k, st) for k in range(far) for st in range(m + 1)):
        out.append(("W", k, st))
        if st == 0:
            out.append(("Wf", k))
    out += [("Ob",), ("Ub",), ("Vb",)] + [("ln1", r) for r in range(parts)]
    out += [(a, i, r) for i in range(nz) for r in range(parts) for a in ("pj", "sums")]
    out += [("loc", 0, r) for r in range(parts)] + [("pack",)]
    out += [("s1",), ("keep",), ("C", 0), ("U", 0, 0), ("V", 0, 0)] + [("loc", i, r) for i in range(1, nz - 1) for r in range(parts)]
    out += [("s2",), ("U", 0, 1), ("V", 0, 1)] + [("loc", nz - 1, r) for r in range(parts)]
    out += [("s3",)] + [("C", r) for r in range(1, parts)]
    out += [("Uf", 0), ("Vf", 0), ("U", 0, 2), ("V", 0, 2), ("sf",)] + [("state", i) for i in range(nz)]
    out += [(a, 0, st) for st in range(3, m + 1) for a in "UV"]
    for k in range(far):
        out += [("O", k, 0), ("Of", k)] + [("O", k, st) for st in range(1, m + 1)]
    out += [("mid",), ("prep",)]
    for j in range(nz * per):
        for k in range(1, far):
            for st in range(m + 1):
                if max(0, (k + 1) * per - (m - st)) == j:
                    out += [("U", k, st), ("V", k, st)]
                    if st == 0:
                        out += [("Uf", k), ("Vf", k)]
        out.append(("F", j))
    return out


def fore_kernel(ns, nz, nb, *refs):
    lengths, tok, cot, wq, wo, wu, wd, gains, biases, pads = refs[:10]
    xo, coo, fqo, fko, vbo, atto, rdeno, stateso, mido, w4o, lo, da2o, gu, gd = refs[10:24]
    (xv, cov, av, fq, fk, vb, att, a2t, ct, rden, mid, acc, da2, inc, states,
     w4v, wuv, wdv, gub, gdb, msg, r1, r2, tot, outb, got,
     lsem, tsend, trecv, zsend, zrecv, psend, precv, wsem, ysem, osem,
     c1s, c1r, c2s, c2r, c3s, c3r, pad, wov) = refs[24:]
    P_ = Places(ns, nz)
    t, d = xv.shape
    blk = t // nb
    ew = wq.shape[2]
    ff = wu.shape[2]
    h = P_.h
    m = P_.m
    np_ = d // 128
    pg = msg.shape[1] // MSG
    order = group_order(nz)
    gidx = [pick_group(order, h, i) for i in range(nz)]
    W = Gather(P_, w4v, (0, 3), zsend, zrecv, psend, precv, 0)
    U = Gather(P_, wuv, (0, 1), zsend, zrecv, psend, precv, 1)
    V = Gather(P_, wdv, (0, 1), zsend, zrecv, psend, precv, 2)
    O = Gather(P_, w4v, (3, 1), zsend, zrecv, psend, precv, 3)
    X = RowsIn(P_, tok, xv, tsend, trecv, lsem, 0)
    C = RowsIn(P_, cot, cov, tsend, trecv, lsem, 1)
    greet(P_.zdev + P_.sdev)
    items = Items(P_, lengths, t, nb)
    cflag = items.keep
    scan = Scan(P_, items.fore, msg, r1, r2, tot, outb, got, (c1s, c1r, c2s, c2r, c3s, c3r))
    own = [
        pltpu.make_async_copy(wq, w4v.at[h, 0:3], wsem.at[0]),
        pltpu.make_async_copy(wo, wov, wsem.at[1]),
        pltpu.make_async_copy(wu, wuv.at[h], wsem.at[2]),
        pltpu.make_async_copy(wd, wdv.at[h], wsem.at[3]),
    ]
    for cp in own + [X.own(), C.own()]:
        cp.start()
    outs = []

    def keep(src, dst):
        cp = pltpu.make_async_copy(src, dst, ysem.at[len(outs)])
        outs.append(cp)
        cp.start()

    far = nz - 1
    tile = gub.shape[2]
    per = ff // tile
    steps = nz * per

    def sums_of(p, n):
        chunk_sums(p, blk, n, fk, vb, inc)

    def pack_of(p):
        cur = inc[0, p]
        for n in range(1, nb):
            cur = cflag[n] * cur + inc[n, p]
        g, rr = msg_rows(p, pg)
        msg[g, rr, :] = pack_state(cur, 1)

    def local_of(p, n):
        rows = pl.ds(n * blk, blk)
        c = cols(p, 128)
        q2, k2, v2 = fq[rows, c], fk[rows, c], vb[rows, c]
        s0, s1 = masked_scores(q2, k2, causal_mask(blk))
        g0, g1 = with_ones(v2)
        x0, x1 = dot(s0, g0), dot(s1, g1)
        low = lane_low(x0.shape)
        acc[rows, c] = jnp.where(low, x0, x1)
        rden[rows, c] = pltpu.roll(jnp.where(low, x1, x0), HD, 1)

    def state_of(p):
        g, rr = msg_rows(p, pg)
        cur = unpack_state(got[g, rr, :], True)
        for n in range(nb):
            rows = pl.ds(n * blk, blk)
            c = cols(p, 128)
            used = cflag[n] * cur
            st = used.astype(BF)
            states[n, p] = st
            cur = used + inc[n, p]
            num, den = state_part(p, n, blk, fq, st)
            rd = 1.0 / (1.0 + rden[rows, c] + den)
            att[rows, c] = ((acc[rows, c] + num) * rd).astype(BF)
            rden[rows, c] = rd

    once = []

    def do_ln1(r):
        if not once:
            once.append(r)
            make_pad()
            X.own().wait()
        X.finish(r)
        norm_forward(xv, gains.at[0:1], biases.at[0:1], av, r * blk, blk)

    def make_pad():
        at = h * t + lax.broadcasted_iota(jnp.int32, (t, 128), 0)
        lane = lax.broadcasted_iota(jnp.int32, (t, 128), 1)
        row = lax.broadcasted_iota(jnp.int32, (t, pads.shape[0]), 1)
        at_r = h * t + lax.broadcasted_iota(jnp.int32, (t, pads.shape[0]), 0)
        mine = dot(jnp.where(at_r // 128 == row, 1.0, 0.0).astype(BF), pads[...].astype(F32).astype(BF))
        mine = jnp.where(at % 128 == lane, mine, 0.0)
        pad[...] = jnp.broadcast_to(jnp.sum(mine, axis=1, keepdims=True), (t, 128))

    def do_project(i, r):
        project(av, w4v, gidx[i], pad, fq, fk, vb, pl.ds(r * blk, blk))

    def do_sums(i, r):
        loop_pairs(pg, lambda p: sums_of(p + gidx[i] * pg, r))

    def do_pack():
        loop_pairs(np_, pack_of)

    def do_keep():
        keep(xv, xo)
        keep(fq, fqo)
        keep(fk, fko)
        keep(vb, vbo)

    def do_local(i, r):
        loop_pairs(pg, lambda p: local_of(p + gidx[i] * pg, r))

    def do_state(i):
        loop_pairs(pg, lambda p: state_of(p + i * pg))

    def do_mid():
        keep(w4v, w4o)
        keep(att, atto)
        keep(rden, rdeno)
        keep(states, stateso)
        mid[...] = xv[...].astype(F32) + sum(dot_t(att[:, g * ew : (g + 1) * ew], w4v[g, 3]) for g in range(nz))
        norm_forward(mid, gains.at[1:2], biases.at[1:2], av, 0, t)
        keep(mid, mido)
        transpose_perm(ns, av, a2t)

    def do_prep():
        C.own().wait()
        for r in range(C.parts):
            C.finish(r)
        keep(cov, coo)
        transpose_perm(ns, cov, ct)
        acc[...] = mid[...]
        da2[...] = jnp.zeros_like(da2)

    def begin_own(i, a):
        own[i].wait()
        a.begin()

    def place(i):
        g = pick_group(order, h, i // per)
        return g, pl.ds(pl.multiple_of(lax.rem(i, per) * tile, 128), tile)

    def flush(i, slot):
        g, c = place(i)
        return (
            pltpu.make_async_copy(gub.at[slot], gu.at[g, :, c], osem.at[slot, 0]),
            pltpu.make_async_copy(gdb.at[slot], gd.at[g, :, c], osem.at[slot, 1]),
        )

    todo = {
        "X": X.begin,
        "C": C.begin,
        "W": W.advance,
        "O": O.advance,
        "Of": O.forward,
        "Ob": O.begin,
        "U": U.advance,
        "V": V.advance,
        "Wb": W.begin,
        "Ub": lambda: begin_own(2, U),
        "Vb": lambda: begin_own(3, V),
        "Wf": W.forward,
        "Uf": U.forward,
        "Vf": V.forward,
        "s1": scan.phase1,
        "s2": scan.phase2,
        "s3": scan.phase3,
        "sf": scan.finish,
        "ln1": do_ln1,
        "pj": do_project,
        "sums": do_sums,
        "pack": do_pack,
        "keep": do_keep,
        "loc": do_local,
        "state": do_state,
        "mid": do_mid,
        "prep": do_prep,
    }
    plan = fore_plan(nz, m, per, X.parts)
    cuts = [[]]
    for tok_ in plan:
        if tok_[0] == "F":
            cuts.append([])
        else:
            cuts[-1].append(tok_)

    def run(tokens):
        for tok_ in tokens:
            todo[tok_[0]](*tok_[1:])

    own[1].wait()
    for j in range(d // 256):
        w4v[h, 3, j * 256 : (j + 1) * 256, :] = wov[:, j * 256 : (j + 1) * 256].T
    own[0].wait()
    greeted(P_.zdev + P_.sdev)
    run(cuts[0])

    def step(i, _):
        slot = lax.rem(i, 2)
        for j in range(1, steps):
            if cuts[j]:
                pl.when(i == j)(functools.partial(run, cuts[j]))

        @pl.when(i >= 2)
        def _():
            for cp in flush(i - 2, slot):
                cp.wait()

        g, c = place(i)
        wub, wdb = wuv[g, 0, :, c], wdv[g, 0, c, :]
        up = dot(av[...], wub)
        hidf, slope = gelu_parts(up)
        hid = hidf.astype(BF)
        acc[...] += dot(hid, wdb)
        gdb[slot] = dot(ct[...], hid).astype(BF)
        dup = (slope * dot_t(cov[...], wdb)).astype(BF)
        da2[...] += dot_t(dup, wub)
        gub[slot] = dot(a2t[...], dup).astype(BF)
        for cp in flush(i, slot):
            cp.start()
        return 0

    lax.fori_loop(0, steps, step, 0)
    run(cuts[steps])
    keep(da2, da2o)
    av[...] = acc[...].astype(BF)
    keep(av, lo)
    for i in range(max(0, steps - 2), steps):
        for cp in flush(i, i % 2):
            cp.wait()
    for cp in outs:
        cp.wait()
    X.drain()
    C.drain()
    scan.drain()
    for a in (W, U, V, O):
        a.drain()


def fore(ns, nz, nb, lengths, tok, cot, wq, wo, wu, wd, gains, biases, pad):
    t, d = tok.shape[0] // nz, wq.shape[1]
    ew, ff = wq.shape[2], wu.shape[2]
    np_ = d // 128
    m = ns.bit_length() - 1
    dma = pltpu.SemaphoreType.DMA
    vm = pltpu.VMEM
    tile = 512 if ff % 512 == 0 else ff
    one = ((ew // 128) * MSG, 128)
    nzs = 4 * 2 * (nz - 1) * 2
    td, tdf = ((t, d), BF), ((t, d), F32)
    outs = [td, td, td, td, td, td, tdf, ((nb, np_, 128, 128), BF), tdf, ((nz, 4, d, ew), BF), td, tdf,
            ((nz, d, ff), BF), ((nz, d, ff), BF)]
    args = (lengths, tok, cot, wq, wo, wu, wd, gains, biases, pad)
    return pl.pallas_call(
        functools.partial(fore_kernel, ns, nz, nb),
        out_shape=tuple(jax.ShapeDtypeStruct(s, dt) for s, dt in outs),
        in_specs=[smem_spec()] + [any_spec()] * 6 + [vmem_spec()] * 3,
        out_specs=(any_spec(),) * len(outs),
        scratch_shapes=[vm((t, d), BF)] * 7
        + [vm((d, t), BF)] * 2
        + [vm((t, d), F32)] * 4
        + [
            vm((nb, np_, 128, 128), F32),
            vm((nb, np_, 128, 128), BF),
            vm((nz, 4, d, ew), BF),
            vm((nz, 1, d, ff), BF),
            vm((nz, 1, ff, d), BF),
            vm((2, d, tile), BF),
            vm((2, d, tile), BF),
            vm((nz,) + one, BF),
            vm((nz,) + one, BF),
            vm((ns,) + one, BF),
            vm(one, BF),
            vm((nz,) + one, BF),
            vm((nz,) + one, BF),
            dma((2,)),
            dma((2 * (nz - 1) * parts_of(t),)),
            dma((2 * (nz - 1) * parts_of(t),)),
            dma((nzs,)),
            dma((nzs,)),
            dma((nzs * m,)),
            dma((nzs * m,)),
            dma((4,)),
            dma((16,)),
            dma((2, 2)),
        ]
        + [dma((nz - 1,)), dma((nz - 1,)), dma((ns - 1,)), dma((ns - 1,)), dma((nz - 1,)), dma((nz - 1,))]
        + [vm((t, 128), F32), vm((ew, d), BF)],
        name="fore",
        compiler_params=pltpu.CompilerParams(collective_id=0, has_side_effects=True, vmem_limit_bytes=62 * 2**20),
    )(*args)


def add_block(dst, dlead, dstart, src, slead, n):
    blk = min(n, 64)

    def step(i, _):
        a = dst[dlead + (pl.ds(pl.multiple_of(dstart + i * blk, 16), blk), slice(None))]
        b = src[slead + (pl.ds(pl.multiple_of(i * blk, 16), blk), slice(None))]
        dst[dlead + (pl.ds(pl.multiple_of(dstart + i * blk, 16), blk), slice(None))] = (
            a.astype(F32) + b.astype(F32)
        ).astype(BF)
        return 0

    lax.fori_loop(0, n // blk, step, 0)


class Reduce:
    def __init__(self, p, idx, tz, acc, lead, src, own, rec, zbuf, zslot, zx, xslot, sems, out):
        self.p, self.idx, self.tz = p, idx, tz
        self.acc, self.lead, self.src, self.own, self.rec = acc, lead, src, own, rec
        self.zbuf, self.zslot, self.zx, self.xslot, self.out = zbuf, zslot, zx, xslot, out
        self.cs, self.cr, self.zs, self.zr, self.ls = sems
        orders = ([0] + p.o0, [0] + p.o1)
        self.orders = orders
        self.units = rec[0].shape[2] * 2 // p.ns
        self.bit = [[(p.s >> orders[f][j]) & 1 for j in range(p.m)] for f in range(2)]
        self.pos = []
        for f in range(2):
            pos, seq = 0, []
            for j in range(1, p.m):
                seq.append(pos)
                pos = pos + self.bit[f][j] * self.size(j)
            self.pos.append(seq + [pos])

    def size(self, j):
        return self.units * (self.p.ns >> (j + 1))

    def step(self, f, j):
        i = (self.idx * self.p.m + j) * 2 + f
        b = self.bit[f][j]
        n = self.size(j)
        if j == 0:
            src = self.src(f, 1 - b)
        else:
            at = self.pos[f][j - 1] + (1 - b) * n
            src = self.acc.at[self.lead(f) + (pl.ds(pl.multiple_of(at, 16), n), slice(None))]
        dst = self.rec[j].at[self.rslot(j), f]
        return rcopy(src, dst, self.cs.at[i], self.cr.at[i], self.p.bit[self.orders[f][j]])

    def rslot(self, j):
        return self.idx

    def load(self, f):
        return pltpu.make_async_copy(
            self.src(f, self.bit[f][0]), self.acc.at[self.lead(f)], self.ls.at[self.idx * 2 + f]
        )

    def route(self, hh):
        nz, tz = self.p.nz, self.tz
        q, count, inward = (hh, tz, 1) if hh < tz else (nz - 1 - hh, nz - 1 - tz, -1)
        if q % 2 == 0 and q + 1 < count:
            return False, hh + inward, 0
        return q % 2 == 1, tz, q // 2 + (0 if hh < tz else (tz + 1) // 2)

    def landing(self, f, slot):
        return self.zbuf.at[self.zslot, f] if slot == 0 else self.zx.at[self.xslot, slot - 1, f]

    def zcopy(self, f, to, slot):
        i = self.idx * 2 + f
        mine = self.acc.at[self.lead(f) + (pl.ds(pl.multiple_of(self.pos[f][-1], 16), self.units), slice(None))]
        r = (self.idx * (self.p.nz // 2) + slot) * 2 + f
        return rcopy(mine, self.landing(f, slot), self.zs.at[i], self.zr.at[r], (self.p.s, to))

    def advance(self, st):
        m, tz, nz = self.p.m, self.tz, self.p.nz
        if st <= m:
            for f in range(2):
                if st > 0:
                    self.step(f, st - 1).wait_recv()
                    if st == 1 and self.own:
                        self.load(f).wait()
                    add_block(self.acc, self.lead(f), self.pos[f][st - 1], self.rec[st - 1], (self.rslot(st - 1), f), self.size(st - 1))
                elif self.own:
                    self.load(f).start()
                if st < m:
                    self.step(f, st).start()
        if st == m or st == m + 1:
            for hh in range(nz):
                inner, to, slot = self.route(hh) if hh != tz else (None, 0, 0)
                if inner is None or inner != (st == m + 1):
                    continue

                @pl.when(self.p.h == hh)
                def _(inner=inner, to=to, slot=slot):
                    for f in range(2):
                        if inner:
                            self.zcopy(f, to, 0).wait_recv()
                            add_block(self.acc, self.lead(f), self.pos[f][-1], self.zbuf, (self.zslot, f), self.units)
                        self.zcopy(f, to, slot).start()

        if st == m + 2:

            @pl.when(self.p.h == tz)
            def _():
                both = []
                for f in range(2):
                    v = self.acc[self.lead(f) + (pl.ds(pl.multiple_of(self.pos[f][-1], 16), self.units), slice(None))]
                    v = v.astype(F32)
                    for slot in range((tz + 1) // 2 + (nz - tz) // 2):
                        self.zcopy(f, tz, slot).wait_recv()
                        ref = self.landing(f, slot)
                        v = v + ref[...].astype(F32)
                    both.append(v)
                self.out(jnp.concatenate(both, axis=0))

    def drain(self):
        for f in range(2):
            for j in range(self.p.m):
                self.step(f, j).wait_send()

        @pl.when(self.p.h != self.tz)
        def _():
            for f in range(2):
                self.zcopy(f, 0, 0).wait_send()


class RowsOut:
    def __init__(self, pl_, src, dst, ssem, rsem, lsem, base):
        self.p, self.src, self.dst, self.sems, self.base = pl_, src, dst, (ssem, rsem, lsem), base
        self.t, self.ew = src.shape[0], dst.shape[1]
        self.parts = parts_of(self.t)
        self.n = self.t // self.parts

    def copy(self, r, d, dev, row):
        i = (self.base * (self.p.nz - 1) + d) * self.parts + r
        return rcopy(
            self.src.at[pl.ds(r * self.n, self.n), pl.ds(pl.multiple_of(dev[1] * self.ew, 128), self.ew)],
            self.dst.at[pl.ds(pl.multiple_of(row * self.t + r * self.n, 16), self.n), :],
            self.sems[0].at[i],
            self.sems[1].at[i],
            dev,
        )

    def own(self):
        h = self.p.h
        return pltpu.make_async_copy(
            self.src.at[:, pl.ds(pl.multiple_of(h * self.ew, 128), self.ew)],
            self.dst.at[pl.ds(pl.multiple_of(h * self.t, 16), self.t), :],
            self.sems[2].at[self.base],
        )

    def begin(self, r):
        if r == 0:
            self.own().start()
        for d, dev in enumerate(self.p.zdev):
            self.copy(r, d, dev, self.p.h).start()

    def finish(self):
        for r in range(self.parts):
            for d, frm in enumerate(self.p.zfrom):
                self.copy(r, d, frm, frm[1]).wait_recv()
            for d, dev in enumerate(self.p.zdev):
                self.copy(r, d, dev, self.p.h).wait_send()
        self.own().wait()


class Small:
    def __init__(self, pl_, cur, rec, gz, ssem, rsem, out):
        self.p, self.cur, self.rec, self.gz, self.sems, self.out = pl_, cur, rec, gz, (ssem, rsem), out

    def hop(self, j):
        return rcopy(self.cur.at[j], self.rec.at[j], self.sems[0].at[j], self.sems[1].at[j], self.p.bit[j])

    def zhop(self, d, dev, slot):
        i = self.p.m + d
        return rcopy(self.cur.at[self.p.m], self.gz.at[slot], self.sems[0].at[i], self.sems[1].at[i], dev)

    def advance(self, st):
        m = self.p.m
        if 0 < st <= m:
            self.hop(st - 1).wait_recv()
            self.cur[st] = self.cur[st - 1] + self.rec[st - 1]
        if st < m:
            self.hop(st).start()
        if st == m:
            for d, dev in enumerate(self.p.zdev):
                self.zhop(d, dev, self.p.h).start()
            self.gz[self.p.h] = self.cur[m]
        if st == m + 1:
            for d, frm in enumerate(self.p.zfrom):
                self.zhop(d, frm, frm[1]).wait_recv()
            total = self.gz[0]
            for z in range(1, self.p.nz):
                total = total + self.gz[z]
            self.out[...] = total
            for j in range(m):
                self.hop(j).wait_send()
            for d, dev in enumerate(self.p.zdev):
                self.zhop(d, dev, self.p.h).wait_send()


def back_queries(p, n, blk, fk, vb, fq, dr0, dr1, st, dq):
    rows = pl.ds(n * blk, blk)
    c = cols(p, 128)
    q2, k2, v2, e0, e1 = fq[rows, c], fk[rows, c], vb[rows, c], dr0[rows, c], dr1[rows, c]
    g0, g1 = with_ones(v2)
    keep = causal_mask(blk)
    ds0 = jnp.where(keep, dot_t(e0, g0), 0.0).astype(BF)
    ds1 = jnp.where(keep, dot_t(e1, g1), 0.0).astype(BF)
    dfq = jnp.where(lane_low(q2.shape), dot(ds0, k2), dot(ds1, k2))
    dfq = dfq + dot_t(jnp.concatenate([e0, e1], axis=1), split_state(st))
    dq[rows, c] = (dfq * jnp.minimum(q2.astype(F32), 1.0)).astype(BF)


def back_keys(p, n, blk, fk, vb, fq, dr0, dr1, dst):
    rows = pl.ds(n * blk, blk)
    c = cols(p, 128)
    q2, k2, v2, e0, e1 = fq[rows, c], fk[rows, c], vb[rows, c], dr0[rows, c], dr1[rows, c]
    g0, g1 = with_ones(v2)
    keep_t = lax.broadcasted_iota(jnp.int32, (blk, blk), 0) <= lax.broadcasted_iota(jnp.int32, (blk, blk), 1)
    low = lane_low(q2.shape)
    dt0 = jnp.where(keep_t, dot_t(g0, e0), 0.0).astype(BF)
    dt1 = jnp.where(keep_t, dot_t(g1, e1), 0.0).astype(BF)
    dfk = jnp.where(low, dot(dt0, q2), dot(dt1, q2))
    dfk = dfk + dot_t(jnp.concatenate([g0, g1], axis=1), split_state(dst))
    st0, st1 = masked_scores(k2, q2, keep_t)
    own = jnp.where(row_low((128, 128)) == lane_low((128, 128)), dst, jnp.zeros_like(dst))
    dvv = jnp.where(low, dot(st0, e0), dot(st1, e1)) + dot(k2, own)
    fk[rows, c] = (dfk * jnp.minimum(k2.astype(F32), 1.0)).astype(BF)
    vb[rows, c] = dvv.astype(BF)


def aft_plan(nz, m, parts, quads):
    if (nz, m, parts, quads) == (4, 3, 3, 4):
        return AFT_ORDER
    n, last = 2 * nz, m + 2
    half = nz
    gaps = [half + 0.5] * (m - 1) + [3, 3]
    at = [sum(gaps[:st]) for st in range(last)]
    ffn = [("S", i, st) for _, i, st in sorted((i + at[st - 1], i, st) for i in range(n) for st in range(1, last + 1))]
    heads = 1 + max(j for j, x in enumerate(ffn) if x[2] == 1)
    out = []
    state = {"j": 0}

    def tick(k):
        out.extend(ffn[state["j"] : state["j"] + k])
        state["j"] = min(len(ffn), state["j"] + k)

    out += [("lo", r) for r in range(parts - 1)] + [("lnb2",)]
    tick(half - 2)
    out.append(("datt",))
    tick(1)
    for i in range(quads):
        out.append(("t", i))
        if i == 1:
            tick(1)
    out += [("s1",), ("lo", parts - 1), ("dmt",), ("s2",)]
    tick(3)
    for i in range(quads):
        out.append(("q", i))
        if i == min(1, quads - 1):
            tick(max(0, heads - state["j"]))
            out.append(("s3",))
        else:
            tick(1)
    out.append(("a1",))
    out += [("o", i) for i in range(nz)] + [("sf",)]
    for i in range(quads):
        out.append(("k", i))
        tick(1)
    attn = {w: [("A", i, w - i) for i in range(nz) if 0 <= w - i <= last] for w in range(nz + last)}
    for i in range(nz):
        out.append(("g", i))
        out += attn[i]
        out.append(("d", i))
        tick(1)
    out.append(("lnb1",))
    out += [("gt", r) for r in range(parts)]
    tick(len(ffn))
    for w in range(nz, nz + last):
        if w - nz <= m + 1:
            out.append(("m", w - nz))
        out += attn[w]
    out += [("m", st) for st in range(last, m + 2)]
    return out


def aft_kernel(ns, nz, nb, *refs):
    lengths, x, co, fqi, fki, vbi, atti, rdeni, statesi, midi, w4, lo, da2i, gu, gd, gains, biases = refs[:17]
    lo_o, gt_o, gbo, oq, oo, ou, od = refs[17:24]
    (fq, fk, vb, dr0, dr1, att, dml, dq, a1t, dmt, datt, mid, dmid, rden, ginc, states, ring, sums2, sums1,
     pool, rec0, *more) = refs[24:]
    m = ns.bit_length() - 1
    rec = [rec0] + list(more[: m - 1])
    (zbuf, zx, msg, r1, r2, tot, outb, got, gcur, grec, gz,
     lsem, rsem, asem, tsend, trecv, tl, csend, crecv, zsend, zrecv, gsend, grecv,
     c1s, c1r, c2s, c2r, c3s, c3r) = more[m - 1 :]
    P_ = Places(ns, nz)
    t, d = fq.shape
    blk = t // nb
    ew = lo_o.shape[1]
    np_ = d // 128
    pg = msg.shape[1] // MSG
    quarter = d // 4
    greet(P_.zdev + P_.sdev)
    items = Items(P_, lengths, t, nb)
    cflag = items.keep
    scan = Scan(P_, items.back, msg, r1, r2, tot, outb, got, (c1s, c1r, c2s, c2r, c3s, c3r))
    lo_a = RowsOut(P_, lo, lo_o, tsend, trecv, tl, 0)
    gt_a = RowsOut(P_, dml, gt_o, tsend, trecv, tl, 1)
    small = Small(P_, gcur, grec, gz, gsend, grecv, gbo)
    sems = (csend, crecv, zsend, zrecv, asem)
    ends_first = [z for pair in zip(range(nz // 2), range(nz - 1, nz // 2 - 1, -1)) for z in pair]
    ffn, attn = [], []

    def out_down(v):
        od[...] = v.T.astype(BF)

    def out_up(v):
        ou[...] = v.astype(BF)

    def out_attn(v):
        for c in range(3):
            oq[c] = v[:, c * ew : (c + 1) * ew].astype(BF)
        oo[...] = v[:, 3 * ew :].T.astype(BF)

    for a, (g, out) in enumerate(((gd, out_down), (gu, out_up))):
        for i, tz in enumerate(ends_first):
            idx = a * nz + i
            ffn.append(
                Reduce(
                    P_, idx, tz, pool, lambda f, idx=idx: (idx, f),
                    lambda f, b, g=g, tz=tz: g.at[tz, f, pl.ds(pl.multiple_of(b * quarter, 16), quarter), :],
                    True, rec, zbuf, idx, zx, a, sems, out,
                )
            )
    top = [[(P_.s >> o[0]) & 1 for o in ([0] + P_.o0, [0] + P_.o1)][f] for f in range(2)]
    for i, tz in enumerate(ends_first):
        idx = 2 * nz + i
        attn.append(
            Reduce(
                P_, idx, tz, rec0, lambda f, tz=tz: (2 * tz + f, top[f]),
                lambda f, b, tz=tz: rec0.at[2 * tz + f, b],
                False, rec, zbuf, idx, zx, 2, sems, out_attn,
            )
        )
    loads = {}

    def load(name, src, dst):
        i = len(loads)
        loads[name] = (src, dst, i)
        pltpu.make_async_copy(src, dst, lsem.at[i]).start()

    here = set()

    def ready(*names):
        for name in names:
            if name not in here:
                here.add(name)
                src, dst, i = loads[name]
                pltpu.make_async_copy(src, dst, lsem.at[i]).wait()

    uses = [(g, 3) for g in range(nz)] + [(g, c) for g in ends_first for c in range(3)]
    depth = ring.shape[0]

    def ring_copy(i):
        g, c = uses[i]
        return pltpu.make_async_copy(w4.at[g, c], ring.at[i % depth], rsem.at[i % depth])

    load("da2", da2i, datt)
    load("mid", midi, mid)
    load("co", co, dr0)
    for i in range(depth):
        ring_copy(i).start()
    load("att", atti, att)
    load("rden", rdeni, rden)
    load("fq", fqi, fq)
    greeted(P_.zdev + P_.sdev)
    for it in ffn:
        it.advance(0)
    load("fk", fki, fk)
    load("vb", vbi, vb)
    load("states", statesi, states)
    da1 = mid
    quads = 4 if np_ % 4 == 0 else 1

    def emit(rows, v):
        dmid[rows, :] = v
        dml[rows, :] = v.astype(BF)

    def do_lnb2():
        ready("da2", "mid", "co")
        norm_backward(datt, mid, gains.at[1:2], dr0, emit, sums2)

    def use_ring(i, body):
        ring_copy(i).wait()
        body(ring[i % depth])
        if i + depth < len(uses):
            ring_copy(i + depth).start()

    def do_datt():
        for i in range(nz):

            def body(w, i=i):
                datt[:, i * ew : (i + 1) * ew] = dot(dml[...], w)

            use_ring(i, body)

    def turn(p):
        for n in range(nb):
            attend_gradient(p, n, blk, datt, att, rden, dr0, dr1)
        chunk_gradients(p, blk, nb, fq, dr0, dr1, ginc)
        cur = cflag[nb - 1] * ginc[nb - 1, p]
        for n in range(nb - 2, -1, -1):
            cur = cflag[n] * (cur + ginc[n, p])
        g, rr = msg_rows(p, pg)
        msg[g, rr, :] = pack_state(cur, 2)

    def queries(p):
        for n in range(nb):
            back_queries(p, n, blk, fk, vb, fq, dr0, dr1, states[n, p], dq)

    def keys(p):
        g, rr = msg_rows(p, pg)
        cur = unpack_state(got[g, rr, :], False)
        for n in range(nb - 1, -1, -1):
            back_keys(p, n, blk, fk, vb, fq, dr0, dr1, cur.astype(BF))
            cur = cflag[n] * (cur + ginc[n, p])

    def pairs(body, i):
        n = np_ // quads
        loop_pairs(n, lambda p: body(p + i * n))

    def do_turn(i):
        ready("att", "rden", "fq")
        pairs(turn, i)

    def do_dmt():
        transpose_perm(ns, dml, dmt)
        load("x", x, dml)

    def do_queries(i):
        ready("fk", "vb", "states")
        pairs(queries, i)

    def do_a1():
        ready("x")
        norm_forward(dml, gains.at[0:1], biases.at[0:1], dml, 0, t)
        transpose_perm(ns, dml, a1t)
        load("x2", x, dml)

    def do_keys_part(i):
        pairs(keys, i)

    def put(tz, c, v):
        v = v.astype(BF)
        for f in range(2):
            for b in range(2):
                r = (2 * f + b) * quarter
                rec0[2 * tz + f, b, :, c * ew : (c + 1) * ew] = v[r : r + quarter, :]

    def group(i):
        tz = ends_first[i]
        return tz, slice(tz * ew, (tz + 1) * ew)

    def do_out_grad(i):
        tz, c0 = group(i)
        put(tz, 3, dot(dmt[...], att[:, c0]))

    def do_grads(i):
        tz, c0 = group(i)
        for k, r in enumerate((dq, fk, vb)):
            put(tz, k, dot(a1t[...], r[:, c0]))

    def do_da1(i):
        tz, c0 = group(i)
        j = nz + i * 3
        for k in range(3):
            ring_copy(j + k).wait()
        v = sum(dot_t(r[:, c0], ring[(j + k) % depth]) for k, r in enumerate((dq, fk, vb)))
        if i == 0:
            da1[...] = v
        else:
            da1[...] += v
        for k in range(3):
            if j + k + depth < len(uses):
                ring_copy(j + k + depth).start()

    def emit1(rows, v):
        dml[rows, :] = v.astype(BF)

    def do_lnb1():
        ready("x2")
        norm_backward(da1, dml, gains.at[0:1], dmid, emit1, sums1)
        gcur[0] = jnp.zeros(gcur.shape[1:], F32)
        for i, (ref, k) in enumerate(((sums1, 0), (sums2, 0), (sums1, 1), (sums2, 1))):
            gcur[0, i : i + 1, :] = jnp.sum(ref[k], axis=0, keepdims=True)

    todo = {
        "S": lambda i, st: ffn[i].advance(st),
        "A": lambda i, st: attn[i].advance(st),
        "lo": lo_a.begin,
        "gt": gt_a.begin,
        "m": small.advance,
        "s1": scan.phase1,
        "s2": scan.phase2,
        "s3": scan.phase3,
        "sf": scan.finish,
        "lnb2": do_lnb2,
        "datt": do_datt,
        "t": do_turn,
        "dmt": do_dmt,
        "q": do_queries,
        "a1": do_a1,
        "o": do_out_grad,
        "k": do_keys_part,
        "g": do_grads,
        "d": do_da1,
        "lnb1": do_lnb1,
    }
    for tok_ in aft_plan(nz, m, lo_a.parts, quads):
        todo[tok_[0]](*tok_[1:])
    lo_a.finish()
    gt_a.finish()
    for it in ffn + attn:
        it.drain()
    scan.drain()


def aft(ns, nz, nb, lengths, x, co, fq, fk, vb, att, rden, states, mid, w4g, lo, da2, gu, gd, gains, biases):
    t, d = x.shape
    ew, ff = w4g.shape[3], gu.shape[3]
    m = ns.bit_length() - 1
    np_ = d // 128
    dma = pltpu.SemaphoreType.DMA
    vm = pltpu.VMEM
    one = ((ew // 128) * MSG, 128)
    unit = d // (2 * ns)
    n_items = 3 * nz
    depth = 4
    args = (lengths, x, co, fq, fk, vb, att, rden, states, mid, w4g, lo, da2, gu, gd, gains, biases)
    pieces = [((3, 2 * unit, ew), BF), ((ew, 2 * unit), BF), ((2 * unit, ff), BF), ((ff, 2 * unit), BF)]
    rows = jax.ShapeDtypeStruct((t * nz, ew), BF)
    return pl.pallas_call(
        functools.partial(aft_kernel, ns, nz, nb),
        out_shape=(rows, rows, jax.ShapeDtypeStruct((8, d), F32)) + tuple(jax.ShapeDtypeStruct(*x) for x in pieces),
        in_specs=[smem_spec()] + [any_spec()] * 14 + [vmem_spec()] * 2,
        out_specs=(any_spec(),) * 2 + (vmem_spec(),) * 5,
        scratch_shapes=[vm((t, d), BF)] * 8
        + [vm((d, t), BF)] * 2
        + [vm((t, d), F32)] * 4
        + [
            vm((nb, np_, 128, 128), F32),
            vm((nb, np_, 128, 128), BF),
            vm((depth, d, ew), BF),
            vm((2, 8, d), F32),
            vm((2, 8, d), F32),
            vm((2 * nz, 2, d // 4, ff), BF),
        ]
        + [vm((n_items, 2, d // 4 >> j, ff), BF) for j in range(m)]
        + [
            vm((n_items, 2, unit, ff), BF),
            vm((3, max(1, nz // 2 - 1), 2, unit, ff), BF),
            vm((nz,) + one, BF),
            vm((nz,) + one, BF),
            vm((ns,) + one, BF),
            vm(one, BF),
            vm((nz,) + one, BF),
            vm((nz,) + one, BF),
            vm((m + 1, 8, d), F32),
            vm((m, 8, d), F32),
            vm((nz, 8, d), F32),
            dma((16,)),
            dma((depth,)),
            dma((2 * n_items,)),
            dma((2 * (nz - 1) * parts_of(t),)),
            dma((2 * (nz - 1) * parts_of(t),)),
            dma((2,)),
            dma((n_items * m * 2,)),
            dma((n_items * m * 2,)),
            dma((n_items * 2,)),
            dma((n_items * nz,)),
            dma((m + nz - 1,)),
            dma((m + nz - 1,)),
        ]
        + [dma((nz - 1,)), dma((nz - 1,)), dma((ns - 1,)), dma((ns - 1,)), dma((nz - 1,)), dma((nz - 1,))],
        name="aft",
        compiler_params=pltpu.CompilerParams(collective_id=1, has_side_effects=True, vmem_limit_bytes=63 * 2**20),
    )(*args)


def finish_kernel(where, gt, lo, oq, oo, ou, od, gb, gt_o, lo_o, oq_o, oo_o, ou_o, od_o, gg, gbias):
    gt_o[...] = gt[...].astype(F32)
    lo_o[...] = lo[...]

    @pl.when(pl.program_id(0) == 0)
    def _():
        for src, dst in ((oq, oq_o), (oo, oo_o), (ou, ou_o), (od, od_o)):
            dst[...] = src[...].astype(F32)
        w = gg.shape[1]
        shape = (gb.shape[1], w)
        at = lax.broadcasted_iota(jnp.int32, shape, 0) - where[0] * w
        pick = jnp.where(at == lax.broadcasted_iota(jnp.int32, shape, 1), 1.0, 0.0)
        v = jnp.dot(gb[...], pick, precision=lax.Precision.HIGHEST, preferred_element_type=F32)
        gg[...] = v[:2]
        gbias[...] = v[2:4]


def finish(where, w, gt, lo, oq, oo, ou, od, gb):
    n = 4
    rows, ew = gt.shape
    blk = pl.BlockSpec((rows // n, ew), lambda i: (i, 0))

    def whole(a):
        return pl.BlockSpec(a.shape, lambda i, k=len(a.shape): (0,) * k)

    small = jax.ShapeDtypeStruct((2, w), F32)
    outs = [jax.ShapeDtypeStruct(gt.shape, F32), jax.ShapeDtypeStruct(lo.shape, BF)]
    outs += [jax.ShapeDtypeStruct(a.shape, F32) for a in (oq, oo, ou, od)] + [small, small]
    return pl.pallas_call(
        finish_kernel,
        grid=(n,),
        out_shape=tuple(outs),
        in_specs=[smem_spec(), blk, blk] + [whole(a) for a in (oq, oo, ou, od, gb)],
        out_specs=(blk, blk) + tuple(whole(a) for a in outs[2:]),
        name="finish",
        compiler_params=pltpu.CompilerParams(vmem_limit_bytes=60 * 2**20),
    )(where, gt, lo, oq, oo, ou, od, gb)


def shards(ns, nz, tokens, lengths, pad_mask, w_qkv, w_out, w_up, w_down, norm_gains, norm_biases, out_cotangent):
    rows = tokens.shape[0]
    t = rows // nz
    d = w_qkv.shape[1]
    ff = w_up.shape[1]
    ew = d // nz
    blk = math.gcd(t, UNIT)
    nb = t // blk
    s, h = lax.axis_index("seq"), lax.axis_index("head")
    x, co, fq, fk, vb, att, rden, states, mid, w4g, lo, da2, gu, gd = fore(
        ns, nz, nb, lengths, tokens, out_cotangent, w_qkv, w_out, w_up[None], w_down[None],
        norm_gains, norm_biases, pad_mask.reshape(rows // 128, 128),
    )
    half = (nz, 2, d // 2, ff)
    lo_o, gt_o, gbo, oq, oo, ou, od = aft(
        ns, nz, nb, lengths, x, co, fq, fk, vb, att, rden, states, mid, w4g, lo, da2,
        gu.reshape(half), gd.reshape(half), norm_gains, norm_biases,
    )
    w = d // (ns * nz)
    where = jnp.reshape(h * ns + s, (1,)).astype(jnp.int32)
    gt_f, lo_f, gq, go, gup, gdown, gg, gbias = finish(where, w, gt_o, lo_o, oq, oo, ou, od, gbo)
    return lo_f, gt_f, gq, go, gup, gdown, gg, gbias


def solution(mesh):
    in_specs = (
        P("seq", "head"),
        P(),
        P("seq"),
        P(None, None, "head"),
        P("head", None),
        P(None, "head"),
        P("head", None),
        P(),
        P(),
        P("seq", "head"),
    )
    out_specs = (
        P("seq", "head"),
        P("seq", "head"),
        P(None, "seq", "head"),
        P("head", "seq"),
        P("seq", "head"),
        P("head", "seq"),
        P(None, ("head", "seq")),
        P(None, ("head", "seq")),
    )
    f = functools.partial(shards, mesh.shape["seq"], mesh.shape["head"])
    return jax.shard_map(f, mesh=mesh, in_specs=in_specs, out_specs=out_specs, check_vma=False)
```

```python
import functools
import math

import jax
import jax.numpy as jnp
from jax import lax
from jax.experimental import pallas as pl
from jax.experimental.pallas import tpu as pltpu
from jax.sharding import PartitionSpec as P

HD = 64
UNIT = 768
EPS = 1e-05
MESH = pl.DeviceIdType.MESH
BF = jnp.bfloat16
F32 = jnp.float32


def bit_orders(ns):
    m = ns.bit_length() - 1
    xs = list(range(1, 1 + (m - 1) // 2))
    ys = list(range(1 + (m - 1) // 2, m))
    return xs + ys, ys + xs


def bits_to(s, order):
    out = 0
    for j, b in enumerate(order):
        out = out + (((s >> b) & 1) << j)
    return out


def rcopy(src, dst, send, recv, dev):
    return pltpu.make_async_remote_copy(
        src_ref=src, dst_ref=dst, send_sem=send, recv_sem=recv, device_id=dev, device_id_type=MESH
    )


def greet(devs):
    bar = pltpu.get_barrier_semaphore()
    for d in devs:
        pl.semaphore_signal(bar, inc=1, device_id=d, device_id_type=MESH)


def greeted(devs):
    pl.semaphore_wait(pltpu.get_barrier_semaphore(), len(devs))


def z_others(s, h, nz):
    return [(s, lax.rem(h + d, nz)) for d in range(1, nz)]


def any_spec():
    return pl.BlockSpec(memory_space=pl.ANY)


def vmem_spec():
    return pl.BlockSpec(memory_space=pltpu.VMEM)


def smem_spec():
    return pl.BlockSpec(memory_space=pltpu.SMEM)


def dot(a, b):
    return lax.dot_general(a, b, (((1,), (0,)), ((), ())), preferred_element_type=F32)


def dot_t(a, b):
    return lax.dot_general(a, b, (((1,), (1,)), ((), ())), preferred_element_type=F32)


def t_dot(a, b):
    return lax.dot_general(a, b, (((0,), (0,)), ((), ())), preferred_element_type=F32)


def lane_low(shape):
    return lax.broadcasted_iota(jnp.int32, shape, 1) < HD


def row_low(shape):
    return lax.broadcasted_iota(jnp.int32, shape, 0) < HD


def row_block(t):
    return 96 if t % 96 == 0 else 32


def over_rows(t, body, start=0):
    rb = row_block(t)

    def step(i, _):
        body(pl.ds(pl.multiple_of(start + i * rb, 32), rb))
        return 0

    lax.fori_loop(0, t // rb, step, 0)


def normed(v):
    mean = jnp.mean(v, axis=1, keepdims=True)
    c = v - mean
    w = lax.rsqrt(jnp.mean(c * c, axis=1, keepdims=True) + EPS)
    return c * w, w


def norm_forward(src, gain, bias, dst, start, n):
    def body(rows):
        xh, _ = normed(src[rows, :].astype(F32))
        dst[rows, :] = (xh * gain[...] + bias[...]).astype(BF)

    over_rows(n, body, start)


def norm_backward(e_ref, src, gain, add, emit, sums):
    sums[0] = jnp.zeros(sums.shape[1:], F32)
    sums[1] = jnp.zeros(sums.shape[1:], F32)

    def body(rows):
        e = e_ref[rows, :]
        xh, w = normed(src[rows, :].astype(F32))
        eg = e * gain[...]
        m1 = jnp.mean(eg, axis=1, keepdims=True)
        m2 = jnp.mean(eg * xh, axis=1, keepdims=True)
        emit(rows, add[rows, :].astype(F32) + w * (eg - m1 - xh * m2))
        n = e.shape[0]
        sums[0] += jnp.sum((e * xh).reshape(n // 8, 8, -1), axis=0)
        sums[1] += jnp.sum(e.reshape(n // 8, 8, -1), axis=0)

    over_rows(src.shape[0], body)


def transpose_perm(ns, src, dst):
    d = dst.shape[0]
    u = d // (2 * ns)
    o0, o1 = bit_orders(ns)
    m = ns.bit_length() - 1
    orders = ([0] + o0, [0] + o1)
    for j in range(d // 128):
        tr = src[:, j * 128 : (j + 1) * 128].T
        for i in range(128 // u):
            g = j * (128 // u) + i
            dev, f = g // 2, g % 2
            q = sum(((dev >> b) & 1) << (m - 1 - k) for k, b in enumerate(orders[f]))
            row = f * (d // 2) + q * u
            dst[row : row + u, :] = tr[i * u : (i + 1) * u, :]


def phi(y):
    return jnp.where(y > 0, y + 1.0, jnp.exp(jnp.minimum(y, 0.0)))


def cols(i, n):
    return pl.ds(pl.multiple_of(i * n, 128), n)


def project(a1, wg, g, pad, fq, fk, vb, rows):
    ew = wg.shape[3]
    c = cols(g, ew)
    a = a1[rows, :]
    mask = jnp.concatenate([pad[rows, :]] * (ew // 128), axis=1)
    fq[rows, c] = phi(dot(a, wg[g, 0])).astype(BF)
    fk[rows, c] = (mask * phi(dot(a, wg[g, 1]))).astype(BF)
    vb[rows, c] = dot(a, wg[g, 2]).astype(BF)


def with_ones(v2):
    one = jnp.ones_like(v2)
    low = lane_low(v2.shape)
    return jnp.where(low, v2, one), jnp.where(low, one, v2)


def chunk_sums(p, blk, n, fk, vb, inc):
    rows = pl.ds(n * blk, blk)
    k2, v2 = fk[rows, cols(p, 128)], vb[rows, cols(p, 128)]
    r = t_dot(k2, jnp.concatenate(with_ones(v2), axis=1))
    inc[n, p] = jnp.where(row_low((128, 128)), r[:, :128], r[:, 128:])


def causal_mask(blk):
    return lax.broadcasted_iota(jnp.int32, (blk, blk), 0) >= lax.broadcasted_iota(jnp.int32, (blk, blk), 1)


def masked_scores(a2, b2, keep):
    low = lane_low(b2.shape)
    zero = jnp.zeros_like(b2)
    return [
        jnp.where(keep, dot_t(a2, b), 0.0).astype(BF)
        for b in (jnp.where(low, b2, zero), jnp.where(low, zero, b2))
    ]


def split_state(st):
    low = row_low(st.shape)
    zero = jnp.zeros_like(st)
    return jnp.concatenate([jnp.where(low, st, zero), jnp.where(low, zero, st)], axis=1)


def attend_gradient(p, n, blk, datt, att, rden, dr0, dr1):
    rows = pl.ds(n * blk, blk)
    c = cols(p, 128)
    e = datt[rows, c]
    rd = rden[rows, c]
    low = lane_low(e.shape)
    lane = lax.broadcasted_iota(jnp.int32, e.shape, 1)
    dn = e * rd
    w = dn * att[rows, c].astype(F32)
    d0 = -jnp.sum(jnp.where(low, w, 0.0), axis=1, keepdims=True)
    d1 = -jnp.sum(jnp.where(low, 0.0, w), axis=1, keepdims=True)

    def parts(dd, first):
        hi = dd.astype(BF).astype(F32)
        return jnp.where(lane == first, hi, jnp.where(lane == first + 1, dd - hi, 0.0))

    dr0[rows, c] = jnp.where(low, dn, parts(d0, HD)).astype(BF)
    dr1[rows, c] = jnp.where(low, parts(d1, 0), dn).astype(BF)


def chunk_gradients(p, blk, nb, fq, dr0, dr1, ginc):
    for n in range(nb):
        rows = pl.ds(n * blk, blk)
        c = cols(p, 128)
        r = t_dot(fq[rows, c], jnp.concatenate([dr0[rows, c], dr1[rows, c]], axis=1))
        ginc[n, p] = jnp.where(row_low((128, 128)), r[:, :128], r[:, 128:])


def gelu_parts(s):
    c0 = math.sqrt(2.0 / math.pi)
    s2 = s * s
    th = jnp.tanh(c0 * (s + 0.044715 * s * s2))
    h = 0.5 * (1.0 + th)
    slope = h + 0.5 * s * (1.0 - th * th) * (c0 * (1.0 + 3 * 0.044715 * s2))
    return s * h, slope


def loop_pairs(n, body):
    def step(p, _):
        body(p)
        return 0

    lax.fori_loop(0, n, step, 0)


def group_order(nz):
    out = []
    for h in range(nz):
        seq = [h]
        for k in range(nz - 1):
            for o in (h - 1 - k, h + 1 + k):
                if 0 <= o < nz:
                    seq.append(o)
        out.append(seq)
    return out


def pick_group(order, h, i):
    out = 0
    for hh, seq in enumerate(order):
        for ii, g in enumerate(seq):
            if isinstance(i, int):
                if ii == i:
                    out = out + jnp.where(h == hh, g, 0)
            else:
                out = out + jnp.where((h == hh) & (i == ii), g, 0)
    return out


class Places:
    def __init__(self, ns, nz):
        self.ns, self.nz = ns, nz
        self.s, self.h = lax.axis_index("seq"), lax.axis_index("head")
        self.o0, self.o1 = bit_orders(ns)
        self.m = ns.bit_length() - 1
        self.zdev = z_others(self.s, self.h, nz)
        self.zfrom = [(self.s, lax.rem(self.h + nz - 1 - d, nz)) for d in range(nz - 1)]
        self.sdev = [(jnp.bitwise_xor(self.s, d), self.h) for d in range(1, ns)]
        self.bit = [(jnp.bitwise_xor(self.s, 1 << b), self.h) for b in range(self.m)]
        self.left, self.right = (self.s, self.h - 1), (self.s, self.h + 1)


class Gather:
    def __init__(self, pl_, buf, planes, zs, zr, ps, pr, base):
        self.p, self.buf, self.base = pl_, buf, base
        self.planes = pl.ds(*planes)
        self.sems = (zs, zr, ps, pr)
        self.orders = (pl_.o0 + [0], pl_.o1 + [0])
        self.half = buf.shape[2] // 2
        self.r = self.half // pl_.ns
        pos = [bits_to(pl_.s, o) for o in self.orders]
        self.zrow = [f * self.half + pos[f] * self.r for f in range(2)]
        self.mine = [
            [f * self.half + ((pos[f] >> j) << j) * self.r for j in range(pl_.m)] for f in range(2)
        ]
        self.theirs = [
            [f * self.half + jnp.bitwise_xor((pos[f] >> j) << j, 1 << j) * self.r for j in range(pl_.m)]
            for f in range(2)
        ]
        h, nz = pl_.h, pl_.nz
        self.origin = [(h - 1 - k, h + 1 + k) for k in range(nz - 1)]
        self.valid = [(h - 1 - k >= 0, h + 1 + k < nz) for k in range(nz - 1)]
        self.more = [((h - 1 - k >= 0) & (h + 1 < nz), (h + 1 + k < nz) & (h >= 1)) for k in range(nz - 1)]

    def rows(self, start, n):
        return pl.ds(pl.multiple_of(start, 16), n)

    def zcopy(self, f, k, d, origin):
        ref = self.buf.at[origin, self.planes, self.rows(self.zrow[f], self.r), :]
        i = ((self.base * 2 + f) * (self.p.nz - 1) + k) * 2 + d
        return rcopy(ref, ref, self.sems[0].at[i], self.sems[1].at[i], self.p.right if d == 0 else self.p.left)

    def pcopy(self, f, k, d, j, starts):
        n = self.r << j
        ref = self.buf.at[self.origin[k][d], self.planes, self.rows(starts[f][j], n), :]
        i = (((self.base * 2 + f) * (self.p.nz - 1) + k) * 2 + d) * self.p.m + j
        return rcopy(ref, ref, self.sems[2].at[i], self.sems[3].at[i], self.p.bit[self.orders[f][j]])

    def begin(self):
        for d, cond in enumerate((self.p.h + 1 < self.p.nz, self.p.h >= 1)):

            @pl.when(cond)
            def _(d=d):
                for f in range(2):
                    self.zcopy(f, 0, d, self.p.h).start()

    def forward(self, k):
        if k + 1 < self.p.nz - 1:
            for d in range(2):

                @pl.when(self.more[k][d])
                def _(d=d):
                    for f in range(2):
                        self.zcopy(f, k + 1, d, self.origin[k][d]).start()

    def advance(self, k, st):
        for d in range(2):

            @pl.when(self.valid[k][d])
            def _(d=d):
                for f in range(2):
                    if st == 0:
                        self.zcopy(f, k, d, self.origin[k][d]).wait_recv()
                    else:
                        self.pcopy(f, k, d, st - 1, self.theirs).wait_recv()
                if st < self.p.m:
                    for f in range(2):
                        self.pcopy(f, k, d, st, self.mine).start()

    def drain(self):
        for d, cond in enumerate((self.p.h + 1 < self.p.nz, self.p.h >= 1)):

            @pl.when(cond)
            def _(d=d):
                for f in range(2):
                    self.zcopy(f, 0, d, self.p.h).wait_send()

        for k in range(self.p.nz - 1):
            for d in range(2):

                @pl.when(self.valid[k][d])
                def _(d=d, k=k):
                    for f in range(2):
                        for j in range(self.p.m):
                            self.pcopy(f, k, d, j, self.mine).wait_send()
                    if k + 1 < self.p.nz - 1:

                        @pl.when(self.more[k][d])
                        def _():
                            for f in range(2):
                                self.zcopy(f, k + 1, d, self.origin[k][d]).wait_send()


def parts_of(t):
    return t // math.gcd(t, UNIT)


class RowsIn:
    def __init__(self, pl_, src, dst, ssem, rsem, lsem, base):
        self.p, self.src, self.dst, self.sems, self.base = pl_, src, dst, (ssem, rsem, lsem), base
        self.t, self.ew = dst.shape[0], src.shape[1]
        self.parts = parts_of(self.t)
        self.n = self.t // self.parts

    def copy(self, r, d, dev, col):
        i = (self.base * (self.p.nz - 1) + d) * self.parts + r
        return rcopy(
            self.src.at[pl.ds(pl.multiple_of(dev[1] * self.t + r * self.n, 16), self.n), :],
            self.dst.at[pl.ds(r * self.n, self.n), pl.ds(pl.multiple_of(col * self.ew, 128), self.ew)],
            self.sems[0].at[i],
            self.sems[1].at[i],
            dev,
        )

    def own(self):
        h = self.p.h
        return pltpu.make_async_copy(
            self.src.at[pl.ds(pl.multiple_of(h * self.t, 16), self.t), :],
            self.dst.at[:, pl.ds(pl.multiple_of(h * self.ew, 128), self.ew)],
            self.sems[2].at[self.base],
        )

    def begin(self, r):
        for d, dev in enumerate(self.p.zdev):
            self.copy(r, d, dev, self.p.h).start()

    def finish(self, r):
        for d, frm in enumerate(self.p.zfrom):
            self.copy(r, d, frm, frm[1]).wait_recv()

    def drain(self):
        for r in range(self.parts):
            for d, dev in enumerate(self.p.zdev):
                self.copy(r, d, dev, self.p.h).wait_send()


class Items:
    def __init__(self, p, lengths, t, nb):
        ns, nz, s, h = p.ns, p.nz, p.s, p.h
        ends, total = [], 0
        for i in range(lengths.shape[0]):
            total = total + lengths[i]
            ends.append(total)

        def item(pos):
            out = 0
            for e in ends:
                out = out + jnp.where(pos >= e, 1, 0)
            return out

        rows = nz * t
        first = s * rows
        me = first + h * t
        blk = t // nb

        def same(a, b):
            return jnp.where(a == b, 1.0, 0.0)

        line = [jnp.where(s == 0, -1, item(first - 1))] + [item(first + (z + 1) * t - 1) for z in range(nz)]
        before, last = line[:nz], line[1:]
        lines = [-1] + [item((k + 1) * rows - 1) for k in range(ns)]
        seq = [jnp.where(me == 0, -1, item(me - 1))] + [item(me + n * blk) for n in range(nb)]
        self.keep = [same(seq[n + 1], seq[n]) for n in range(nb)]
        zs, ks = range(nz), range(ns)
        zero = jnp.float32(0.0)
        self.fore = (
            [same(last[z], last[nz - 1]) for z in zs],
            [[jnp.where(k < s, same(lines[k + 1], before[z]), 0.0) for k in ks] for z in zs],
            [[same(last[k], before[z]) if k < z else zero for k in zs] for z in zs],
        )
        self.back = (
            [same(before[z], before[0]) for z in zs],
            [[jnp.where(k > s, same(lines[k], last[z]), 0.0) for k in ks] for z in zs],
            [[same(before[k], last[z]) if k > z else zero for k in zs] for z in zs],
        )


class Scan:
    def __init__(self, pl_, w, msg, r1, r2, tot, outb, got, sems):
        self.p, self.w, self.msg, self.r1, self.r2 = pl_, w, msg, r1, r2
        self.tot, self.outb, self.got, self.sems = tot, outb, got, sems

    def c1(self, d, dev, slot):
        return rcopy(self.msg.at[dev[1]], self.r1.at[slot], self.sems[0].at[d], self.sems[1].at[d], dev)

    def c2(self, d, dev, slot):
        return rcopy(self.tot, self.r2.at[slot], self.sems[2].at[d], self.sems[3].at[d], dev)

    def c3(self, d, dev, slot):
        return rcopy(self.outb.at[dev[1]], self.got.at[slot], self.sems[4].at[d], self.sems[5].at[d], dev)

    def phase1(self):
        for d, dev in enumerate(self.p.zdev):
            self.c1(d, dev, self.p.h).start()
        self.r1[self.p.h] = self.msg[self.p.h]

    def phase2(self):
        for d, frm in enumerate(self.p.zfrom):
            self.c1(d, frm, frm[1]).wait_recv()
        wt = self.w[0]
        self.tot[...] = sum(wt[z] * self.r1[z].astype(F32) for z in range(self.p.nz)).astype(BF)
        for d, dev in enumerate(self.p.sdev):
            self.c2(d, dev, self.p.s).start()
        self.r2[self.p.s] = self.tot[...]

    def phase3(self):
        for d, dev in enumerate(self.p.sdev):
            self.c2(d, dev, dev[0]).wait_recv()
        _, wp, wl = self.w
        for z in range(self.p.nz):
            v = sum(wl[z][k] * self.r1[k].astype(F32) for k in range(self.p.nz))
            v = v + sum(wp[z][k] * self.r2[k].astype(F32) for k in range(self.p.ns))
            self.outb[z] = v.astype(BF)
        for d, dev in enumerate(self.p.zdev):
            self.c3(d, dev, self.p.h).start()
        self.got[self.p.h] = self.outb[self.p.h]

    def finish(self):
        for d, frm in enumerate(self.p.zfrom):
            self.c3(d, frm, frm[1]).wait_recv()

    def drain(self):
        for d, dev in enumerate(self.p.zdev):
            self.c1(d, dev, self.p.h).wait_send()
            self.c3(d, dev, self.p.h).wait_send()
        for d, dev in enumerate(self.p.sdev):
            self.c2(d, dev, self.p.s).wait_send()


ZROWS = 16
MSG = HD + ZROWS


def msg_rows(p, pg):
    return p // pg, pl.ds(pl.multiple_of(lax.rem(p, pg) * MSG, 16), MSG)


def is_own(shape=(128, 128)):
    return row_low(shape) == lane_low(shape)


def pack_state(sa, lanes):
    own = is_own()
    state = jnp.where(lane_low((HD, 128)), sa[:HD], sa[HD:])
    z = jnp.where(own, 0.0, sa)
    hi = z.astype(BF)
    lo = (z - hi.astype(F32)).astype(BF)
    lane = lax.broadcasted_iota(jnp.int32, (ZROWS, 128), 1)
    row = lax.broadcasted_iota(jnp.int32, (ZROWS, 128), 0)
    sel = jnp.where((lane % HD) < lanes, 1.0, 0.0).astype(BF)
    zr = jnp.where(row == 0, dot_t(sel, hi), jnp.where(row == 1, dot_t(sel, lo), 0.0))
    return jnp.concatenate([state, zr], axis=0).astype(BF)


def unpack_state(msg, every):
    st = msg[:HD].astype(F32)
    z = t_dot(msg[HD:], jnp.ones((ZROWS, 128), BF))
    if not every:
        lane = lax.broadcasted_iota(jnp.int32, (128, 128), 1)
        z = jnp.where(lane % HD == 0, z, 0.0)
    return jnp.where(is_own(), jnp.concatenate([st, st], axis=0), z)


def state_part(p, n, blk, fq, st):
    rows = pl.ds(n * blk, blk)
    r = dot(fq[rows, cols(p, 128)], split_state(st))
    low = lane_low((blk, 128))
    num = jnp.where(low, r[:, :128], r[:, 128:])
    den = pltpu.roll(jnp.where(low, r[:, 128:], r[:, :128]), HD, 1)
    return num, den


FORE_ORDER = [
    ("Wb",), ("Ob",), ("Vb",), ("W", 0, 0), ("O", 0, 0), ("Wf", 0), ("X", 1), ("W", 0, 1), ("X", 0), ("W", 1, 0),
    ("Wf", 1), ("X", 2), ("W", 0, 2), ("W", 2, 0), ("W", 2, 1), ("V", 0, 0), ("Ub",), ("W", 0, 3), ("W", 1, 1),
    ("Of", 0), ("O", 0, 1), ("ln1", 0), ("pj", 1, 0), ("sums", 1, 0), ("ln1", 1), ("ln1", 2), ("W", 2, 2),
    ("W", 2, 3), ("loc", 1, 0), ("Vf", 0), ("W", 1, 2), ("U", 0, 0), ("W", 1, 3), ("pj", 3, 0), ("O", 1, 0),
    ("Of", 1), ("pj", 3, 2), ("O", 0, 2), ("O", 2, 0), ("Uf", 0), ("pj", 0, 1), ("sums", 0, 1), ("pj", 2, 0),
    ("loc", 2, 0), ("sums", 3, 2), ("Wf", 2), ("V", 1, 0), ("pj", 2, 1), ("loc", 2, 1), ("sums", 2, 1), ("Vf", 1),
    ("pj", 1, 1), ("sums", 2, 0), ("O", 1, 1), ("C", 0), ("pj", 3, 1), ("pj", 0, 2), ("V", 0, 1), ("sums", 0, 2),
    ("U", 1, 0), ("sums", 3, 0), ("loc", 1, 1), ("sums", 1, 1), ("sums", 3, 1), ("pj", 2, 2), ("pj", 1, 2),
    ("sums", 1, 2), ("pj", 0, 0), ("sums", 0, 0), ("sums", 2, 2), ("pack",), ("s1",), ("V", 2, 0), ("loc", 3, 2),
    ("loc", 0, 0), ("Uf", 1), ("loc", 1, 2), ("loc", 3, 1), ("loc", 2, 2), ("C", 2), ("Vf", 2), ("O", 2, 1), ("s2",),
    ("loc", 0, 1), ("U", 0, 1), ("loc", 3, 0), ("O", 2, 2), ("O", 0, 3), ("O", 2, 3), ("s3",), ("O", 1, 2),
    ("V", 0, 2), ("U", 2, 0), ("Of", 2), ("O", 1, 3), ("V", 1, 1), ("loc", 0, 2), ("keep",), ("U", 1, 1), ("C", 1),
    ("V", 0, 3), ("sf",), ("state", 0), ("state", 2), ("U", 0, 2), ("state", 3), ("state", 1), ("mid",), ("V", 1, 2),
    ("U", 2, 1), ("prep",), ("F", 0), ("U", 1, 2), ("F", 1), ("U", 2, 2), ("V", 2, 1), ("U", 0, 3), ("U", 1, 3),
    ("V", 1, 3), ("F", 2), ("F", 3), ("F", 4), ("V", 2, 2), ("U", 2, 3), ("F", 5), ("V", 2, 3), ("F", 6), ("Uf", 2),
    ("F", 7),
]
AFT_ORDER = [
    ("lnb2",), ("S", 0, 1), ("lo", 0), ("datt",), ("t", 0), ("t", 2), ("S", 0, 2), ("S", 5, 1), ("t", 3), ("t", 1),
    ("s1",), ("S", 6, 1), ("q", 1), ("s2",), ("S", 7, 1), ("S", 5, 2), ("lo", 2), ("S", 1, 1), ("q", 3), ("q", 0),
    ("s3",), ("q", 2), ("S", 6, 2), ("dmt",), ("S", 7, 2), ("S", 0, 3), ("lo", 1), ("sf",), ("k", 1), ("k", 3),
    ("S", 5, 3), ("S", 3, 1), ("k", 0), ("k", 2), ("S", 1, 2), ("d", 0), ("S", 6, 3), ("d", 1), ("S", 5, 4),
    ("S", 0, 4), ("d", 2), ("S", 4, 1), ("S", 7, 3), ("a1",), ("S", 2, 1), ("d", 3), ("o", 1), ("lnb1",), ("m", 0),
    ("gt", 1), ("S", 3, 2), ("o", 2), ("S", 6, 4), ("g", 3), ("o", 0), ("S", 1, 3), ("g", 1), ("A", 1, 0),
    ("S", 2, 2), ("S", 4, 2), ("gt", 2), ("g", 0), ("g", 2), ("S", 3, 3), ("A", 0, 0), ("A", 1, 1), ("S", 2, 3),
    ("S", 7, 4), ("A", 2, 0), ("o", 3), ("A", 2, 1), ("A", 0, 1), ("A", 2, 2), ("S", 0, 5), ("gt", 0), ("S", 4, 3),
    ("A", 3, 0), ("S", 1, 4), ("S", 2, 4), ("m", 1), ("A", 1, 2), ("A", 3, 1), ("m", 2), ("S", 4, 4), ("A", 2, 3),
    ("A", 2, 4), ("A", 0, 2), ("A", 1, 3), ("S", 3, 4), ("S", 5, 5), ("S", 2, 5), ("A", 1, 4), ("A", 3, 2), ("m", 3),
    ("A", 0, 3), ("S", 7, 5), ("S", 3, 5), ("S", 6, 5), ("A", 3, 3), ("S", 4, 5), ("A", 3, 4), ("A", 0, 4),
    ("A", 3, 5), ("A", 0, 5), ("m", 4), ("A", 1, 5), ("S", 1, 5), ("A", 2, 5),
]


def fore_plan(nz, m, per, parts):
    if (nz, m, per, parts) == (4, 3, 2, 3):
        return FORE_ORDER
    far = nz - 1
    out = [("Wb",)] + [("X", r) for r in range(parts)]
    for w, k, st in sorted((2 * k + st, k, st) for k in range(far) for st in range(m + 1)):
        out.append(("W", k, st))
        if st == 0:
            out.append(("Wf", k))
    out += [("Ob",), ("Ub",), ("Vb",)] + [("ln1", r) for r in range(parts)]
    out += [(a, i, r) for i in range(nz) for r in range(parts) for a in ("pj", "sums")]
    out += [("loc", 0, r) for r in range(parts)] + [("pack",)]
    out += [("s1",), ("keep",), ("C", 0), ("U", 0, 0), ("V", 0, 0)] + [("loc", i, r) for i in range(1, nz - 1) for r in range(parts)]
    out += [("s2",), ("U", 0, 1), ("V", 0, 1)] + [("loc", nz - 1, r) for r in range(parts)]
    out += [("s3",)] + [("C", r) for r in range(1, parts)]
    out += [("Uf", 0), ("Vf", 0), ("U", 0, 2), ("V", 0, 2), ("sf",)] + [("state", i) for i in range(nz)]
    out += [(a, 0, st) for st in range(3, m + 1) for a in "UV"]
    for k in range(far):
        out += [("O", k, 0), ("Of", k)] + [("O", k, st) for st in range(1, m + 1)]
    out += [("mid",), ("prep",)]
    for j in range(nz * per):
        for k in range(1, far):
            for st in range(m + 1):
                if max(0, (k + 1) * per - (m - st)) == j:
                    out += [("U", k, st), ("V", k, st)]
                    if st == 0:
                        out += [("Uf", k), ("Vf", k)]
        out.append(("F", j))
    return out


def fore_kernel(ns, nz, nb, *refs):
    lengths, tok, cot, wq, wo, wu, wd, gains, biases, pads = refs[:10]
    xo, coo, fqo, fko, vbo, atto, rdeno, stateso, mido, w4o, lo, da2o, gu, gd = refs[10:24]
    (xv, cov, av, fq, fk, vb, att, a2t, ct, rden, mid, acc, da2, inc, states,
     w4v, wuv, wdv, gub, gdb, msg, r1, r2, tot, outb, got,
     lsem, tsend, trecv, zsend, zrecv, psend, precv, wsem, ysem, osem,
     c1s, c1r, c2s, c2r, c3s, c3r, pad, wov) = refs[24:]
    P_ = Places(ns, nz)
    t, d = xv.shape
    blk = t // nb
    ew = wq.shape[2]
    ff = wu.shape[2]
    h = P_.h
    m = P_.m
    np_ = d // 128
    pg = msg.shape[1] // MSG
    order = group_order(nz)
    gidx = [pick_group(order, h, i) for i in range(nz)]
    W = Gather(P_, w4v, (0, 3), zsend, zrecv, psend, precv, 0)
    U = Gather(P_, wuv, (0, 1), zsend, zrecv, psend, precv, 1)
    V = Gather(P_, wdv, (0, 1), zsend, zrecv, psend, precv, 2)
    O = Gather(P_, w4v, (3, 1), zsend, zrecv, psend, precv, 3)
    X = RowsIn(P_, tok, xv, tsend, trecv, lsem, 0)
    C = RowsIn(P_, cot, cov, tsend, trecv, lsem, 1)
    greet(P_.zdev + P_.sdev)
    items = Items(P_, lengths, t, nb)
    cflag = items.keep
    scan = Scan(P_, items.fore, msg, r1, r2, tot, outb, got, (c1s, c1r, c2s, c2r, c3s, c3r))
    own = [
        pltpu.make_async_copy(wq, w4v.at[h, 0:3], wsem.at[0]),
        pltpu.make_async_copy(wo, wov, wsem.at[1]),
        pltpu.make_async_copy(wu, wuv.at[h], wsem.at[2]),
        pltpu.make_async_copy(wd, wdv.at[h], wsem.at[3]),
    ]
    for cp in own + [X.own(), C.own()]:
        cp.start()
    outs = []

    def keep(src, dst):
        cp = pltpu.make_async_copy(src, dst, ysem.at[len(outs)])
        outs.append(cp)
        cp.start()

    far = nz - 1
    tile = gub.shape[2]
    per = ff // tile
    steps = nz * per

    def sums_of(p, n):
        chunk_sums(p, blk, n, fk, vb, inc)

    def pack_of(p):
        cur = inc[0, p]
        for n in range(1, nb):
            cur = cflag[n] * cur + inc[n, p]
        g, rr = msg_rows(p, pg)
        msg[g, rr, :] = pack_state(cur, 1)

    def local_of(p, n):
        rows = pl.ds(n * blk, blk)
        c = cols(p, 128)
        q2, k2, v2 = fq[rows, c], fk[rows, c], vb[rows, c]
        s0, s1 = masked_scores(q2, k2, causal_mask(blk))
        g0, g1 = with_ones(v2)
        x0, x1 = dot(s0, g0), dot(s1, g1)
        low = lane_low(x0.shape)
        acc[rows, c] = jnp.where(low, x0, x1)
        rden[rows, c] = pltpu.roll(jnp.where(low, x1, x0), HD, 1)

    def state_of(p):
        g, rr = msg_rows(p, pg)
        cur = unpack_state(got[g, rr, :], True)
        for n in range(nb):
            rows = pl.ds(n * blk, blk)
            c = cols(p, 128)
            used = cflag[n] * cur
            st = used.astype(BF)
            states[n, p] = st
            cur = used + inc[n, p]
            num, den = state_part(p, n, blk, fq, st)
            rd = 1.0 / (1.0 + rden[rows, c] + den)
            att[rows, c] = ((acc[rows, c] + num) * rd).astype(BF)
            rden[rows, c] = rd

    once = []

    def do_ln1(r):
        if not once:
            once.append(r)
            make_pad()
            X.own().wait()
        X.finish(r)
        norm_forward(xv, gains.at[0:1], biases.at[0:1], av, r * blk, blk)

    def make_pad():
        at = h * t + lax.broadcasted_iota(jnp.int32, (t, 128), 0)
        lane = lax.broadcasted_iota(jnp.int32, (t, 128), 1)
        row = lax.broadcasted_iota(jnp.int32, (t, pads.shape[0]), 1)
        at_r = h * t + lax.broadcasted_iota(jnp.int32, (t, pads.shape[0]), 0)
        mine = dot(jnp.where(at_r // 128 == row, 1.0, 0.0).astype(BF), pads[...].astype(F32).astype(BF))
        mine = jnp.where(at % 128 == lane, mine, 0.0)
        pad[...] = jnp.broadcast_to(jnp.sum(mine, axis=1, keepdims=True), (t, 128))

    def do_project(i, r):
        project(av, w4v, gidx[i], pad, fq, fk, vb, pl.ds(r * blk, blk))

    def do_sums(i, r):
        loop_pairs(pg, lambda p: sums_of(p + gidx[i] * pg, r))

    def do_pack():
        loop_pairs(np_, pack_of)

    def do_keep():
        keep(xv, xo)
        keep(fq, fqo)
        keep(fk, fko)
        keep(vb, vbo)

    def do_local(i, r):
        loop_pairs(pg, lambda p: local_of(p + gidx[i] * pg, r))

    def do_state(i):
        loop_pairs(pg, lambda p: state_of(p + i * pg))

    def do_mid():
        keep(w4v, w4o)
        keep(att, atto)
        keep(rden, rdeno)
        keep(states, stateso)
        mid[...] = xv[...].astype(F32) + sum(dot_t(att[:, g * ew : (g + 1) * ew], w4v[g, 3]) for g in range(nz))
        norm_forward(mid, gains.at[1:2], biases.at[1:2], av, 0, t)
        keep(mid, mido)
        transpose_perm(ns, av, a2t)

    def do_prep():
        C.own().wait()
        for r in range(C.parts):
            C.finish(r)
        keep(cov, coo)
        transpose_perm(ns, cov, ct)
        acc[...] = mid[...]
        da2[...] = jnp.zeros_like(da2)

    def begin_own(i, a):
        own[i].wait()
        a.begin()

    def place(i):
        g = pick_group(order, h, i // per)
        return g, pl.ds(pl.multiple_of(lax.rem(i, per) * tile, 128), tile)

    def flush(i, slot):
        g, c = place(i)
        return (
            pltpu.make_async_copy(gub.at[slot], gu.at[g, :, c], osem.at[slot, 0]),
            pltpu.make_async_copy(gdb.at[slot], gd.at[g, :, c], osem.at[slot, 1]),
        )

    todo = {
        "X": X.begin,
        "C": C.begin,
        "W": W.advance,
        "O": O.advance,
        "Of": O.forward,
        "Ob": O.begin,
        "U": U.advance,
        "V": V.advance,
        "Wb": W.begin,
        "Ub": lambda: begin_own(2, U),
        "Vb": lambda: begin_own(3, V),
        "Wf": W.forward,
        "Uf": U.forward,
        "Vf": V.forward,
        "s1": scan.phase1,
        "s2": scan.phase2,
        "s3": scan.phase3,
        "sf": scan.finish,
        "ln1": do_ln1,
        "pj": do_project,
        "sums": do_sums,
        "pack": do_pack,
        "keep": do_keep,
        "loc": do_local,
        "state": do_state,
        "mid": do_mid,
        "prep": do_prep,
    }
    plan = fore_plan(nz, m, per, X.parts)
    cuts = [[]]
    for tok_ in plan:
        if tok_[0] == "F":
            cuts.append([])
        else:
            cuts[-1].append(tok_)

    def run(tokens):
        for tok_ in tokens:
            todo[tok_[0]](*tok_[1:])

    own[1].wait()
    for j in range(d // 256):
        w4v[h, 3, j * 256 : (j + 1) * 256, :] = wov[:, j * 256 : (j + 1) * 256].T
    own[0].wait()
    greeted(P_.zdev + P_.sdev)
    run(cuts[0])

    def step(i, _):
        slot = lax.rem(i, 2)
        for j in range(1, steps):
            if cuts[j]:
                pl.when(i == j)(functools.partial(run, cuts[j]))

        @pl.when(i >= 2)
        def _():
            for cp in flush(i - 2, slot):
                cp.wait()

        g, c = place(i)
        wub, wdb = wuv[g, 0, :, c], wdv[g, 0, c, :]
        up = dot(av[...], wub)
        hidf, slope = gelu_parts(up)
        hid = hidf.astype(BF)
        acc[...] += dot(hid, wdb)
        gdb[slot] = dot(ct[...], hid).astype(BF)
        dup = (slope * dot_t(cov[...], wdb)).astype(BF)
        da2[...] += dot_t(dup, wub)
        gub[slot] = dot(a2t[...], dup).astype(BF)
        for cp in flush(i, slot):
            cp.start()
        return 0

    lax.fori_loop(0, steps, step, 0)
    run(cuts[steps])
    keep(da2, da2o)
    av[...] = acc[...].astype(BF)
    keep(av, lo)
    for i in range(max(0, steps - 2), steps):
        for cp in flush(i, i % 2):
            cp.wait()
    for cp in outs:
        cp.wait()
    X.drain()
    C.drain()
    scan.drain()
    for a in (W, U, V, O):
        a.drain()


def fore(ns, nz, nb, lengths, tok, cot, wq, wo, wu, wd, gains, biases, pad):
    t, d = tok.shape[0] // nz, wq.shape[1]
    ew, ff = wq.shape[2], wu.shape[2]
    np_ = d // 128
    m = ns.bit_length() - 1
    dma = pltpu.SemaphoreType.DMA
    vm = pltpu.VMEM
    tile = 512 if ff % 512 == 0 else ff
    one = ((ew // 128) * MSG, 128)
    nzs = 4 * 2 * (nz - 1) * 2
    td, tdf = ((t, d), BF), ((t, d), F32)
    outs = [td, td, td, td, td, td, tdf, ((nb, np_, 128, 128), BF), tdf, ((nz, 4, d, ew), BF), td, tdf,
            ((nz, d, ff), BF), ((nz, d, ff), BF)]
    args = (lengths, tok, cot, wq, wo, wu, wd, gains, biases, pad)
    return pl.pallas_call(
        functools.partial(fore_kernel, ns, nz, nb),
        out_shape=tuple(jax.ShapeDtypeStruct(s, dt) for s, dt in outs),
        in_specs=[smem_spec()] + [any_spec()] * 6 + [vmem_spec()] * 3,
        out_specs=(any_spec(),) * len(outs),
        scratch_shapes=[vm((t, d), BF)] * 7
        + [vm((d, t), BF)] * 2
        + [vm((t, d), F32)] * 4
        + [
            vm((nb, np_, 128, 128), F32),
            vm((nb, np_, 128, 128), BF),
            vm((nz, 4, d, ew), BF),
            vm((nz, 1, d, ff), BF),
            vm((nz, 1, ff, d), BF),
            vm((2, d, tile), BF),
            vm((2, d, tile), BF),
            vm((nz,) + one, BF),
            vm((nz,) + one, BF),
            vm((ns,) + one, BF),
            vm(one, BF),
            vm((nz,) + one, BF),
            vm((nz,) + one, BF),
            dma((2,)),
            dma((2 * (nz - 1) * parts_of(t),)),
            dma((2 * (nz - 1) * parts_of(t),)),
            dma((nzs,)),
            dma((nzs,)),
            dma((nzs * m,)),
            dma((nzs * m,)),
            dma((4,)),
            dma((16,)),
            dma((2, 2)),
        ]
        + [dma((nz - 1,)), dma((nz - 1,)), dma((ns - 1,)), dma((ns - 1,)), dma((nz - 1,)), dma((nz - 1,))]
        + [vm((t, 128), F32), vm((ew, d), BF)],
        name="fore",
        compiler_params=pltpu.CompilerParams(collective_id=0, has_side_effects=True, vmem_limit_bytes=62 * 2**20),
    )(*args)


def add_block(dst, dlead, dstart, src, slead, n):
    blk = min(n, 64)

    def step(i, _):
        a = dst[dlead + (pl.ds(pl.multiple_of(dstart + i * blk, 16), blk), slice(None))]
        b = src[slead + (pl.ds(pl.multiple_of(i * blk, 16), blk), slice(None))]
        dst[dlead + (pl.ds(pl.multiple_of(dstart + i * blk, 16), blk), slice(None))] = (
            a.astype(F32) + b.astype(F32)
        ).astype(BF)
        return 0

    lax.fori_loop(0, n // blk, step, 0)


class Reduce:
    def __init__(self, p, idx, tz, acc, lead, src, own, rec, zbuf, zslot, zx, xslot, sems, out):
        self.p, self.idx, self.tz = p, idx, tz
        self.acc, self.lead, self.src, self.own, self.rec = acc, lead, src, own, rec
        self.zbuf, self.zslot, self.zx, self.xslot, self.out = zbuf, zslot, zx, xslot, out
        self.cs, self.cr, self.zs, self.zr, self.ls = sems
        orders = ([0] + p.o0, [0] + p.o1)
        self.orders = orders
        self.units = rec[0].shape[2] * 2 // p.ns
        self.bit = [[(p.s >> orders[f][j]) & 1 for j in range(p.m)] for f in range(2)]
        self.pos = []
        for f in range(2):
            pos, seq = 0, []
            for j in range(1, p.m):
                seq.append(pos)
                pos = pos + self.bit[f][j] * self.size(j)
            self.pos.append(seq + [pos])

    def size(self, j):
        return self.units * (self.p.ns >> (j + 1))

    def step(self, f, j):
        i = (self.idx * self.p.m + j) * 2 + f
        b = self.bit[f][j]
        n = self.size(j)
        if j == 0:
            src = self.src(f, 1 - b)
        else:
            at = self.pos[f][j - 1] + (1 - b) * n
            src = self.acc.at[self.lead(f) + (pl.ds(pl.multiple_of(at, 16), n), slice(None))]
        dst = self.rec[j].at[self.rslot(j), f]
        return rcopy(src, dst, self.cs.at[i], self.cr.at[i], self.p.bit[self.orders[f][j]])

    def rslot(self, j):
        return self.idx

    def load(self, f):
        return pltpu.make_async_copy(
            self.src(f, self.bit[f][0]), self.acc.at[self.lead(f)], self.ls.at[self.idx * 2 + f]
        )

    def route(self, hh):
        nz, tz = self.p.nz, self.tz
        q, count, inward = (hh, tz, 1) if hh < tz else (nz - 1 - hh, nz - 1 - tz, -1)
        if q % 2 == 0 and q + 1 < count:
            return False, hh + inward, 0
        return q % 2 == 1, tz, q // 2 + (0 if hh < tz else (tz + 1) // 2)

    def landing(self, f, slot):
        return self.zbuf.at[self.zslot, f] if slot == 0 else self.zx.at[self.xslot, slot - 1, f]

    def zcopy(self, f, to, slot):
        i = self.idx * 2 + f
        mine = self.acc.at[self.lead(f) + (pl.ds(pl.multiple_of(self.pos[f][-1], 16), self.units), slice(None))]
        r = (self.idx * (self.p.nz // 2) + slot) * 2 + f
        return rcopy(mine, self.landing(f, slot), self.zs.at[i], self.zr.at[r], (self.p.s, to))

    def advance(self, st):
        m, tz, nz = self.p.m, self.tz, self.p.nz
        if st <= m:
            for f in range(2):
                if st > 0:
                    self.step(f, st - 1).wait_recv()
                    if st == 1 and self.own:
                        self.load(f).wait()
                    add_block(self.acc, self.lead(f), self.pos[f][st - 1], self.rec[st - 1], (self.rslot(st - 1), f), self.size(st - 1))
                elif self.own:
                    self.load(f).start()
                if st < m:
                    self.step(f, st).start()
        if st == m or st == m + 1:
            for hh in range(nz):
                inner, to, slot = self.route(hh) if hh != tz else (None, 0, 0)
                if inner is None or inner != (st == m + 1):
                    continue

                @pl.when(self.p.h == hh)
                def _(inner=inner, to=to, slot=slot):
                    for f in range(2):
                        if inner:
                            self.zcopy(f, to, 0).wait_recv()
                            add_block(self.acc, self.lead(f), self.pos[f][-1], self.zbuf, (self.zslot, f), self.units)
                        self.zcopy(f, to, slot).start()

        if st == m + 2:

            @pl.when(self.p.h == tz)
            def _():
                both = []
                for f in range(2):
                    v = self.acc[self.lead(f) + (pl.ds(pl.multiple_of(self.pos[f][-1], 16), self.units), slice(None))]
                    v = v.astype(F32)
                    for slot in range((tz + 1) // 2 + (nz - tz) // 2):
                        self.zcopy(f, tz, slot).wait_recv()
                        ref = self.landing(f, slot)
                        v = v + ref[...].astype(F32)
                    both.append(v)
                self.out(jnp.concatenate(both, axis=0))

    def drain(self):
        for f in range(2):
            for j in range(self.p.m):
                self.step(f, j).wait_send()

        @pl.when(self.p.h != self.tz)
        def _():
            for f in range(2):
                self.zcopy(f, 0, 0).wait_send()


class RowsOut:
    def __init__(self, pl_, src, dst, ssem, rsem, lsem, base):
        self.p, self.src, self.dst, self.sems, self.base = pl_, src, dst, (ssem, rsem, lsem), base
        self.t, self.ew = src.shape[0], dst.shape[1]
        self.parts = parts_of(self.t)
        self.n = self.t // self.parts

    def copy(self, r, d, dev, row):
        i = (self.base * (self.p.nz - 1) + d) * self.parts + r
        return rcopy(
            self.src.at[pl.ds(r * self.n, self.n), pl.ds(pl.multiple_of(dev[1] * self.ew, 128), self.ew)],
            self.dst.at[pl.ds(pl.multiple_of(row * self.t + r * self.n, 16), self.n), :],
            self.sems[0].at[i],
            self.sems[1].at[i],
            dev,
        )

    def own(self):
        h = self.p.h
        return pltpu.make_async_copy(
            self.src.at[:, pl.ds(pl.multiple_of(h * self.ew, 128), self.ew)],
            self.dst.at[pl.ds(pl.multiple_of(h * self.t, 16), self.t), :],
            self.sems[2].at[self.base],
        )

    def begin(self, r):
        if r == 0:
            self.own().start()
        for d, dev in enumerate(self.p.zdev):
            self.copy(r, d, dev, self.p.h).start()

    def finish(self):
        for r in range(self.parts):
            for d, frm in enumerate(self.p.zfrom):
                self.copy(r, d, frm, frm[1]).wait_recv()
            for d, dev in enumerate(self.p.zdev):
                self.copy(r, d, dev, self.p.h).wait_send()
        self.own().wait()


class Small:
    def __init__(self, pl_, cur, rec, gz, ssem, rsem, out):
        self.p, self.cur, self.rec, self.gz, self.sems, self.out = pl_, cur, rec, gz, (ssem, rsem), out

    def hop(self, j):
        return rcopy(self.cur.at[j], self.rec.at[j], self.sems[0].at[j], self.sems[1].at[j], self.p.bit[j])

    def zhop(self, d, dev, slot):
        i = self.p.m + d
        return rcopy(self.cur.at[self.p.m], self.gz.at[slot], self.sems[0].at[i], self.sems[1].at[i], dev)

    def advance(self, st):
        m = self.p.m
        if 0 < st <= m:
            self.hop(st - 1).wait_recv()
            self.cur[st] = self.cur[st - 1] + self.rec[st - 1]
        if st < m:
            self.hop(st).start()
        if st == m:
            for d, dev in enumerate(self.p.zdev):
                self.zhop(d, dev, self.p.h).start()
            self.gz[self.p.h] = self.cur[m]
        if st == m + 1:
            for d, frm in enumerate(self.p.zfrom):
                self.zhop(d, frm, frm[1]).wait_recv()
            total = self.gz[0]
            for z in range(1, self.p.nz):
                total = total + self.gz[z]
            self.out[...] = total
            for j in range(m):
                self.hop(j).wait_send()
            for d, dev in enumerate(self.p.zdev):
                self.zhop(d, dev, self.p.h).wait_send()


def back_queries(p, n, blk, fk, vb, fq, dr0, dr1, st, dq):
    rows = pl.ds(n * blk, blk)
    c = cols(p, 128)
    q2, k2, v2, e0, e1 = fq[rows, c], fk[rows, c], vb[rows, c], dr0[rows, c], dr1[rows, c]
    g0, g1 = with_ones(v2)
    keep = causal_mask(blk)
    ds0 = jnp.where(keep, dot_t(e0, g0), 0.0).astype(BF)
    ds1 = jnp.where(keep, dot_t(e1, g1), 0.0).astype(BF)
    dfq = jnp.where(lane_low(q2.shape), dot(ds0, k2), dot(ds1, k2))
    dfq = dfq + dot_t(jnp.concatenate([e0, e1], axis=1), split_state(st))
    dq[rows, c] = (dfq * jnp.minimum(q2.astype(F32), 1.0)).astype(BF)


def back_keys(p, n, blk, fk, vb, fq, dr0, dr1, dst):
    rows = pl.ds(n * blk, blk)
    c = cols(p, 128)
    q2, k2, v2, e0, e1 = fq[rows, c], fk[rows, c], vb[rows, c], dr0[rows, c], dr1[rows, c]
    g0, g1 = with_ones(v2)
    keep_t = lax.broadcasted_iota(jnp.int32, (blk, blk), 0) <= lax.broadcasted_iota(jnp.int32, (blk, blk), 1)
    low = lane_low(q2.shape)
    dt0 = jnp.where(keep_t, dot_t(g0, e0), 0.0).astype(BF)
    dt1 = jnp.where(keep_t, dot_t(g1, e1), 0.0).astype(BF)
    dfk = jnp.where(low, dot(dt0, q2), dot(dt1, q2))
    dfk = dfk + dot_t(jnp.concatenate([g0, g1], axis=1), split_state(dst))
    st0, st1 = masked_scores(k2, q2, keep_t)
    own = jnp.where(row_low((128, 128)) == lane_low((128, 128)), dst, jnp.zeros_like(dst))
    dvv = jnp.where(low, dot(st0, e0), dot(st1, e1)) + dot(k2, own)
    fk[rows, c] = (dfk * jnp.minimum(k2.astype(F32), 1.0)).astype(BF)
    vb[rows, c] = dvv.astype(BF)


def aft_plan(nz, m, parts, quads):
    if (nz, m, parts, quads) == (4, 3, 3, 4):
        return AFT_ORDER
    n, last = 2 * nz, m + 2
    half = nz
    gaps = [half + 0.5] * (m - 1) + [3, 3]
    at = [sum(gaps[:st]) for st in range(last)]
    ffn = [("S", i, st) for _, i, st in sorted((i + at[st - 1], i, st) for i in range(n) for st in range(1, last + 1))]
    heads = 1 + max(j for j, x in enumerate(ffn) if x[2] == 1)
    out = []
    state = {"j": 0}

    def tick(k):
        out.extend(ffn[state["j"] : state["j"] + k])
        state["j"] = min(len(ffn), state["j"] + k)

    out += [("lo", r) for r in range(parts - 1)] + [("lnb2",)]
    tick(half - 2)
    out.append(("datt",))
    tick(1)
    for i in range(quads):
        out.append(("t", i))
        if i == 1:
            tick(1)
    out += [("s1",), ("lo", parts - 1), ("dmt",), ("s2",)]
    tick(3)
    for i in range(quads):
        out.append(("q", i))
        if i == min(1, quads - 1):
            tick(max(0, heads - state["j"]))
            out.append(("s3",))
        else:
            tick(1)
    out.append(("a1",))
    out += [("o", i) for i in range(nz)] + [("sf",)]
    for i in range(quads):
        out.append(("k", i))
        tick(1)
    attn = {w: [("A", i, w - i) for i in range(nz) if 0 <= w - i <= last] for w in range(nz + last)}
    for i in range(nz):
        out.append(("g", i))
        out += attn[i]
        out.append(("d", i))
        tick(1)
    out.append(("lnb1",))
    out += [("gt", r) for r in range(parts)]
    tick(len(ffn))
    for w in range(nz, nz + last):
        if w - nz <= m + 1:
            out.append(("m", w - nz))
        out += attn[w]
    out += [("m", st) for st in range(last, m + 2)]
    return out


def aft_kernel(ns, nz, nb, *refs):
    lengths, x, co, fqi, fki, vbi, atti, rdeni, statesi, midi, w4, lo, da2i, gu, gd, gains, biases = refs[:17]
    lo_o, gt_o, gbo, oq, oo, ou, od = refs[17:24]
    (fq, fk, vb, dr0, dr1, att, dml, dq, a1t, dmt, datt, mid, dmid, rden, ginc, states, ring, sums2, sums1,
     pool, rec0, *more) = refs[24:]
    m = ns.bit_length() - 1
    rec = [rec0] + list(more[: m - 1])
    (zbuf, zx, msg, r1, r2, tot, outb, got, gcur, grec, gz,
     lsem, rsem, asem, tsend, trecv, tl, csend, crecv, zsend, zrecv, gsend, grecv,
     c1s, c1r, c2s, c2r, c3s, c3r) = more[m - 1 :]
    P_ = Places(ns, nz)
    t, d = fq.shape
    blk = t // nb
    ew = lo_o.shape[1]
    np_ = d // 128
    pg = msg.shape[1] // MSG
    quarter = d // 4
    greet(P_.zdev + P_.sdev)
    items = Items(P_, lengths, t, nb)
    cflag = items.keep
    scan = Scan(P_, items.back, msg, r1, r2, tot, outb, got, (c1s, c1r, c2s, c2r, c3s, c3r))
    lo_a = RowsOut(P_, lo, lo_o, tsend, trecv, tl, 0)
    gt_a = RowsOut(P_, dml, gt_o, tsend, trecv, tl, 1)
    small = Small(P_, gcur, grec, gz, gsend, grecv, gbo)
    sems = (csend, crecv, zsend, zrecv, asem)
    ends_first = [z for pair in zip(range(nz // 2), range(nz - 1, nz // 2 - 1, -1)) for z in pair]
    ffn, attn = [], []

    def out_down(v):
        od[...] = v.T.astype(BF)

    def out_up(v):
        ou[...] = v.astype(BF)

    def out_attn(v):
        for c in range(3):
            oq[c] = v[:, c * ew : (c + 1) * ew].astype(BF)
        oo[...] = v[:, 3 * ew :].T.astype(BF)

    for a, (g, out) in enumerate(((gd, out_down), (gu, out_up))):
        for i, tz in enumerate(ends_first):
            idx = a * nz + i
            ffn.append(
                Reduce(
                    P_, idx, tz, pool, lambda f, idx=idx: (idx, f),
                    lambda f, b, g=g, tz=tz: g.at[tz, f, pl.ds(pl.multiple_of(b * quarter, 16), quarter), :],
                    True, rec, zbuf, idx, zx, a, sems, out,
                )
            )
    top = [[(P_.s >> o[0]) & 1 for o in ([0] + P_.o0, [0] + P_.o1)][f] for f in range(2)]
    for i, tz in enumerate(ends_first):
        idx = 2 * nz + i
        attn.append(
            Reduce(
                P_, idx, tz, rec0, lambda f, tz=tz: (2 * tz + f, top[f]),
                lambda f, b, tz=tz: rec0.at[2 * tz + f, b],
                False, rec, zbuf, idx, zx, 2, sems, out_attn,
            )
        )
    loads = {}

    def load(name, src, dst):
        i = len(loads)
        loads[name] = (src, dst, i)
        pltpu.make_async_copy(src, dst, lsem.at[i]).start()

    here = set()

    def ready(*names):
        for name in names:
            if name not in here:
                here.add(name)
                src, dst, i = loads[name]
                pltpu.make_async_copy(src, dst, lsem.at[i]).wait()

    uses = [(g, 3) for g in range(nz)] + [(g, c) for g in ends_first for c in range(3)]
    depth = ring.shape[0]

    def ring_copy(i):
        g, c = uses[i]
        return pltpu.make_async_copy(w4.at[g, c], ring.at[i % depth], rsem.at[i % depth])

    load("da2", da2i, datt)
    load("mid", midi, mid)
    load("co", co, dr0)
    for i in range(depth):
        ring_copy(i).start()
    load("att", atti, att)
    load("rden", rdeni, rden)
    load("fq", fqi, fq)
    greeted(P_.zdev + P_.sdev)
    for it in ffn:
        it.advance(0)
    load("fk", fki, fk)
    load("vb", vbi, vb)
    load("states", statesi, states)
    da1 = mid
    quads = 4 if np_ % 4 == 0 else 1

    def emit(rows, v):
        dmid[rows, :] = v
        dml[rows, :] = v.astype(BF)

    def do_lnb2():
        ready("da2", "mid", "co")
        norm_backward(datt, mid, gains.at[1:2], dr0, emit, sums2)

    def use_ring(i, body):
        ring_copy(i).wait()
        body(ring[i % depth])
        if i + depth < len(uses):
            ring_copy(i + depth).start()

    def do_datt():
        for i in range(nz):

            def body(w, i=i):
                datt[:, i * ew : (i + 1) * ew] = dot(dml[...], w)

            use_ring(i, body)

    def turn(p):
        for n in range(nb):
            attend_gradient(p, n, blk, datt, att, rden, dr0, dr1)
        chunk_gradients(p, blk, nb, fq, dr0, dr1, ginc)
        cur = cflag[nb - 1] * ginc[nb - 1, p]
        for n in range(nb - 2, -1, -1):
            cur = cflag[n] * (cur + ginc[n, p])
        g, rr = msg_rows(p, pg)
        msg[g, rr, :] = pack_state(cur, 2)

    def queries(p):
        for n in range(nb):
            back_queries(p, n, blk, fk, vb, fq, dr0, dr1, states[n, p], dq)

    def keys(p):
        g, rr = msg_rows(p, pg)
        cur = unpack_state(got[g, rr, :], False)
        for n in range(nb - 1, -1, -1):
            back_keys(p, n, blk, fk, vb, fq, dr0, dr1, cur.astype(BF))
            cur = cflag[n] * (cur + ginc[n, p])

    def pairs(body, i):
        n = np_ // quads
        loop_pairs(n, lambda p: body(p + i * n))

    def do_turn(i):
        ready("att", "rden", "fq")
        pairs(turn, i)

    def do_dmt():
        transpose_perm(ns, dml, dmt)
        load("x", x, dml)

    def do_queries(i):
        ready("fk", "vb", "states")
        pairs(queries, i)

    def do_a1():
        ready("x")
        norm_forward(dml, gains.at[0:1], biases.at[0:1], dml, 0, t)
        transpose_perm(ns, dml, a1t)
        load("x2", x, dml)

    def do_keys_part(i):
        pairs(keys, i)

    def put(tz, c, v):
        v = v.astype(BF)
        for f in range(2):
            for b in range(2):
                r = (2 * f + b) * quarter
                rec0[2 * tz + f, b, :, c * ew : (c + 1) * ew] = v[r : r + quarter, :]

    def group(i):
        tz = ends_first[i]
        return tz, slice(tz * ew, (tz + 1) * ew)

    def do_out_grad(i):
        tz, c0 = group(i)
        put(tz, 3, dot(dmt[...], att[:, c0]))

    def do_grads(i):
        tz, c0 = group(i)
        for k, r in enumerate((dq, fk, vb)):
            put(tz, k, dot(a1t[...], r[:, c0]))

    def do_da1(i):
        tz, c0 = group(i)
        j = nz + i * 3
        for k in range(3):
            ring_copy(j + k).wait()
        v = sum(dot_t(r[:, c0], ring[(j + k) % depth]) for k, r in enumerate((dq, fk, vb)))
        if i == 0:
            da1[...] = v
        else:
            da1[...] += v
        for k in range(3):
            if j + k + depth < len(uses):
                ring_copy(j + k + depth).start()

    def emit1(rows, v):
        dml[rows, :] = v.astype(BF)

    def do_lnb1():
        ready("x2")
        norm_backward(da1, dml, gains.at[0:1], dmid, emit1, sums1)
        gcur[0] = jnp.zeros(gcur.shape[1:], F32)
        for i, (ref, k) in enumerate(((sums1, 0), (sums2, 0), (sums1, 1), (sums2, 1))):
            gcur[0, i : i + 1, :] = jnp.sum(ref[k], axis=0, keepdims=True)

    todo = {
        "S": lambda i, st: ffn[i].advance(st),
        "A": lambda i, st: attn[i].advance(st),
        "lo": lo_a.begin,
        "gt": gt_a.begin,
        "m": small.advance,
        "s1": scan.phase1,
        "s2": scan.phase2,
        "s3": scan.phase3,
        "sf": scan.finish,
        "lnb2": do_lnb2,
        "datt": do_datt,
        "t": do_turn,
        "dmt": do_dmt,
        "q": do_queries,
        "a1": do_a1,
        "o": do_out_grad,
        "k": do_keys_part,
        "g": do_grads,
        "d": do_da1,
        "lnb1": do_lnb1,
    }
    for tok_ in aft_plan(nz, m, lo_a.parts, quads):
        todo[tok_[0]](*tok_[1:])
    lo_a.finish()
    gt_a.finish()
    for it in ffn + attn:
        it.drain()
    scan.drain()


def aft(ns, nz, nb, lengths, x, co, fq, fk, vb, att, rden, states, mid, w4g, lo, da2, gu, gd, gains, biases):
    t, d = x.shape
    ew, ff = w4g.shape[3], gu.shape[3]
    m = ns.bit_length() - 1
    np_ = d // 128
    dma = pltpu.SemaphoreType.DMA
    vm = pltpu.VMEM
    one = ((ew // 128) * MSG, 128)
    unit = d // (2 * ns)
    n_items = 3 * nz
    depth = 4
    args = (lengths, x, co, fq, fk, vb, att, rden, states, mid, w4g, lo, da2, gu, gd, gains, biases)
    pieces = [((3, 2 * unit, ew), BF), ((ew, 2 * unit), BF), ((2 * unit, ff), BF), ((ff, 2 * unit), BF)]
    rows = jax.ShapeDtypeStruct((t * nz, ew), BF)
    return pl.pallas_call(
        functools.partial(aft_kernel, ns, nz, nb),
        out_shape=(rows, rows, jax.ShapeDtypeStruct((8, d), F32)) + tuple(jax.ShapeDtypeStruct(*x) for x in pieces),
        in_specs=[smem_spec()] + [any_spec()] * 14 + [vmem_spec()] * 2,
        out_specs=(any_spec(),) * 2 + (vmem_spec(),) * 5,
        scratch_shapes=[vm((t, d), BF)] * 8
        + [vm((d, t), BF)] * 2
        + [vm((t, d), F32)] * 4
        + [
            vm((nb, np_, 128, 128), F32),
            vm((nb, np_, 128, 128), BF),
            vm((depth, d, ew), BF),
            vm((2, 8, d), F32),
            vm((2, 8, d), F32),
            vm((2 * nz, 2, d // 4, ff), BF),
        ]
        + [vm((n_items, 2, d // 4 >> j, ff), BF) for j in range(m)]
        + [
            vm((n_items, 2, unit, ff), BF),
            vm((3, max(1, nz // 2 - 1), 2, unit, ff), BF),
            vm((nz,) + one, BF),
            vm((nz,) + one, BF),
            vm((ns,) + one, BF),
            vm(one, BF),
            vm((nz,) + one, BF),
            vm((nz,) + one, BF),
            vm((m + 1, 8, d), F32),
            vm((m, 8, d), F32),
            vm((nz, 8, d), F32),
            dma((16,)),
            dma((depth,)),
            dma((2 * n_items,)),
            dma((2 * (nz - 1) * parts_of(t),)),
            dma((2 * (nz - 1) * parts_of(t),)),
            dma((2,)),
            dma((n_items * m * 2,)),
            dma((n_items * m * 2,)),
            dma((n_items * 2,)),
            dma((n_items * nz,)),
            dma((m + nz - 1,)),
            dma((m + nz - 1,)),
        ]
        + [dma((nz - 1,)), dma((nz - 1,)), dma((ns - 1,)), dma((ns - 1,)), dma((nz - 1,)), dma((nz - 1,))],
        name="aft",
        compiler_params=pltpu.CompilerParams(collective_id=1, has_side_effects=True, vmem_limit_bytes=63 * 2**20),
    )(*args)


def finish_kernel(where, gt, lo, oq, oo, ou, od, gb, gt_o, lo_o, oq_o, oo_o, ou_o, od_o, gg, gbias):
    gt_o[...] = gt[...].astype(F32)
    lo_o[...] = lo[...]

    @pl.when(pl.program_id(0) == 0)
    def _():
        for src, dst in ((oq, oq_o), (oo, oo_o), (ou, ou_o), (od, od_o)):
            dst[...] = src[...].astype(F32)
        w = gg.shape[1]
        shape = (gb.shape[1], w)
        at = lax.broadcasted_iota(jnp.int32, shape, 0) - where[0] * w
        pick = jnp.where(at == lax.broadcasted_iota(jnp.int32, shape, 1), 1.0, 0.0)
        v = jnp.dot(gb[...], pick, precision=lax.Precision.HIGHEST, preferred_element_type=F32)
        gg[...] = v[:2]
        gbias[...] = v[2:4]


def finish(where, w, gt, lo, oq, oo, ou, od, gb):
    n = 2
    rows, ew = gt.shape
    blk = pl.BlockSpec((rows // n, ew), lambda i: (i, 0))

    def whole(a):
        return pl.BlockSpec(a.shape, lambda i, k=len(a.shape): (0,) * k)

    small = jax.ShapeDtypeStruct((2, w), F32)
    outs = [jax.ShapeDtypeStruct(gt.shape, F32), jax.ShapeDtypeStruct(lo.shape, BF)]
    outs += [jax.ShapeDtypeStruct(a.shape, F32) for a in (oq, oo, ou, od)] + [small, small]
    return pl.pallas_call(
        finish_kernel,
        grid=(n,),
        out_shape=tuple(outs),
        in_specs=[smem_spec(), blk, blk] + [whole(a) for a in (oq, oo, ou, od, gb)],
        out_specs=(blk, blk) + tuple(whole(a) for a in outs[2:]),
        name="finish",
        compiler_params=pltpu.CompilerParams(vmem_limit_bytes=60 * 2**20),
    )(where, gt, lo, oq, oo, ou, od, gb)


def shards(ns, nz, tokens, lengths, pad_mask, w_qkv, w_out, w_up, w_down, norm_gains, norm_biases, out_cotangent):
    rows = tokens.shape[0]
    t = rows // nz
    d = w_qkv.shape[1]
    ff = w_up.shape[1]
    ew = d // nz
    blk = math.gcd(t, UNIT)
    nb = t // blk
    s, h = lax.axis_index("seq"), lax.axis_index("head")
    x, co, fq, fk, vb, att, rden, states, mid, w4g, lo, da2, gu, gd = fore(
        ns, nz, nb, lengths, tokens, out_cotangent, w_qkv, w_out, w_up[None], w_down[None],
        norm_gains, norm_biases, pad_mask.reshape(rows // 128, 128),
    )
    half = (nz, 2, d // 2, ff)
    lo_o, gt_o, gbo, oq, oo, ou, od = aft(
        ns, nz, nb, lengths, x, co, fq, fk, vb, att, rden, states, mid, w4g, lo, da2,
        gu.reshape(half), gd.reshape(half), norm_gains, norm_biases,
    )
    w = d // (ns * nz)
    where = jnp.reshape(h * ns + s, (1,)).astype(jnp.int32)
    gt_f, lo_f, gq, go, gup, gdown, gg, gbias = finish(where, w, gt_o, lo_o, oq, oo, ou, od, gbo)
    return lo_f, gt_f, gq, go, gup, gdown, gg, gbias


def solution(mesh):
    in_specs = (
        P("seq", "head"),
        P(),
        P("seq"),
        P(None, None, "head"),
        P("head", None),
        P(None, "head"),
        P("head", None),
        P(),
        P(),
        P("seq", "head"),
    )
    out_specs = (
        P("seq", "head"),
        P("seq", "head"),
        P(None, "seq", "head"),
        P("head", "seq"),
        P("seq", "head"),
        P("head", "seq"),
        P(None, ("head", "seq")),
        P(None, ("head", "seq")),
    )
    f = functools.partial(shards, mesh.shape["seq"], mesh.shape["head"])
    return jax.shard_map(f, mesh=mesh, in_specs=in_specs, out_specs=out_specs, check_vma=False)
```
